32 devices in a mesh: dp: 32 (over z, y, x, core).
Axes of the slice: x: 2, y: 2, z: 4, core: 2. Of those that a mesh axis runs over, the one named last changes fastest.
Arguments:
- activations: float32 [24576, 1024], P('dp'), may hold values from -6 to 6
- segment_ids: int32 [96, 256], P('dp'), may hold values from 0 to 3, never falling along the last dimension, each value on 1 to 128 neighbouring positions
- out_grad: float32 [24576, 1024], P('dp'), may hold values from -6 to 6
- qkv_weight: float32 [4096, 1024], P('dp'), may hold values from -0.1875 to 0.1875
- qkv_first: float32 [4096, 1024], P('dp'), may hold values from -32 to 32
- qkv_second: float32 [4096, 1024], P('dp'), may hold values from 110.592 to 442.368
- out_weight: float32 [1024, 2048], P('dp'), may hold values from -0.5 to 0.5
- out_first: float32 [1024, 2048], P('dp'), may hold values from -28 to 28
- out_second: float32 [1024, 2048], P('dp'), may hold values from 76.1856 to 307.2
- gate_up_weight: float32 [6144, 1024], P('dp'), may hold values from -0.1875 to 0.1875
- gate_up_first: float32 [6144, 1024], P('dp'), may hold values from -56 to 56
- gate_up_second: float32 [6144, 1024], P('dp'), may hold values from 307.2 to 1228.8
- down_weight: float32 [1024, 3072], P('dp'), may hold values from -0.109375 to 0.109375
- down_first: float32 [1024, 3072], P('dp'), may hold values from -40 to 40
- down_second: float32 [1024, 3072], P('dp'), may hold values from 196.608 to 786.432
- norm_gains: float32 [2304], P('dp'), may hold values from 0.5 to 1.5
- gains_first: float32 [2304], P('dp'), may hold values from -112 to 112
- gains_second: float32 [2304], P('dp'), may hold values from 1228.8 to 4915.2
Outputs:
- layer_output: float32 [24576, 1024], P('dp')
- input_grad: float32 [24576, 1024], P('dp')
- qkv_updated: float32 [4096, 1024], P('dp')
- qkv_first_new: float32 [4096, 1024], P('dp')
- qkv_second_new: float32 [4096, 1024], P('dp')
- out_updated: float32 [1024, 2048], P('dp')
- out_first_new: float32 [1024, 2048], P('dp')
- out_second_new: float32 [1024, 2048], P('dp')
- gate_up_updated: float32 [6144, 1024], P('dp')
- gate_up_first_new: float32 [6144, 1024], P('dp')
- gate_up_second_new: float32 [6144, 1024], P('dp')
- down_updated: float32 [1024, 3072], P('dp')
- down_first_new: float32 [1024, 3072], P('dp')
- down_second_new: float32 [1024, 3072], P('dp')
- gains_updated: float32 [2304], P('dp')
- gains_first_new: float32 [2304], P('dp')
- gains_second_new: float32 [2304], P('dp')
The draws below stay inside these ranges and needn't reach their ends.
Inputs may be any that keep to these rules, and one draw needn't show every extreme that they name: `segment_ids`: in each row (micro-batch) segment ids never fall; each of the 4 documents has 1 to 128 tokens, one exactly 128.
All inputs are finite; a program needn't handle non-finite values.
Results may differ from the reference program's by a relative error of at most 0.013.
The reference program's roundings to bfloat16 on the way count: a program that leaves them out, or rounds other values in their place, can miss the bound.
Values may be sent and summed in bfloat16 or wider, within the bound.
No kernel may reach another device: no remote copies, remote signals or barrier semaphores. Data moves between devices by JAX's collectives and lax.ppermute only.
A program may use at most 320 MiB of HBM per device.

```python
import math
from functools import partial
import jax
import jax.numpy as jnp
import numpy as np
from jax import lax

D = 1024
QUERY_HEADS = 16
KEY_VALUE_HEADS = 8
HEAD_WIDTH = 128
FF = 3072
MICRO_TOKENS = 256
MICRO_BATCHES = 3
SEGS = 4
STEP = 10
TOK_DEV = 768
TOKENS = 24576
QKV = 4096
GAINS = 2304
N_DP = 32


def steps_of(stream_key, extent, cuts, low, high):
    level, own = 1.0, jax.random.fold_in(stream_key, 6)
    for axis_at, shards_of in cuts:
        draws = jnp.exp(jax.random.uniform(jax.random.fold_in(own, axis_at), (shards_of,), jnp.float32, low / len(cuts), high / len(cuts)))
        level = level * jnp.repeat(draws, extent[axis_at] // shards_of).reshape([-1 if axis == axis_at else 1 for axis in range(len(extent))])
    return level


def profile(amount, total, limit, slope):
    portions = [(1 << 20) // math.isqrt(grade ** slope) + 1 for grade in range(2, amount + 1)]
    spare, counts = total - limit - (amount - 1), [1] * (amount - 1)
    while spare > 0:
        free = [i for i in range(amount - 1) if counts[i] < limit]
        mass, budget = sum([portions[i] for i in free]), spare
        for i in free:
            addition = min(limit - counts[i], max(1, budget * portions[i] // mass), spare)
            counts[i] = counts[i] + addition
            spare = spare - addition
    return np.array([limit] + counts)


def ragged_sizes(own_key, number_of, total, most, lean):
    if number_of == 2:
        one = jax.random.randint(own_key, (), max(1, total - most), min(most, total - 1) + 1)
        return jnp.stack([one, total - one])
    tallies = jnp.asarray(profile(number_of, total, most, lean), jnp.int32)
    twos = (number_of - 1) // 2
    source_of, receiver = tallies[1:1 + 2 * twos:2], tallies[2:2 + 2 * twos:2]
    room = jnp.minimum(source_of - 1, most - receiver)
    passed = jax.random.randint(jax.random.fold_in(own_key, 1), (twos,), 0, 1 << 20) % (room + 1)
    tallies = tallies.at[1:1 + 2 * twos:2].set(source_of - passed).at[2:2 + 2 * twos:2].set(receiver + passed)
    return tallies[jax.random.permutation(jax.random.fold_in(own_key, 2), number_of)]


def bell_draw(own_key, dims, spread, reach, shards=(), held_as=jnp.bfloat16):
    level = steps_of(own_key, dims, shards, -0.22, 0.18) if shards else 1.0
    drawn = jax.random.normal(own_key, dims, jnp.float32) * spread * level
    return jnp.minimum(jnp.maximum(drawn, -reach), reach).astype(held_as)


def setup_inputs(seed: int = 0) -> dict:
    key_of = jax.random.split(jax.random.key(seed), 19)
    return {
        "activations": bell_draw(key_of[0], (TOKENS, D), 1.0, 6.0, ((0, 32),), jnp.float32),
        "segment_ids": jax.vmap(lambda own: jnp.searchsorted(jnp.cumsum(ragged_sizes(own, SEGS, MICRO_TOKENS, MICRO_TOKENS // 2, 2)), jnp.arange(MICRO_TOKENS), side="right"))(jax.random.split(key_of[1], (N_DP * MICRO_BATCHES))).reshape((N_DP * MICRO_BATCHES, MICRO_TOKENS)).astype(jnp.int32),
        "out_grad": bell_draw(key_of[2], (TOKENS, D), 1.0, 6.0, ((0, 32),), jnp.float32),
        "qkv_weight": bell_draw(key_of[3], (QKV, D), D ** -0.5, 0.1875, ((0, 32),), jnp.float32),
        "qkv_first": bell_draw(key_of[4], (QKV, D), (0.033 * TOKENS ** 0.5), 32.0, ((0, 32),), jnp.float32),
        "qkv_second": jnp.clip(jnp.exp(math.log(442.368) - 1.3862944 * jax.random.uniform(key_of[5], (QKV, D), jnp.float32) ** steps_of(key_of[5], (QKV, D), ((0, 32),), -0.2, 0.2)), 110.592, 442.368),
        "out_weight": bell_draw(key_of[6], (D, QUERY_HEADS * HEAD_WIDTH), (QUERY_HEADS * HEAD_WIDTH // 16) ** -0.5, 0.5, ((0, 32),), jnp.float32),
        "out_first": bell_draw(key_of[7], (D, QUERY_HEADS * HEAD_WIDTH), (0.028 * TOKENS ** 0.5), 28.0, ((0, 32),), jnp.float32),
        "out_second": jnp.clip(jnp.exp(math.log(307.2) - 1.3943266 * jax.random.uniform(key_of[8], (D, QUERY_HEADS * HEAD_WIDTH), jnp.float32) ** steps_of(key_of[8], (D, QUERY_HEADS * HEAD_WIDTH), ((0, 32),), -0.2, 0.2)), 76.1856, 307.2),
        "gate_up_weight": bell_draw(key_of[9], (2 * FF, D), D ** -0.5, 0.1875, ((0, 32),), jnp.float32),
        "gate_up_first": bell_draw(key_of[10], (2 * FF, D), (0.055 * TOKENS ** 0.5), 56.0, ((0, 32),), jnp.float32),
        "gate_up_second": jnp.clip(jnp.exp(math.log(1228.8) - 1.3862944 * jax.random.uniform(key_of[11], (2 * FF, D), jnp.float32) ** steps_of(key_of[11], (2 * FF, D), ((0, 32),), -0.2, 0.2)), 307.2, 1228.8),
        "down_weight": bell_draw(key_of[12], (D, FF), FF ** -0.5, 0.109375, ((0, 32),), jnp.float32),
        "down_first": bell_draw(key_of[13], (D, FF), (0.044 * TOKENS ** 0.5), 40.0, ((0, 32),), jnp.float32),
        "down_second": jnp.clip(jnp.exp(math.log(786.432) - 1.3862944 * jax.random.uniform(key_of[14], (D, FF), jnp.float32) ** steps_of(key_of[14], (D, FF), ((0, 32),), -0.2, 0.2)), 196.608, 786.432),
        "norm_gains": jnp.clip(1.0 + 0.1 * jax.random.normal(key_of[15], (GAINS,), jnp.float32), 0.5, 1.5),
        "gains_first": bell_draw(key_of[16], (GAINS,), (0.11 * TOKENS ** 0.5), 112.0, ((0, 32),), jnp.float32),
        "gains_second": jnp.clip(jnp.exp(math.log(4915.2) - 1.3862944 * jax.random.uniform(key_of[17], (GAINS,), jnp.float32) ** steps_of(key_of[17], (GAINS,), ((0, 32),), -0.2, 0.2)), 1228.8, 4915.2),
    }


@jax.custom_vjp
def reduced_precision(v):
    return lax.optimization_barrier(v.astype(jnp.bfloat16)).astype(jnp.float32)

@jax.custom_vjp
def low_back(v):
    return v

def low_keep(v):
    return (reduced_precision(v), None)

def low_pass(kept, grad):
    return (grad,)

def back_keep(v):
    return (v, None)

def back_low(kept, grad):
    return (reduced_precision(grad),)
reduced_precision.defvjp(low_keep, low_pass)
low_back.defvjp(back_keep, back_low)
NORM_EPS = 1e-06
ROPE_BASE = 1000000.0
BETA_ONE = 0.9
BETA_TWO = 0.95
ADAM_EPS = 1e-08
HIGHEST = lax.Precision.HIGHEST

def rms_scale(values):
    return lax.rsqrt(lax.optimization_barrier(jnp.mean(values * values, axis=-1, keepdims=True)) + NORM_EPS)

def rotate_half(values):
    half_size = values.shape[-1] // 2
    return jnp.concatenate([-values[..., half_size:], values[..., :half_size]], axis=-1)

def segment_tables(segment_row, head_size):
    length = segment_row.shape[0]
    token_order = jnp.arange(length, dtype=jnp.int32)
    same_segment = segment_row[:, None] == segment_row[None, :]
    earlier = token_order[None, :] < token_order[:, None]
    positions = lax.optimization_barrier(jnp.sum(jnp.where(same_segment & earlier, 1, 0), axis=1)).astype(jnp.int32)
    mask_allowed = same_segment & (token_order[None, :] <= token_order[:, None])
    half_size = head_size // 2
    frequency = ROPE_BASE ** (-(jnp.arange(half_size, dtype=jnp.float32) * (2.0 / head_size)))
    angles = positions.astype(jnp.float32)[:, None] * frequency[None, :]
    cosine_table = jnp.concatenate([jnp.cos(angles), jnp.cos(angles)], axis=-1)
    sine_table = jnp.concatenate([jnp.sin(angles), jnp.sin(angles)], axis=-1)
    return (mask_allowed, cosine_table, sine_table)

def attend_mask(queries, keys_in, values_in, mask_allowed):
    query_group_width = QUERY_HEADS // KEY_VALUE_HEADS
    keys_all = jnp.repeat(keys_in, query_group_width, axis=1)
    values_all = jnp.repeat(values_in, query_group_width, axis=1)
    scores = low_back(jnp.einsum('qhd,khd->hqk', queries, keys_all, precision=HIGHEST) * HEAD_WIDTH ** (-0.5))
    scores = jnp.where(mask_allowed[None], scores, -1e+30)
    highest = lax.optimization_barrier(jnp.max(scores, axis=-1, keepdims=True))
    expvals = jnp.exp(scores - highest)
    probs = reduced_precision(expvals / lax.optimization_barrier(jnp.sum(expvals, axis=-1, keepdims=True)))
    return jnp.einsum('hqk,khd->qhd', probs, values_all, precision=HIGHEST)

def layer_block(block, segment_block, weights):
    qkv_w, out_w, gate_up_w, down_w, gains = weights
    gain_one = gains[:D]
    gain_two = gains[D:2 * D]
    gain_query = gains[2 * D:2 * D + HEAD_WIDTH]
    gain_key = gains[2 * D + HEAD_WIDTH:]
    token_rows = block.shape[0]
    mask_allowed, cosine_table, sine_table = jax.vmap(partial(segment_tables, head_size=HEAD_WIDTH))(segment_block)
    cosine_flat = cosine_table.reshape(token_rows, 1, HEAD_WIDTH)
    sine_flat = sine_table.reshape(token_rows, 1, HEAD_WIDTH)
    normed_one = reduced_precision(block * rms_scale(block) * gain_one)
    mixed_output = low_back(jnp.dot(normed_one, qkv_w.T, precision=HIGHEST))
    raw_queries = mixed_output[:, :QUERY_HEADS * HEAD_WIDTH].reshape(token_rows, QUERY_HEADS, HEAD_WIDTH)
    unrotated_keys = mixed_output[:, QUERY_HEADS * HEAD_WIDTH:(QUERY_HEADS + KEY_VALUE_HEADS) * HEAD_WIDTH].reshape(token_rows, KEY_VALUE_HEADS, HEAD_WIDTH)
    value_rows_reduced = reduced_precision(mixed_output[:, (QUERY_HEADS + KEY_VALUE_HEADS) * HEAD_WIDTH:].reshape(token_rows, KEY_VALUE_HEADS, HEAD_WIDTH))
    normed_q = raw_queries * rms_scale(raw_queries) * gain_query
    normed_k = unrotated_keys * rms_scale(unrotated_keys) * gain_key
    query_rows_reduced = reduced_precision(normed_q * cosine_flat + rotate_half(normed_q) * sine_flat)
    key_rows_reduced = reduced_precision(normed_k * cosine_flat + rotate_half(normed_k) * sine_flat)
    context_output = jax.vmap(attend_mask)(query_rows_reduced.reshape(MICRO_BATCHES, MICRO_TOKENS, QUERY_HEADS, HEAD_WIDTH), key_rows_reduced.reshape(MICRO_BATCHES, MICRO_TOKENS, KEY_VALUE_HEADS, HEAD_WIDTH), value_rows_reduced.reshape(MICRO_BATCHES, MICRO_TOKENS, KEY_VALUE_HEADS, HEAD_WIDTH), mask_allowed)
    context_low = low_back(reduced_precision(context_output.reshape(token_rows, QUERY_HEADS * HEAD_WIDTH)))
    middle = block + low_back(jnp.dot(context_low, out_w.T, precision=HIGHEST))
    normed_two = reduced_precision(middle * rms_scale(middle) * gain_two)
    gate_up = low_back(jnp.dot(normed_two, gate_up_w.T, precision=HIGHEST))
    hidden_low = reduced_precision(jax.nn.silu(gate_up[:, :FF]) * gate_up[:, FF:])
    return middle + low_back(jnp.dot(hidden_low, down_w.T, precision=HIGHEST))

def adamw(weight, first, second, grad, rate, decay):
    first_new = BETA_ONE * first + (1.0 - BETA_ONE) * grad
    second_new = BETA_TWO * second + (1.0 - BETA_TWO) * grad * grad
    corrected = first_new / (1.0 - BETA_ONE ** STEP) / (jnp.sqrt(second_new / (1.0 - BETA_TWO ** STEP)) + ADAM_EPS)
    return (weight - rate * (corrected + decay * weight), first_new, second_new)

def reference(activations, segment_ids, out_grad, qkv_weight, qkv_first, qkv_second, out_weight, out_first, out_second, gate_up_weight, gate_up_first, gate_up_second, down_weight, down_first, down_second, norm_gains, gains_first, gains_second):
    seg_blocks = segment_ids.reshape(N_DP, MICRO_BATCHES, MICRO_TOKENS)

    def forward(inputs, qkv_w, out_w, gate_up_w, down_w, gains):
        weights = (reduced_precision(qkv_w), reduced_precision(out_w), reduced_precision(gate_up_w), reduced_precision(down_w), reduced_precision(gains))
        blocks = inputs.reshape(N_DP, TOK_DEV, D)

        def one_device(pair):
            return layer_block(pair[0], pair[1], weights)
        result = lax.map(jax.checkpoint(one_device), (blocks, seg_blocks))
        return result.reshape(TOKENS, D)
    layer_output, pullback = jax.vjp(forward, activations, qkv_weight, out_weight, gate_up_weight, down_weight, norm_gains)
    grads = pullback(out_grad)
    qkv_new = adamw(qkv_weight, qkv_first, qkv_second, grads[1], 0.06, 0.1)
    out_new = adamw(out_weight, out_first, out_second, grads[2], 0.25, 0.1)
    gate_up_new = adamw(gate_up_weight, gate_up_first, gate_up_second, grads[3], 0.06, 0.1)
    down_new = adamw(down_weight, down_first, down_second, grads[4], 0.04, 0.1)
    gains_new = adamw(norm_gains, gains_first, gains_second, grads[5], 0.3, 0.0)
    return (layer_output, grads[0], qkv_new[0], qkv_new[1], qkv_new[2], out_new[0], out_new[1], out_new[2], gate_up_new[0], gate_up_new[1], gate_up_new[2], down_new[0], down_new[1], down_new[2], gains_new[0], gains_new[1], gains_new[2])
```

```python
import functools

import jax
import jax.numpy as jnp
from jax import lax
from jax.experimental import pallas as pl
from jax.experimental.pallas import tpu as pltpu
from jax.sharding import PartitionSpec as P

D = 1024
QUERY_HEADS = 16
KEY_VALUE_HEADS = 8
HEAD_WIDTH = 128
FF = 3072
STEP = 10


NORM_EPS = 1e-06
ROPE_BASE = 1000000.0
BETA_ONE = 0.9
BETA_TWO = 0.95
ADAM_EPS = 1e-08


def contract_last(left_side, right_side):
    return lax.dot_general(
        left_side, right_side, (((1,), (1,)), ((), ())), preferred_element_type=jnp.float32
    )


def contract_first(left_side, right_side):
    return lax.dot_general(
        left_side, right_side, (((0,), (0,)), ((), ())), preferred_element_type=jnp.float32
    )


def plain_product(left_side, right_side):
    return jnp.dot(left_side, right_side, preferred_element_type=jnp.float32)


def rms_scale(values):
    return lax.rsqrt(jnp.mean(values * values, axis=-1, keepdims=True) + NORM_EPS)


class Grid:
    def __init__(self, count):
        chips = count // 2
        flat = 2 if chips <= 16 else 4
        self.size = {"z": chips // (flat * flat), "y": flat, "x": flat, "c": 2}
        self.step = {"z": 2 * flat * flat, "y": 2 * flat, "x": 2, "c": 1}
        self.count = count

    def at(self, axis):
        return (lax.axis_index("dp") // self.step[axis]) % self.size[axis]

    def ahead(self, axis, hops):
        return (self.at(axis) + hops) % self.size[axis]

    def hops(self, axis):
        return range(1, self.size[axis])

    def shift(self, value, axis, hops):
        size, step = self.size[axis], self.step[axis]
        pairs = []
        for device in range(self.count):
            here = (device // step) % size
            pairs.append((device, device + ((here + hops) % size - here) * step))
        return lax.ppermute(value, "dp", pairs)


def after(value, *others):
    return lax.optimization_barrier((value,) + others)[0]


GROUP = QUERY_HEADS // KEY_VALUE_HEADS
SCORE_SCALE = HEAD_WIDTH ** (-0.5)
VMEM_BYTES = 56 * 1024 * 1024


def norm_backward(values, scale_rows, gain, grad_out):
    scaled = gain * grad_out
    grad_in = scale_rows * scaled - values * scale_rows**3 * jnp.mean(
        scaled * values, axis=-1, keepdims=True
    )
    return (grad_in, grad_out * values * scale_rows)


def z_pieces(grid, shard, chained, *dependencies):
    moved = [shard]
    for hops in grid.hops("z"):
        moved.append(grid.shift(after(shard, *dependencies) if dependencies else shard, "z", hops))
        if chained:
            dependencies = (moved[-1],)
    return moved


def swap_cores(grid, pieces):
    return pieces + [
        (grid.shift(buffer, "c", 1), [dict(place, c=1) for place in places])
        for buffer, places in pieces
    ]


def plane_pieces(grid, column, *dependencies):
    places = [{"z": hops} for hops in range(column.shape[0])]
    half = column.shape[0] // 2
    sent = after(column, *dependencies) if dependencies else column
    from_x = {hops: grid.shift(sent, "x", hops) for hops in grid.hops("x")}
    from_y = {hops: grid.shift(sent, "y", hops) for hops in grid.hops("y")}
    pieces = [(column, places)]
    pieces += [(from_x[j], [dict(place, x=j) for place in places]) for j in from_x]
    pieces += [(from_y[l], [dict(place, y=l) for place in places]) for l in from_y]
    last = []
    for j in from_x:
        for l in from_y:
            first_half = grid.shift(from_x[j][:half], "y", l)
            second_half = grid.shift(from_y[l][half:], "x", j)
            pieces.append((first_half, [dict(place, x=j, y=l) for place in places[:half]]))
            pieces.append((second_half, [dict(place, x=j, y=l) for place in places[half:]]))
            last += [first_half, second_half]
    return pieces, last


def chip_plane(grid, shard):
    half = shard.shape[0] // 2
    from_x = {hops: grid.shift(shard, "x", hops) for hops in grid.hops("x")}
    from_y = {hops: grid.shift(shard, "y", hops) for hops in grid.hops("y")}
    shards = [shard, *from_x.values(), *from_y.values()]
    places = [{}] + [{"x": j} for j in from_x] + [{"y": l} for l in from_y]
    last = []
    for j in from_x:
        for l in from_y:
            last += [grid.shift(from_x[j][:half], "y", l), grid.shift(from_y[l][half:], "x", j)]
            shards.append(jnp.concatenate(last[-2:], axis=0))
            places.append({"x": j, "y": l})
    return jnp.stack(shards), places, last


def assemble_kernel(grid, places_of, *refs):
    pieces, out, sems = refs[: len(places_of)], refs[-2], refs[-1]
    copies = []
    for piece, places in zip(pieces, places_of):
        for slot, place in enumerate(places):
            index = 0
            for axis in ("z", "y", "x", "c"):
                size = grid.size[axis]
                index = index + (grid.at(axis) + size - place.get(axis, 0)) % size * grid.step[axis]
            copies.append(
                pltpu.make_async_copy(piece.at[slot], out.at[index], sems.at[len(copies)])
            )
    for copy in copies:
        copy.start()
    for copy in copies:
        copy.wait()


def assemble(grid, pieces):
    rows, width = pieces[0][0].shape[1:]
    gathered = pl.pallas_call(
        functools.partial(assemble_kernel, grid, [places for _, places in pieces]),
        out_shape=jax.ShapeDtypeStruct((grid.count, rows, width), jnp.bfloat16),
        in_specs=[pl.BlockSpec(memory_space=pl.ANY)] * len(pieces),
        out_specs=pl.BlockSpec(memory_space=pltpu.VMEM),
        scratch_shapes=[pltpu.SemaphoreType.DMA((grid.count,))],
        compiler_params=pltpu.CompilerParams(vmem_limit_bytes=VMEM_BYTES),
        cost_estimate=pl.CostEstimate(
            flops=0, bytes_accessed=4 * grid.count * rows * width, transcendentals=0
        ),
        name="assemble",
    )(*[buffer for buffer, _ in pieces])
    return gathered.reshape(grid.count * rows, width)


def take(value, axis, index):
    return lax.dynamic_index_in_dim(value, index, axis, keepdims=False)


def add_low(*terms):
    return sum(term.astype(jnp.float32) for term in terms).astype(jnp.bfloat16)


def split_parts(grid, partial, rows):
    size = grid.size
    return partial.reshape(size["z"], size["y"], size["x"], 2, rows, partial.shape[-1])


def reduce_cores(grid, partial):
    received = grid.shift(take(partial, 3, grid.ahead("c", 1)), "c", 1)
    return [take(partial, 3, grid.at("c")), received]


def reduce_plane(grid, block):
    here_y, here_x = grid.at("y"), grid.at("x")
    for_x = {j: [] for j in grid.hops("x")}
    for_y = {l: [] for l in grid.hops("y")}
    for j in for_x:
        for l in for_y:
            corner = block(grid.ahead("y", l), grid.ahead("x", j))
            half = corner.shape[0] // 2
            for_y[l].append(grid.shift(corner[:half], "x", j))
            for_x[j].append(grid.shift(corner[half:], "y", l))
    terms = [block(here_y, here_x)]
    for j in for_x:
        own = block(here_y, grid.ahead("x", j))
        half = own.shape[0] // 2
        sent = jnp.concatenate([own[:half], add_low(own[half:], *for_x[j])], axis=0)
        terms.append(grid.shift(sent, "x", j))
    for l in for_y:
        own = block(grid.ahead("y", l), here_x)
        half = own.shape[0] // 2
        sent = jnp.concatenate([add_low(own[:half], *for_y[l]), own[half:]], axis=0)
        terms.append(grid.shift(sent, "y", l))
    return terms


def reduce_line(grid, block):
    terms = [block(grid.at("z"))]
    for hops in grid.hops("z"):
        terms.append(grid.shift(block(grid.ahead("z", hops)), "z", hops))
    return terms


def cut(terms, *places):
    parts = []
    for term in terms:
        axis = 0
        for place in places:
            if place is None:
                axis += 1
            else:
                term = take(term, axis, place)
        parts.append(term)
    return add_low(*parts) if len(parts) > 1 else parts[0]


def total_of(terms):
    return sum(term.astype(jnp.float32) for term in terms)


def reduce_plane_first(grid, partial, rows):
    chip = reduce_cores(grid, split_parts(grid, partial, rows))
    line = reduce_plane(grid, lambda y, x: cut(chip, None, y, x))
    return total_of(reduce_line(grid, lambda z: cut(line, z)))


def reduce_line_first(grid, partial, rows):
    chip = reduce_cores(grid, split_parts(grid, partial, rows))
    plane = reduce_line(grid, lambda z: cut(chip, z))
    return total_of(reduce_plane(grid, lambda y, x: cut(plane, y, x)))


def small_sum(grid, value):
    for axis in ("c", "x", "y", "z"):
        value = value + sum(grid.shift(value, axis, hops) for hops in grid.hops(axis))
    return value


def head_scale(raw):
    return lax.rsqrt(jnp.mean(raw * raw, axis=-1, keepdims=True) + NORM_EPS)


def rotated(raw, gain, cosine, sine):
    normed = raw * head_scale(raw) * gain
    return (normed * cosine + pltpu.roll(normed, HEAD_WIDTH // 2, 1) * sine).astype(jnp.bfloat16)


def allowed_pairs(segment_column, segment_row):
    count = segment_row.shape[1]
    later = lax.broadcasted_iota(jnp.int32, (count, count), 0)
    earlier = lax.broadcasted_iota(jnp.int32, (count, count), 1)
    allowed = (segment_column == segment_row) & (earlier <= later)
    return jnp.concatenate([allowed] * GROUP, axis=0)


def group_rows(values, rows):
    return jnp.concatenate(
        [values[rows, g * HEAD_WIDTH : (g + 1) * HEAD_WIDTH] for g in range(GROUP)], axis=0
    )


def probabilities(queries, keys, allowed):
    scores = jnp.where(allowed, contract_last(queries, keys) * SCORE_SCALE, -1e30)
    powers = jnp.exp(scores - jnp.max(scores, axis=-1, keepdims=True))
    return powers / jnp.sum(powers, axis=-1, keepdims=True)


def attention_kernel(
    normed, wq, wk, wv, cosine, sine, column, row, gain_q, gain_k, raw_q, raw_k, value, context
):
    raw_q[...] = contract_last(normed[...], wq[...])
    raw_k[...] = contract_last(normed[...], wk[...])
    value[...] = contract_last(normed[...], wv[...]).astype(jnp.bfloat16)
    micro_count, micro_rows = row.shape
    for micro in range(micro_count):
        rows = slice(micro * micro_rows, (micro + 1) * micro_rows)
        cos, sin = cosine[rows, :], sine[rows, :]
        queries = jnp.concatenate(
            [
                rotated(raw_q[rows, g * HEAD_WIDTH : (g + 1) * HEAD_WIDTH], gain_q[...], cos, sin)
                for g in range(GROUP)
            ],
            axis=0,
        )
        keys = rotated(raw_k[rows, :], gain_k[...], cos, sin)
        allowed = allowed_pairs(column[rows, :], row[micro : micro + 1, :])
        probs = probabilities(queries, keys, allowed).astype(jnp.bfloat16)
        mixed = plain_product(probs, value[rows, :]).astype(jnp.bfloat16)
        for g in range(GROUP):
            context[rows, g * HEAD_WIDTH : (g + 1) * HEAD_WIDTH] = mixed[
                g * micro_rows : (g + 1) * micro_rows, :
            ]


def head_backward(raw, gain, grad_rotated, cos, sin):
    grad_normed = grad_rotated * cos - pltpu.roll(grad_rotated, HEAD_WIDTH // 2, 1) * sin
    grad_raw, terms = norm_backward(raw, head_scale(raw), gain, grad_normed)
    return grad_raw.astype(jnp.bfloat16), jnp.sum(terms, axis=0, keepdims=True)


def attention_backward_kernel(
    raw_q, raw_k, value, grad_context, cosine, sine, column, row, gain_q, gain_k,
    grad_q, grad_k, grad_v, terms_q, terms_k,
):
    @pl.when(pl.program_id(0) == 0)
    def _():
        terms_q[...] = jnp.zeros_like(terms_q)
        terms_k[...] = jnp.zeros_like(terms_k)

    micro_count, micro_rows = row.shape
    for micro in range(micro_count):
        rows = slice(micro * micro_rows, (micro + 1) * micro_rows)
        cos, sin = cosine[rows, :], sine[rows, :]
        queries = jnp.concatenate(
            [
                rotated(raw_q[rows, g * HEAD_WIDTH : (g + 1) * HEAD_WIDTH], gain_q[...], cos, sin)
                for g in range(GROUP)
            ],
            axis=0,
        )
        keys = rotated(raw_k[rows, :], gain_k[...], cos, sin)
        allowed = allowed_pairs(column[rows, :], row[micro : micro + 1, :])
        probs = probabilities(queries, keys, allowed)
        grads = group_rows(grad_context, rows)
        grad_v[rows, :] = contract_first(probs.astype(jnp.bfloat16), grads).astype(jnp.bfloat16)
        grad_probs = contract_last(grads, value[rows, :])
        centre = jnp.sum(probs * grad_probs, axis=-1, keepdims=True)
        grad_scores = (probs * (grad_probs - centre)).astype(jnp.bfloat16)
        grad_queries = plain_product(grad_scores, keys) * SCORE_SCALE
        grad_keys = contract_first(grad_scores, queries) * SCORE_SCALE
        for g in range(GROUP):
            lanes = slice(g * HEAD_WIDTH, (g + 1) * HEAD_WIDTH)
            grad_raw, terms = head_backward(
                raw_q[rows, lanes],
                gain_q[...],
                grad_queries[g * micro_rows : (g + 1) * micro_rows, :],
                cos,
                sin,
            )
            grad_q[rows, lanes] = grad_raw
            terms_q[...] += terms
        grad_raw, terms = head_backward(raw_k[rows, :], gain_k[...], grad_keys, cos, sin)
        grad_k[rows, :] = grad_raw
        terms_k[...] += terms


def whole(array):
    return pl.BlockSpec(array.shape, lambda k: (0,) * array.ndim)


def heads(rows, width, first=0):
    return pl.BlockSpec((rows, width), lambda k: (0, first + k))


def attention(normed, qkv_full, tables, gain_q, gain_k):
    tokens = normed.shape[0]
    wide = GROUP * HEAD_WIDTH
    depth = normed.shape[1]
    return pl.pallas_call(
        attention_kernel,
        grid=(KEY_VALUE_HEADS,),
        out_shape=(
            jax.ShapeDtypeStruct((tokens, QUERY_HEADS * HEAD_WIDTH), jnp.float32),
            jax.ShapeDtypeStruct((tokens, KEY_VALUE_HEADS * HEAD_WIDTH), jnp.float32),
            jax.ShapeDtypeStruct((tokens, KEY_VALUE_HEADS * HEAD_WIDTH), jnp.bfloat16),
            jax.ShapeDtypeStruct((tokens, QUERY_HEADS * HEAD_WIDTH), jnp.bfloat16),
        ),
        in_specs=[
            whole(normed),
            pl.BlockSpec((wide, depth), lambda k: (k, 0)),
            pl.BlockSpec((HEAD_WIDTH, depth), lambda k: (QUERY_HEADS + k, 0)),
            pl.BlockSpec((HEAD_WIDTH, depth), lambda k: (QUERY_HEADS + KEY_VALUE_HEADS + k, 0)),
            *[whole(table) for table in tables],
            whole(gain_q),
            whole(gain_k),
        ],
        out_specs=(
            heads(tokens, wide),
            heads(tokens, HEAD_WIDTH),
            heads(tokens, HEAD_WIDTH),
            heads(tokens, wide),
        ),
        compiler_params=pltpu.CompilerParams(vmem_limit_bytes=VMEM_BYTES),
        cost_estimate=pl.CostEstimate(
            flops=9 * 10**9, bytes_accessed=30 * 10**6, transcendentals=3 * 10**6
        ),
        name="attention",
    )(normed, qkv_full, qkv_full, qkv_full, *tables, gain_q, gain_k)


def attention_backward(raw_q, raw_k, value, grad_context, tables, gain_q, gain_k):
    tokens = raw_q.shape[0]
    wide = GROUP * HEAD_WIDTH
    return pl.pallas_call(
        attention_backward_kernel,
        grid=(KEY_VALUE_HEADS,),
        out_shape=(
            jax.ShapeDtypeStruct((tokens, QUERY_HEADS * HEAD_WIDTH), jnp.bfloat16),
            jax.ShapeDtypeStruct((tokens, KEY_VALUE_HEADS * HEAD_WIDTH), jnp.bfloat16),
            jax.ShapeDtypeStruct((tokens, KEY_VALUE_HEADS * HEAD_WIDTH), jnp.bfloat16),
            jax.ShapeDtypeStruct((1, HEAD_WIDTH), jnp.float32),
            jax.ShapeDtypeStruct((1, HEAD_WIDTH), jnp.float32),
        ),
        in_specs=[
            heads(tokens, wide),
            heads(tokens, HEAD_WIDTH),
            heads(tokens, HEAD_WIDTH),
            heads(tokens, wide),
            *[whole(table) for table in tables],
            whole(gain_q),
            whole(gain_k),
        ],
        out_specs=(
            heads(tokens, wide),
            heads(tokens, HEAD_WIDTH),
            heads(tokens, HEAD_WIDTH),
            whole(gain_q),
            whole(gain_k),
        ),
        compiler_params=pltpu.CompilerParams(vmem_limit_bytes=VMEM_BYTES),
        cost_estimate=pl.CostEstimate(
            flops=6 * 10**9, bytes_accessed=25 * 10**6, transcendentals=3 * 10**6
        ),
        name="attention_backward",
    )(raw_q, raw_k, value, grad_context, *tables, gain_q, gain_k)


def position_tables(segment_ids):
    micro_count, micro_rows = segment_ids.shape
    order = jnp.arange(micro_rows, dtype=jnp.int32)
    same = segment_ids[:, :, None] == segment_ids[:, None, :]
    earlier = order[None, :] < order[:, None]
    positions = jnp.sum(jnp.where(same & earlier[None], 1, 0), axis=2).astype(jnp.int32)
    half_size = HEAD_WIDTH // 2
    frequency = ROPE_BASE ** (-(jnp.arange(half_size, dtype=jnp.float32) * (2.0 / HEAD_WIDTH)))
    angles = positions.reshape(-1, 1).astype(jnp.float32) * frequency[None, :]
    cosine, sine = jnp.cos(angles), jnp.sin(angles)
    return (
        jnp.concatenate([cosine, cosine], axis=-1),
        jnp.concatenate([-sine, sine], axis=-1),
        segment_ids.reshape(-1, 1),
        segment_ids,
    )


def adamw(weight, first, second, grad, rate, decay):
    first_new = BETA_ONE * first + (1.0 - BETA_ONE) * grad
    second_new = BETA_TWO * second + (1.0 - BETA_TWO) * grad * grad
    corrected = (
        first_new
        / (1.0 - BETA_ONE**STEP)
        / (jnp.sqrt(second_new / (1.0 - BETA_TWO**STEP)) + ADAM_EPS)
    )
    return (weight - rate * (corrected + decay * weight), first_new, second_new)


def per_device(
    grid,
    activations,
    segment_ids,
    out_grad,
    qkv_weight,
    qkv_first,
    qkv_second,
    out_weight,
    out_first,
    out_second,
    gate_up_weight,
    gate_up_first,
    gate_up_second,
    down_weight,
    down_first,
    down_second,
    norm_gains,
    gains_first,
    gains_second,
):
    qkv_low = qkv_weight.astype(jnp.bfloat16)
    out_low = out_weight.astype(jnp.bfloat16)
    gate_up_low = gate_up_weight.astype(jnp.bfloat16)
    down_low = down_weight.astype(jnp.bfloat16)

    own_gains = norm_gains.astype(jnp.bfloat16).astype(jnp.float32)
    gain_count = own_gains.shape[0]
    gain_start = lax.axis_index("dp") * gain_count
    all_gains = jnp.zeros((1, gain_count * grid.count), jnp.float32)
    all_gains = lax.dynamic_update_slice(all_gains, own_gains[None], (0, gain_start))
    all_gains = small_sum(grid, all_gains)
    gain_one, gain_two = all_gains[:, :D], all_gains[:, D : 2 * D]
    gain_query = all_gains[:, 2 * D : 2 * D + HEAD_WIDTH]
    gain_key = all_gains[:, 2 * D + HEAD_WIDTH :]

    qkv_line = z_pieces(grid, qkv_low, False)
    down_chip, down_places, down_last = chip_plane(grid, down_low)
    qkv_pieces, qkv_last = plane_pieces(grid, jnp.stack(qkv_line), *down_last)
    out_line = z_pieces(grid, out_low, True, *qkv_line[1:])
    out_pieces, out_last = plane_pieces(grid, jnp.stack(out_line), *qkv_last)
    gate_up_line = z_pieces(grid, gate_up_low, True, *out_line[-1:])
    gate_up_pieces, _ = plane_pieces(grid, jnp.stack(gate_up_line), *out_last)
    down_line = z_pieces(grid, down_chip, True, *gate_up_line[-1:])
    down_pieces = [
        (buffer, [dict(place, z=hops) for place in down_places])
        for hops, buffer in enumerate(down_line)
    ]
    qkv_full = assemble(grid, swap_cores(grid, qkv_pieces))
    out_full = assemble(grid, swap_cores(grid, out_pieces))
    gate_up_full = assemble(grid, swap_cores(grid, gate_up_pieces))
    down_full = assemble(grid, swap_cores(grid, down_pieces))

    tables = position_tables(segment_ids)
    scale_one = rms_scale(activations)
    normed_one = (activations * scale_one * gain_one).astype(jnp.bfloat16)
    raw_q, raw_k, value, context = attention(normed_one, qkv_full, tables, gain_query, gain_key)
    middle = activations + contract_last(context, out_full)
    scale_two = rms_scale(middle)
    normed_two = (middle * scale_two * gain_two).astype(jnp.bfloat16)
    gate = contract_last(normed_two, gate_up_full[:FF])
    upward = contract_last(normed_two, gate_up_full[FF:])
    hidden = (jax.nn.silu(gate) * upward).astype(jnp.bfloat16)
    layer_output = middle + contract_last(hidden, down_full)

    grad_feed = out_grad.astype(jnp.bfloat16)
    down_part = contract_first(grad_feed, hidden).astype(jnp.bfloat16)
    grad_hidden = plain_product(grad_feed, down_full)
    sigma = jax.nn.sigmoid(gate)
    grad_gate = (grad_hidden * upward * sigma * (1.0 + gate * (1.0 - sigma))).astype(jnp.bfloat16)
    grad_upward = (grad_hidden * gate * sigma).astype(jnp.bfloat16)
    gate_part = contract_first(grad_gate, normed_two).astype(jnp.bfloat16)
    up_part = contract_first(grad_upward, normed_two).astype(jnp.bfloat16)
    gate_up_part = jnp.concatenate([gate_part, up_part], axis=0)
    grad_normed_two = plain_product(grad_gate, gate_up_full[:FF]) + plain_product(
        grad_upward, gate_up_full[FF:]
    )
    grad_middle, gain_two_terms = norm_backward(middle, scale_two, gain_two, grad_normed_two)
    grad_middle = out_grad + grad_middle
    grad_branch = grad_middle.astype(jnp.bfloat16)
    out_part = contract_first(grad_branch, context).astype(jnp.bfloat16)
    grad_context = plain_product(grad_branch, out_full).astype(jnp.bfloat16)
    grad_q, grad_k, grad_v, query_terms, key_terms = attention_backward(
        raw_q, raw_k, value, grad_context, tables, gain_query, gain_key
    )
    qkv_part = jnp.concatenate(
        [contract_first(part, normed_one).astype(jnp.bfloat16) for part in (grad_q, grad_k, grad_v)],
        axis=0,
    )
    bounds = (QUERY_HEADS * HEAD_WIDTH, (QUERY_HEADS + KEY_VALUE_HEADS) * HEAD_WIDTH)
    grad_normed_one = (
        plain_product(grad_q, qkv_full[: bounds[0]])
        + plain_product(grad_k, qkv_full[bounds[0] : bounds[1]])
        + plain_product(grad_v, qkv_full[bounds[1] :])
    )
    grad_block, gain_one_terms = norm_backward(activations, scale_one, gain_one, grad_normed_one)
    input_grad = grad_middle + grad_block
    gains_part = jnp.concatenate(
        [
            jnp.sum(gain_one_terms, axis=0, keepdims=True),
            jnp.sum(gain_two_terms, axis=0, keepdims=True),
            query_terms,
            key_terms,
        ],
        axis=1,
    )

    down_total = reduce_line_first(grid, down_part, down_low.shape[0])
    gate_up_total = reduce_plane_first(grid, gate_up_part, gate_up_low.shape[0])
    out_total = reduce_plane_first(grid, out_part, out_low.shape[0])
    qkv_total = reduce_plane_first(grid, qkv_part, qkv_low.shape[0])
    gains_total = small_sum(grid, gains_part)
    gains_total = lax.dynamic_slice(gains_total, (0, gain_start), (1, gain_count))[0]

    return (
        layer_output,
        input_grad,
        *adamw(qkv_weight, qkv_first, qkv_second, qkv_total, 0.06, 0.1),
        *adamw(out_weight, out_first, out_second, out_total, 0.25, 0.1),
        *adamw(gate_up_weight, gate_up_first, gate_up_second, gate_up_total, 0.06, 0.1),
        *adamw(down_weight, down_first, down_second, down_total, 0.04, 0.1),
        *adamw(norm_gains, gains_first, gains_second, gains_total, 0.3, 0.0),
    )


def solution(mesh):
    return jax.shard_map(
        functools.partial(per_device, Grid(mesh.shape["dp"])),
        mesh=mesh,
        in_specs=(
            P("dp", None),
            P("dp", None),
            P("dp", None),
            P("dp", None),
            P("dp", None),
            P("dp", None),
            P("dp", None),
            P("dp", None),
            P("dp", None),
            P("dp", None),
            P("dp", None),
            P("dp", None),
            P("dp", None),
            P("dp", None),
            P("dp", None),
            P("dp"),
            P("dp"),
            P("dp"),
        ),
        out_specs=(
            P("dp", None),
            P("dp", None),
            P("dp", None),
            P("dp", None),
            P("dp", None),
            P("dp", None),
            P("dp", None),
            P("dp", None),
            P("dp", None),
            P("dp", None),
            P("dp", None),
            P("dp", None),
            P("dp", None),
            P("dp", None),
            P("dp"),
            P("dp"),
            P("dp"),
        ),
        check_vma=False,
    )
```

```python
import functools
import itertools
import math

import jax
import jax.numpy as jnp
from jax import lax
from jax.experimental import pallas as pl
from jax.experimental.pallas import tpu as pltpu
from jax.sharding import PartitionSpec as P

D = 1024
QUERY_HEADS = 16
KEY_VALUE_HEADS = 8
HEAD_WIDTH = 128
FF = 3072
STEP = 10


NORM_EPS = 1e-06
ROPE_BASE = 1000000.0
BETA_ONE = 0.9
BETA_TWO = 0.95
ADAM_EPS = 1e-08


def contract_last(left_side, right_side):
    return lax.dot_general(
        left_side, right_side, (((1,), (1,)), ((), ())), preferred_element_type=jnp.float32
    )


def contract_first(left_side, right_side):
    return lax.dot_general(
        left_side, right_side, (((0,), (0,)), ((), ())), preferred_element_type=jnp.float32
    )


def plain_product(left_side, right_side):
    return jnp.dot(left_side, right_side, preferred_element_type=jnp.float32)


def rms_scale(values):
    return lax.rsqrt(jnp.mean(values * values, axis=-1, keepdims=True) + NORM_EPS)


class Grid:
    def __init__(self, count):
        chips = count // 2
        flat = 2 if chips <= 16 else 4
        self.size = {"z": chips // (flat * flat), "y": flat, "x": flat, "c": 2}
        self.step = {"z": 2 * flat * flat, "y": 2 * flat, "x": 2, "c": 1}
        self.count = count

    def at(self, axis):
        return (lax.axis_index("dp") // self.step[axis]) % self.size[axis]

    def ahead(self, axis, hops):
        return (self.at(axis) + hops) % self.size[axis]

    def hops(self, axis):
        return range(1, self.size[axis])

    def shift(self, value, axis, hops):
        size, step = self.size[axis], self.step[axis]
        pairs = []
        for device in range(self.count):
            here = (device // step) % size
            pairs.append((device, device + ((here + hops) % size - here) * step))
        return lax.ppermute(value, "dp", pairs)


def after(value, *others):
    return lax.optimization_barrier((value, *jax.tree.leaves(others)))[0]


GROUP = QUERY_HEADS // KEY_VALUE_HEADS
SCORE_SCALE = HEAD_WIDTH ** (-0.5)
EXP2_SCALE = SCORE_SCALE * math.log2(math.e)
VMEM_BYTES = 60 * 1024 * 1024
VMEM_LESS = 50 * 1024 * 1024


def norm_backward(values, scale_rows, gain, grad_out):
    scaled = gain * grad_out
    grad_in = scale_rows * scaled - values * scale_rows**3 * jnp.mean(
        scaled * values, axis=-1, keepdims=True
    )
    return (grad_in, grad_out * values * scale_rows)


def z_pieces(grid, shard, chained, *dependencies):
    moved = [shard]
    for hops in grid.hops("z"):
        moved.append(grid.shift(after(shard, *dependencies) if dependencies else shard, "z", hops))
        if chained:
            dependencies = (moved[-1],)
    return moved


def swap_tree(grid, buffers):
    return jax.tree.map(lambda buffer: grid.shift(buffer, "c", 1), buffers)


def plane_sides(grid, column, *dependencies):
    sent = after(column, *dependencies) if dependencies else column
    from_x = {hops: grid.shift(sent, "x", hops) for hops in grid.hops("x")}
    from_y = {hops: grid.shift(sent, "y", hops) for hops in grid.hops("y")}
    return from_x, from_y


def plane_corners(grid, sides, *dependencies, halved=True):
    from_x, from_y = sides
    half = from_x[1].shape[0] // 2
    corners = {}
    for j in from_x:
        for l in from_y:
            first, second = from_x[j], from_y[l]
            if halved:
                first, second = first[:half], second[half:]
            if dependencies:
                first, second = after(first, *dependencies), after(second, *dependencies)
            corners[j, l] = (grid.shift(first, "y", l), grid.shift(second, "x", j))
    return corners


def corner_pieces(planes, corners):
    half = len(planes) // 2
    pieces = []
    for (j, l), (first, second) in corners.items():
        pieces.append((first, [{"z": hops, "x": j, "y": l} for hops in planes[:half]]))
        pieces.append((second, [{"z": hops, "x": j, "y": l} for hops in planes[half:]]))
    return pieces


def plane_pieces(planes, column, sides, corners):
    from_x, from_y = sides
    pieces = [(column, [{"z": hops} for hops in planes])]
    pieces += [(from_x[j], [{"z": hops, "x": j} for hops in planes]) for j in from_x]
    pieces += [(from_y[l], [{"z": hops, "y": l} for hops in planes]) for l in from_y]
    return pieces + corner_pieces(planes, corners)


def after_tree(tree, *dependencies):
    leaves, shape = jax.tree.flatten(tree)
    tied = lax.optimization_barrier((*leaves, *flat(dependencies)))
    return jax.tree.unflatten(shape, tied[: len(leaves)])


def flat(*groups):
    return [leaf for leaf in jax.tree.leaves(groups)]


def chip_plane(shard, sides_received, corners_received):
    from_x, from_y = sides_received
    shards = [shard, *from_x.values(), *from_y.values()]
    places = [{}] + [{"x": j} for j in from_x] + [{"y": l} for l in from_y]
    for (j, l), pair in corners_received.items():
        shards.append(jnp.concatenate(pair, axis=0))
        places.append({"x": j, "y": l})
    return jnp.stack(shards), places


def assemble_kernel(grid, places_of, *refs):
    pieces, (out, held, came, went) = refs[: len(places_of)], refs[-4:]
    moves = []
    for piece, places in zip(pieces, places_of):
        for slot, place in enumerate(places):
            index = 0
            for axis in ("z", "y", "x", "c"):
                size = grid.size[axis]
                index = index + (grid.at(axis) + size - place.get(axis, 0)) % size * grid.step[axis]
            at = (index,) if "rows" not in place else (index, pl.ds(*place["rows"]))
            number = len(moves)
            moves.append(
                (
                    pltpu.make_async_copy(piece.at[slot], held.at[at], came.at[number]),
                    pltpu.make_async_copy(held.at[at], out.at[at], went.at[number]),
                )
            )
    for arrive, _ in moves:
        arrive.start()
    for arrive, leave in moves:
        arrive.wait()
        leave.start()
    for _, leave in moves:
        leave.wait()


def down_pieces(buffers, places):
    own, one, three, low, high = buffers
    count = low.shape[1]
    pieces = [
        (buffer, [dict(place, z=hops) for place in places])
        for buffer, hops in ((own, 0), (one, 1), (three, 3))
    ]
    for buffer, start in ((low, 0), (high, count)):
        pieces.append((buffer, [dict(place, z=2, rows=(start, count)) for place in places]))
    return pieces


def assemble(grid, own_pieces, swapped_pieces):
    pieces = own_pieces + [
        (buffer, [dict(place, c=1) for place in places]) for buffer, places in swapped_pieces
    ]
    rows, width = pieces[0][0].shape[1:]
    dims = (grid.count, rows, width)
    moves = sum(len(places) for _, places in pieces)
    gathered = pl.pallas_call(
        functools.partial(assemble_kernel, grid, [places for _, places in pieces]),
        out_shape=jax.ShapeDtypeStruct(dims, jnp.bfloat16),
        in_specs=[pl.BlockSpec(memory_space=pl.ANY)] * len(pieces),
        out_specs=pl.BlockSpec(memory_space=pl.ANY),
        scratch_shapes=[
            pltpu.VMEM(dims, jnp.bfloat16),
            pltpu.SemaphoreType.DMA((moves,)),
            pltpu.SemaphoreType.DMA((moves,)),
        ],
        compiler_params=pltpu.CompilerParams(vmem_limit_bytes=VMEM_BYTES),
        cost_estimate=LITTLE,
        name="assemble",
    )(*[buffer for buffer, _ in pieces])
    return gathered.reshape(grid.count * rows, width)


@jax.tree_util.register_pytree_node_class
class Source:
    def __init__(self, array, first=0):
        self.array, self.first = array, first

    def tree_flatten(self):
        return (self.array,), self.first

    @classmethod
    def tree_unflatten(cls, first, leaves):
        return cls(*leaves, first)


class Merge:
    STRIP = 16

    def __init__(self, grid):
        self.grid = grid
        self.scalars, self.inputs, self.outputs, self.keys = [], [], [], {}

    def scalar(self, value):
        if id(value) not in self.keys:
            self.keys[id(value)] = len(self.scalars)
            self.scalars.append(value)
        return self.keys[id(value)]

    def cut(self, array, places):
        key = (id(array), tuple(None if place is None else id(place) for place in places))
        if key not in self.keys:
            self.keys[key] = len(self.inputs)
            self.inputs.append((array, places))
        return self.keys[key]

    def terms(self, sources, places, low, high):
        found = []
        for source in sources:
            first = source.first
            if first <= low and high <= first + source.array.shape[-2]:
                found.append((self.cut(source.array, places), low - first, high - first))
        return found

    def add(self, *options, chosen=None):
        self.outputs.append((options, None if chosen is None else self.scalar(chosen)))
        return len(self.outputs) - 1

    def shape(self, options):
        array, places = self.inputs[options[0][0][0][0]]
        lead = [size for size, place in zip(array.shape, places) if place is None]
        rows = sum(segment[0][2] - segment[0][1] for segment in options[0])
        return (*lead, rows, array.shape[-1])

    def run(self):
        edges = [
            edge
            for options, _ in self.outputs
            for segments in options
            for segment in segments
            for term in segment
            for edge in term[1:]
        ]
        if any(edge % self.STRIP for edge in edges):
            return self.run_plain()
        shapes = [self.shape(options) for options, _ in self.outputs]
        for _, places in self.inputs:
            for place in places:
                if place is not None:
                    self.scalar(place)
        numbers = jnp.stack([value.astype(jnp.int32) for value in self.scalars])

        def spec(array, places):
            block = [
                None if place is not None else size for size, place in zip(array.shape, places)
            ]
            picks = [None if place is None else self.scalar(place) for place in places]
            return pl.BlockSpec(
                (*block, *array.shape[-2:]),
                lambda step, held: (*[0 if pick is None else held[pick] for pick in picks], 0, 0),
            )

        return pl.pallas_call(
            self.kernel,
            grid_spec=pltpu.PrefetchScalarGridSpec(
                num_scalar_prefetch=1,
                grid=(1,),
                in_specs=[spec(*pair) for pair in self.inputs],
                out_specs=[
                    pl.BlockSpec(dims, lambda step, held, axes=len(dims): (0,) * axes)
                    for dims in shapes
                ],
            ),
            out_shape=[jax.ShapeDtypeStruct(dims, jnp.bfloat16) for dims in shapes],
            compiler_params=pltpu.CompilerParams(vmem_limit_bytes=VMEM_LESS),
            cost_estimate=LITTLE,
            name="merge",
        )(numbers, *[array for array, _ in self.inputs])

    def kernel(self, held, *refs):
        inputs, outputs = refs[: len(self.inputs)], refs[len(self.inputs) :]
        for out, (options, chosen) in zip(outputs, self.outputs):
            for number, segments in enumerate(options):
                write = functools.partial(self.write, out, segments, inputs)
                if chosen is None:
                    write()
                else:
                    pl.when(held[chosen] == number)(write)

    def write(self, out, segments, inputs):
        start = 0
        for segment in segments:
            count = segment[0][2] - segment[0][1]
            for lead in itertools.product(*[range(size) for size in out.shape[:-2]]):

                @pl.loop(0, count // self.STRIP)
                def _(strip, start=start, lead=lead, segment=segment):
                    def rows(first):
                        at = pl.multiple_of(first + strip * self.STRIP, self.STRIP)
                        return (*lead, pl.ds(at, self.STRIP), slice(None))

                    added = sum(inputs[k][rows(low)].astype(jnp.float32) for k, low, _ in segment)
                    out[rows(start)] = added.astype(jnp.bfloat16)

            start += count

    def run_plain(self):
        def part(term):
            array, places = self.inputs[term[0]]
            axis = 0
            for place in places:
                if place is None:
                    axis += 1
                else:
                    array = lax.dynamic_index_in_dim(array, place, axis, keepdims=False)
            return lax.slice_in_dim(array, term[1], term[2], axis=-2 + array.ndim)

        results = []
        for options, chosen in self.outputs:
            made = []
            for segments in options:
                sums = [
                    sum(part(term).astype(jnp.float32) for term in segment).astype(jnp.bfloat16)
                    for segment in segments
                ]
                made.append(jnp.concatenate(sums, axis=-2) if len(sums) > 1 else sums[0])
            if chosen is None:
                results.append(made[0])
            else:
                results.append(lax.select_n(self.scalars[chosen].astype(jnp.int32), *made) if len(made) > 2
                               else jnp.where(self.scalars[chosen] == 0, made[0], made[1]))
        return results


def swapped(grid, kept_and_sent):
    kept, sent = kept_and_sent
    return [Source(kept), Source(grid.shift(sent, "c", 1))]


def halves_of(sources):
    rows = sources[0].array.shape[-2]
    return (0, rows // 2), (rows // 2, rows)


def corners(merge, here, sources, lead=1):
    low, high = halves_of(sources)
    grid, whole_axes = merge.grid, (None,) * lead
    slots = {}
    for j in grid.hops("x"):
        for l in grid.hops("y"):
            place = (*whole_axes, here("y", l), here("x", j))
            slots[j, l] = (
                merge.add([merge.terms(sources, place, *low)]),
                merge.add([merge.terms(sources, place, *high)]),
            )

    def go(made):
        return {
            (j, l): (grid.shift(made[first], "x", j), grid.shift(made[second], "y", l))
            for (j, l), (first, second) in slots.items()
        }

    return go


def sides(merge, here, sources, crossed, lead=1):
    low, high = halves_of(sources)
    grid, whole_axes = merge.grid, (None,) * lead
    own_place = (*whole_axes, here("y", 0), here("x", 0))
    bare = (None,) * lead
    own = merge.add([merge.terms(sources, own_place, *half) for half in (low, high)])
    to_x, to_y = {}, {}
    for j in grid.hops("x"):
        place = (*whole_axes, here("y", 0), here("x", j))
        received = [Source(crossed[j, l][1], high[0]) for l in grid.hops("y")]
        to_x[j] = merge.add(
            [
                merge.terms(sources, place, *low),
                merge.terms(sources, place, *high) + merge.terms(received, bare, *high),
            ]
        )
    for l in grid.hops("y"):
        place = (*whole_axes, here("y", l), here("x", 0))
        received = [Source(crossed[j, l][0]) for j in grid.hops("x")]
        to_y[l] = merge.add(
            [
                merge.terms(sources, place, *low) + merge.terms(received, bare, *low),
                merge.terms(sources, place, *high),
            ]
        )

    def go(made):
        terms = [made[own]]
        terms += [grid.shift(made[to_x[j]], "x", j) for j in to_x]
        terms += [grid.shift(made[to_y[l]], "y", l) for l in to_y]
        return [Source(term) for term in terms]

    return go


def line(merge, here, groups, hops, rows=None, lead=0):
    grid = merge.grid
    plane = here("z", hops)
    options = []
    for sources, planes in groups:
        index = sum(jnp.where(plane == number, at, 0) for at, number in enumerate(planes))
        place = (index, *(None,) * lead)
        parts = halves_of(sources) if rows is None else (rows,)
        options.append([merge.terms(sources, place, *part) for part in parts])
    chosen = None
    if len(groups) > 1:
        chosen = sum(
            jnp.where(plane == number, group, 0)
            for group, (_, planes) in enumerate(groups)
            for number in planes
        )
    slot = merge.add(*options, chosen=chosen)
    return lambda made: grid.shift(made[slot], "z", hops) if hops else made[slot]


def total_of(*terms):
    return sum(term.astype(jnp.float32) for term in terms)


class Steps:
    def __init__(self, **live):
        self.__dict__.update(live)

    def close(self):
        self.__dict__.update(after_tree(dict(self.__dict__)))

    def drop(self, *names):
        for name in names:
            del self.__dict__[name]


def small_sum(grid, value, axes):
    for axis in axes:
        value = value + sum(grid.shift(value, axis, hops) for hops in grid.hops(axis))
    return value


LITTLE = pl.CostEstimate(flops=1, bytes_accessed=1, transcendentals=0)


def whole(array):
    return pl.BlockSpec(array.shape, lambda *k: (0,) * array.ndim)


def in_vmem(array):
    return pl.BlockSpec(memory_space=pltpu.VMEM)


def kernel_call(
    body, name, grid, in_specs, out_shape, out_specs, scratch=(), aliases=None, vmem=VMEM_BYTES
):
    return pl.pallas_call(
        body,
        grid=grid,
        in_specs=in_specs,
        out_shape=out_shape,
        out_specs=out_specs,
        scratch_shapes=scratch,
        input_output_aliases=aliases or {},
        compiler_params=pltpu.CompilerParams(vmem_limit_bytes=vmem),
        cost_estimate=LITTLE,
        name=name,
    )


def shape_of(dims, dtype):
    return jax.ShapeDtypeStruct(dims, dtype)


TRIO = (GROUP + 1) * HEAD_WIDTH


def lanes_of(head):
    return slice(head * HEAD_WIDTH, (head + 1) * HEAD_WIDTH)


def turned(values):
    return pltpu.roll(values, HEAD_WIDTH // 2, 1)


def stacked(values, rows, heads=GROUP):
    return jnp.concatenate([values[rows, lanes_of(g)] for g in range(heads)], axis=0)


def query_blocks(micro_rows):
    half = micro_rows // 2
    return [(0, half), (half, micro_rows)]


def powers_of(queries, keys, bias):
    return jnp.exp2(contract_last(queries, keys) * EXP2_SCALE + bias)


def group_bias(bias, micro, begin, end):
    return jnp.concatenate([bias[micro, begin:end, :end]] * GROUP, axis=0)


def attention_kernel(normed, wq, wk, wv, cosine, sine, bias, gain_q, gain_k, *outputs):
    norms, scales, turns, value, context = outputs[-5:]
    norms[:, : GROUP * HEAD_WIDTH] = contract_last(normed[...], wq[...])
    norms[:, GROUP * HEAD_WIDTH :] = contract_last(normed[...], wk[...])
    value[...] = contract_last(normed[...], wv[...]).astype(jnp.bfloat16)
    micro_count, micro_rows, _ = bias.shape
    for micro in range(micro_count):
        start = micro * micro_rows
        rows = slice(start, start + micro_rows)
        for head in range(GROUP + 1):
            raw = norms[rows, lanes_of(head)]
            scale = lax.rsqrt(jnp.mean(raw * raw, axis=-1, keepdims=True) + NORM_EPS)
            scale = jnp.broadcast_to(scale, raw.shape)
            normal = raw * scale
            gained = normal * (gain_q[...] if head < GROUP else gain_k[...])
            norms[rows, lanes_of(head)] = normal
            scales[rows, lanes_of(head)] = scale
            turns[rows, lanes_of(head)] = (
                gained * cosine[rows, :] + turned(gained) * sine[rows, :]
            ).astype(jnp.bfloat16)
        keys = turns[rows, lanes_of(GROUP)]
        for begin, end in query_blocks(micro_rows):
            block = slice(start + begin, start + end)
            count = end - begin
            powers = powers_of(
                stacked(turns, block), keys[:end], group_bias(bias, micro, begin, end)
            )
            inverse = 1.0 / jnp.sum(powers, axis=-1, keepdims=True)
            probs = (powers * inverse).astype(jnp.bfloat16)
            mixed = plain_product(probs, value[start : start + end, :]).astype(jnp.bfloat16)
            for g in range(GROUP):
                context[block, lanes_of(g)] = mixed[g * count : (g + 1) * count, :]


def with_turn(values):
    return jnp.concatenate([values, turned(values)], axis=1)


def head_backward(normal, scale, gain, grad, cos, sin):
    grad_normed = (grad[:, :HEAD_WIDTH] * cos - grad[:, HEAD_WIDTH:] * sin) * SCORE_SCALE
    scaled = gain * grad_normed
    terms = grad_normed * normal
    mean = jnp.mean(scaled * normal, axis=-1, keepdims=True)
    grad_raw = scale * (scaled - normal * mean)
    return grad_raw.astype(jnp.bfloat16), jnp.sum(terms, axis=0, keepdims=True)


def put_by_core(rows_per_device, grad, normed, part, at, plane, kept, sent, sems, sem):
    result = contract_first(grad[...], normed[...]).astype(jnp.bfloat16)
    rows = result.shape[0]
    if rows >= 2 * rows_per_device:
        chips = rows // (2 * rows_per_device)
        part[0], part[1] = by_core(rows_per_device, result)
        stretch = pl.ds(at * chips, chips)
        return [
            pltpu.make_async_copy(part.at[0], kept.at[plane, stretch], sems.at[sem]),
            pltpu.make_async_copy(part.at[1], sent.at[plane, stretch], sems.at[sem + 1]),
        ]
    part[0, 0] = result
    mine = (at + lax.axis_index("dp")) % 2 == 0
    return [
        Either(
            mine,
            pltpu.make_async_copy(part.at[0, 0], kept.at[plane, at // 2], sems.at[sem]),
            pltpu.make_async_copy(part.at[0, 0], sent.at[plane, at // 2], sems.at[sem + 1]),
        )
    ]


class Either:
    def __init__(self, first_one, first, second):
        self.first_one, self.first, self.second = first_one, first, second

    def start(self):
        pl.when(self.first_one)(self.first.start)
        pl.when(jnp.logical_not(self.first_one))(self.second.start)

    def wait(self):
        pl.when(self.first_one)(self.first.wait)
        pl.when(jnp.logical_not(self.first_one))(self.second.wait)


def attention_backward_kernel(
    first, rows_per_device, held, norms, scales, turns, value, grad_context, cosine, sine, bias,
    gain_q, gain_k, normed, wq, wk, wv, *others,
):
    grad_q, grad_k, grad_v, part_q, part_k, part_v, sems = others[-7:]
    kv_kept, kv_sent, total, terms_q, terms_k = others[-12:-7]

    @pl.when(pl.program_id(0) == 0)
    def _():
        terms_q[...] = jnp.zeros_like(terms_q)
        terms_k[...] = jnp.zeros_like(terms_k)
        if held:
            total[...] = others[0][...]
        else:
            total[...] = jnp.zeros_like(total)

    micro_count, micro_rows, _ = bias.shape
    for micro in range(micro_count):
        start = micro * micro_rows
        rows = slice(start, start + micro_rows)
        keys = turns[rows, lanes_of(GROUP)]
        both_keys = with_turn(keys)
        grad_values, grad_keys = 0.0, 0.0
        for begin, end in query_blocks(micro_rows):
            block = slice(start + begin, start + end)
            count = end - begin
            cos, sin = cosine[block, :], sine[block, :]
            queries = stacked(turns, block)
            powers = powers_of(queries, keys[:end], group_bias(bias, micro, begin, end))
            probs = powers * (1.0 / jnp.sum(powers, axis=-1, keepdims=True))
            grads = stacked(grad_context, block)
            grad_probs = contract_last(grads, value[start : start + end, :])
            weighted = probs * grad_probs
            centre = jnp.sum(weighted, axis=-1, keepdims=True)
            grad_scores = (weighted - probs * centre).astype(jnp.bfloat16)
            pad = ((0, micro_rows - end), (0, 0))
            grad_values += jnp.pad(contract_first(probs.astype(jnp.bfloat16), grads), pad)
            grad_keys += jnp.pad(contract_first(grad_scores, with_turn(queries)), pad)
            grad_queries = plain_product(grad_scores, both_keys[:end])
            for g in range(GROUP):
                grad_raw, terms = head_backward(
                    norms[block, lanes_of(g)],
                    scales[block, lanes_of(g)],
                    gain_q[...],
                    grad_queries[g * count : (g + 1) * count, :],
                    cos,
                    sin,
                )
                grad_q[block, lanes_of(g)] = grad_raw
                terms_q[...] += terms
        grad_v[rows, :] = grad_values.astype(jnp.bfloat16)
        grad_raw, terms = head_backward(
            norms[rows, lanes_of(GROUP)],
            scales[rows, lanes_of(GROUP)],
            gain_k[...],
            grad_keys,
            cosine[rows, :],
            sine[rows, :],
        )
        grad_k[rows, :] = grad_raw
        terms_k[...] += terms
    head = first + pl.program_id(0)
    half = KEY_VALUE_HEADS // 2
    queries_kept, queries_sent = (kv_kept, kv_sent) if first >= half else others[-14:-12]
    copies = [
        *put_by_core(
            rows_per_device, grad_q, normed, part_q, head % half, 0, queries_kept, queries_sent, sems, 0
        ),
        *put_by_core(rows_per_device, grad_k, normed, part_k, head, 1, kv_kept, kv_sent, sems, 2),
        *put_by_core(rows_per_device, grad_v, normed, part_v, head, 2, kv_kept, kv_sent, sems, 4),
    ]
    for copy in copies:
        copy.start()
    total[...] += (
        plain_product(grad_q[...], wq[...])
        + plain_product(grad_k[...], wk[...])
        + plain_product(grad_v[...], wv[...])
    )
    for copy in copies:
        copy.wait()


def by_core(rows_per_device, part):
    pairs = part.reshape(-1, 2, rows_per_device, part.shape[-1])
    here = lax.axis_index("dp") % 2 == 0
    first, second = pairs[:, 0], pairs[:, 1]
    return jnp.where(here, first, second), jnp.where(here, second, first)


def heads(rows, width, first=0):
    return pl.BlockSpec((rows, width), lambda k: (0, first + k))


def head_rows(heads_in, depth, first):
    return pl.BlockSpec((heads_in * HEAD_WIDTH, depth), lambda k: (first + k, 0))


def qkv_rows_of(depth, first):
    return [
        head_rows(GROUP, depth, first),
        head_rows(1, depth, QUERY_HEADS + first),
        head_rows(1, depth, QUERY_HEADS + KEY_VALUE_HEADS + first),
    ]


def attention(normed, qkv_full, tables, gain_q, gain_k, context, first, count):
    tokens, depth = normed.shape
    wide = GROUP * HEAD_WIDTH
    whole_context = shape_of((tokens, QUERY_HEADS * HEAD_WIDTH), jnp.bfloat16)
    held = [] if context is None else [context]
    return kernel_call(
        attention_kernel,
        "attention",
        (count,),
        [
            in_vmem(normed),
            *qkv_rows_of(depth, first),
            *[in_vmem(table) for table in tables],
            in_vmem(gain_q),
            in_vmem(gain_k),
            *[pl.BlockSpec(memory_space=pl.ANY)] * len(held),
        ],
        (
            shape_of((tokens, count * TRIO), jnp.float32),
            shape_of((tokens, count * TRIO), jnp.float32),
            shape_of((tokens, count * TRIO), jnp.bfloat16),
            shape_of((tokens, count * HEAD_WIDTH), jnp.bfloat16),
            whole_context,
        ),
        (
            heads(tokens, TRIO),
            heads(tokens, TRIO),
            heads(tokens, TRIO),
            heads(tokens, HEAD_WIDTH),
            heads(tokens, wide, first),
        ),
        aliases={9: 4} if held else None,
        vmem=VMEM_LESS,
    )(normed, qkv_full, qkv_full, qkv_full, *tables, gain_q, gain_k, *held)


def attention_backward(
    norms, scales, turns, value, grad_context, tables, gain_q, gain_k,
    normed, qkv_full, total, parts, first, rows_per_device,
):
    tokens, depth = normed.shape
    wide = GROUP * HEAD_WIDTH
    count = value.shape[1] // HEAD_WIDTH
    half = KEY_VALUE_HEADS // 2
    stretch = half * wide // (2 * rows_per_device)
    early = shape_of((1, stretch, rows_per_device, depth), jnp.bfloat16)
    late = shape_of((3, stretch, rows_per_device, depth), jnp.bfloat16)
    shapes = [late, late] if first >= half else [early, early, late, late]
    held = [] if total is None else [total, *parts]

    def part_scratch(rows):
        chips = max(rows // (2 * rows_per_device), 1)
        height = min(rows, rows_per_device)
        return pltpu.VMEM((2, chips, height, depth), jnp.bfloat16)

    anywhere = pl.BlockSpec(memory_space=pl.ANY)
    return kernel_call(
        functools.partial(attention_backward_kernel, first, rows_per_device, len(held)),
        "attention_backward",
        (count,),
        [
            heads(tokens, TRIO),
            heads(tokens, TRIO),
            heads(tokens, TRIO),
            heads(tokens, HEAD_WIDTH),
            heads(tokens, wide, first),
            *[in_vmem(table) for table in tables],
            in_vmem(gain_q),
            in_vmem(gain_k),
            in_vmem(normed),
            *qkv_rows_of(depth, first),
            *[in_vmem(total)] * min(len(held), 1),
            *[anywhere] * max(len(held) - 1, 0),
        ],
        (
            *shapes,
            shape_of((tokens, depth), jnp.float32),
            shape_of(gain_q.shape, jnp.float32),
            shape_of(gain_k.shape, jnp.float32),
        ),
        (*[anywhere] * len(shapes), in_vmem(normed), in_vmem(gain_q), in_vmem(gain_k)),
        scratch=[
            pltpu.VMEM((tokens, wide), jnp.bfloat16),
            pltpu.VMEM((tokens, HEAD_WIDTH), jnp.bfloat16),
            pltpu.VMEM((tokens, HEAD_WIDTH), jnp.bfloat16),
            part_scratch(wide),
            part_scratch(HEAD_WIDTH),
            part_scratch(HEAD_WIDTH),
            pltpu.SemaphoreType.DMA((6,)),
        ],
        aliases={15 + slot: slot for slot in range(len(shapes))} if held else None,
        vmem=VMEM_LESS,
    )(
        norms, scales, turns, value, grad_context, *tables, gain_q, gain_k,
        normed, qkv_full, qkv_full, qkv_full, *held,
    )


ROW_TILE = 256
FF_TILE = 512
BACK_TILE = 384
STRIP = 64


def project_kernel(context, weight, residual, gain, middle, normed):
    middle[...] = residual[...] + contract_last(context[...], weight[...])

    @pl.loop(0, middle.shape[0] // STRIP)
    def _(strip):
        rows = pl.ds(pl.multiple_of(strip * STRIP, STRIP), STRIP)
        values = middle[rows, :]
        normed[rows, :] = (values * rms_scale(values) * gain[...]).astype(jnp.bfloat16)


def rows_of(array, tile):
    return pl.BlockSpec((tile, array.shape[1]), lambda k: (k, 0))


def project(context, weight, residual, gain):
    return kernel_call(
        project_kernel,
        "project",
        (residual.shape[0] // ROW_TILE,),
        [rows_of(context, ROW_TILE), whole(weight), rows_of(residual, ROW_TILE), whole(gain)],
        (shape_of(residual.shape, jnp.float32), shape_of(residual.shape, jnp.bfloat16)),
        (rows_of(residual, ROW_TILE), rows_of(residual, ROW_TILE)),
    )(context, weight, residual, gain)


def feed_kernel(normed, gate_weight, up_weight, hidden, slope, lift):
    gate = contract_last(normed[...], gate_weight[...])
    upward = contract_last(normed[...], up_weight[...])
    sigma = jax.nn.sigmoid(gate)
    lifted = gate * sigma
    lift[...] = lifted
    slope[...] = upward * sigma * (1.0 + gate * (1.0 - sigma))
    hidden[...] = (lifted * upward).astype(jnp.bfloat16)


def columns_of(rows, tile, first=0):
    return pl.BlockSpec((rows, tile), lambda k: (0, first + k))


def tile_rows(tile, depth, first):
    return pl.BlockSpec((tile, depth), lambda k: (first + k, 0))


def feed(normed, weight):
    tokens, depth = normed.shape
    columns = columns_of(tokens, FF_TILE)
    tiles = FF // FF_TILE
    return kernel_call(
        feed_kernel,
        "feed",
        (tiles,),
        [whole(normed), tile_rows(FF_TILE, depth, 0), tile_rows(FF_TILE, depth, tiles)],
        (
            shape_of((tokens, FF), jnp.bfloat16),
            shape_of((tokens, FF), jnp.float32),
            shape_of((tokens, FF), jnp.float32),
        ),
        (columns, columns, columns),
    )(normed, weight, weight)


def finish_kernel(hidden, weight, residual, output):
    output[...] = residual[...] + contract_last(hidden[...], weight[...])


def finish(hidden, weight, residual):
    return kernel_call(
        finish_kernel,
        "finish",
        (residual.shape[0] // ROW_TILE,),
        [rows_of(hidden, ROW_TILE), whole(weight), rows_of(residual, ROW_TILE)],
        shape_of(residual.shape, jnp.float32),
        rows_of(residual, ROW_TILE),
    )(hidden, weight, residual)


def outer_kernel(rows_per_device, left, right, kept, sent, turned_left):
    @pl.when(pl.program_id(0) == 0)
    def _():
        turned_left[...] = left[...].T

    part = plain_product(turned_left[...], right[...]).astype(jnp.bfloat16)
    kept[...], sent[...] = by_core(rows_per_device, part)


def chip_columns(chips, rows, width):
    return pl.BlockSpec((chips, rows, width), lambda k: (0, 0, k))


def outer(left, right, rows_per_device):
    chips = left.shape[1] // (2 * rows_per_device)
    shape = shape_of((chips, rows_per_device, right.shape[1]), jnp.bfloat16)
    block = chip_columns(chips, rows_per_device, FF_TILE)
    return kernel_call(
        functools.partial(outer_kernel, rows_per_device),
        "outer",
        (right.shape[1] // FF_TILE,),
        [whole(left), columns_of(right.shape[0], FF_TILE)],
        (shape, shape),
        (block, block),
        scratch=[pltpu.VMEM((left.shape[1], left.shape[0]), jnp.bfloat16)],
    )(left, right)


def feed_backward_kernel(
    rows_per_device, grad_feed, down, slope, lift, normed, gate_weight, up_weight, *others
):
    kept, sent, total = others[-3:]

    @pl.when(pl.program_id(0) == 0)
    def _():
        total[...] = others[0][...] if len(others) > 3 else jnp.zeros_like(total)

    grad_hidden = plain_product(grad_feed[...], down[...])
    grad_gate = (grad_hidden * slope[...]).astype(jnp.bfloat16)
    grad_up = (grad_hidden * lift[...]).astype(jnp.bfloat16)
    for plane, grad in enumerate((grad_gate, grad_up)):
        part = contract_first(grad, normed[...]).astype(jnp.bfloat16)
        kept[plane], sent[plane] = by_core(rows_per_device, part)
    total[...] += plain_product(grad_gate, gate_weight[...]) + plain_product(
        grad_up, up_weight[...]
    )


def feed_backward(grad_feed, down, slope, lift, normed, weight, total, half, rows_per_device):
    tokens, depth = normed.shape
    tiles = FF // BACK_TILE
    count = tiles // 2
    first = half * count
    held = [] if total is None else [total]
    chips = BACK_TILE // (2 * rows_per_device)
    shape = shape_of((2, count * chips, rows_per_device, depth), jnp.bfloat16)
    block = pl.BlockSpec((2, chips, rows_per_device, depth), lambda k: (0, k, 0, 0))
    return kernel_call(
        functools.partial(feed_backward_kernel, rows_per_device),
        "feed_backward",
        (count,),
        [
            whole(grad_feed),
            columns_of(depth, BACK_TILE, first),
            columns_of(tokens, BACK_TILE, first),
            columns_of(tokens, BACK_TILE, first),
            whole(normed),
            tile_rows(BACK_TILE, depth, first),
            tile_rows(BACK_TILE, depth, tiles + first),
            *[whole(total) for total in held],
        ],
        (shape, shape, shape_of((tokens, depth), jnp.float32)),
        (block, block, pl.BlockSpec((tokens, depth), lambda k: (0, 0))),
    )(grad_feed, down, slope, lift, normed, weight, weight, *held)


def project_backward_kernel(
    rows_per_device, grad_normed, middle, out_grad, gain, context, weight,
    kept, sent, grad_context, grad_middle, gain_terms, branch, turned_branch,
):
    @pl.when(pl.program_id(0) == 0)
    def _():
        gain_terms[...] = jnp.zeros_like(gain_terms)

        @pl.loop(0, middle.shape[0] // STRIP)
        def _(strip):
            rows = pl.ds(pl.multiple_of(strip * STRIP, STRIP), STRIP)
            values = middle[rows, :]
            grad, terms = norm_backward(
                values, rms_scale(values), gain[...], grad_normed[rows, :]
            )
            grad = out_grad[rows, :] + grad
            grad_middle[rows, :] = grad
            branch[rows, :] = grad.astype(jnp.bfloat16)
            gain_terms[...] += jnp.sum(terms, axis=0, keepdims=True)

        turned_branch[...] = branch[...].T

    part = plain_product(turned_branch[...], context[...]).astype(jnp.bfloat16)
    kept[...], sent[...] = by_core(rows_per_device, part)
    grad_context[...] = plain_product(branch[...], weight[...]).astype(jnp.bfloat16)


def project_backward(grad_normed, middle, out_grad, gain, context, weight, rows_per_device):
    tokens, depth = middle.shape
    width = context.shape[1]
    chips = depth // (2 * rows_per_device)
    shape = shape_of((chips, rows_per_device, width), jnp.bfloat16)
    block = chip_columns(chips, rows_per_device, FF_TILE)
    return kernel_call(
        functools.partial(project_backward_kernel, rows_per_device),
        "project_backward",
        (width // FF_TILE,),
        [
            whole(grad_normed),
            whole(middle),
            whole(out_grad),
            whole(gain),
            columns_of(tokens, FF_TILE),
            columns_of(depth, FF_TILE),
        ],
        (
            shape,
            shape,
            shape_of((tokens, width), jnp.bfloat16),
            shape_of((tokens, depth), jnp.float32),
            shape_of(gain.shape, jnp.float32),
        ),
        (block, block, columns_of(tokens, FF_TILE), whole(middle), whole(gain)),
        scratch=[
            pltpu.VMEM((tokens, depth), jnp.bfloat16),
            pltpu.VMEM((depth, tokens), jnp.bfloat16),
        ],
    )(grad_normed, middle, out_grad, gain, context, weight)


def position_tables(segment_ids):
    _, micro_rows = segment_ids.shape
    order = jnp.arange(micro_rows, dtype=jnp.int32)
    same = segment_ids[:, :, None] == segment_ids[:, None, :]
    earlier = order[None, :] < order[:, None]
    positions = jnp.sum(jnp.where(same & earlier[None], 1, 0), axis=2).astype(jnp.int32)
    half_size = HEAD_WIDTH // 2
    frequency = ROPE_BASE ** (-(jnp.arange(half_size, dtype=jnp.float32) * (2.0 / HEAD_WIDTH)))
    angles = positions.reshape(-1, 1).astype(jnp.float32) * frequency[None, :]
    cosine, sine = jnp.cos(angles), jnp.sin(angles)
    allowed = same & (earlier | (order[None, :] == order[:, None]))[None]
    return (
        jnp.concatenate([cosine, cosine], axis=-1),
        jnp.concatenate([-sine, sine], axis=-1),
        jnp.where(allowed, 0.0, -1e30).astype(jnp.float32),
    )


def adamw(weight, first, second, grad, rate, decay):
    first_new = BETA_ONE * first + (1.0 - BETA_ONE) * grad
    second_new = BETA_TWO * second + (1.0 - BETA_TWO) * grad * grad
    corrected = (
        first_new
        / (1.0 - BETA_ONE**STEP)
        / (jnp.sqrt(second_new / (1.0 - BETA_TWO**STEP)) + ADAM_EPS)
    )
    return (weight - rate * (corrected + decay * weight), first_new, second_new)


def per_device(
    grid,
    activations,
    segment_ids,
    out_grad,
    qkv_weight,
    qkv_first,
    qkv_second,
    out_weight,
    out_first,
    out_second,
    gate_up_weight,
    gate_up_first,
    gate_up_second,
    down_weight,
    down_first,
    down_second,
    norm_gains,
    gains_first,
    gains_second,
):
    qkv_low = qkv_weight.astype(jnp.bfloat16)
    out_low = out_weight.astype(jnp.bfloat16)
    gate_up_low = gate_up_weight.astype(jnp.bfloat16)
    down_low = down_weight.astype(jnp.bfloat16)

    own_gains = lax.reduce_precision(norm_gains, exponent_bits=8, mantissa_bits=7)
    gain_count = own_gains.shape[0]
    gain_start = lax.axis_index("dp") * gain_count
    all_gains = jnp.zeros((1, gain_count * grid.count), jnp.float32)
    all_gains = lax.dynamic_update_slice(all_gains, own_gains[None], (0, gain_start))
    size = grid.size
    heads_of = KEY_VALUE_HEADS // 4
    out_rows, gate_rows = out_low.shape[0], gate_up_low.shape[0]
    qkv_rows, down_rows = qkv_low.shape[0], down_low.shape[0]

    tables = position_tables(segment_ids)
    scale_one = rms_scale(activations)
    v = Steps(out_low=out_low, gate_up_low=gate_up_low, gains=all_gains)
    v.qkv_line = z_pieces(grid, qkv_low, False)
    down_sides = plane_sides(grid, down_low)
    down_corners = plane_corners(grid, down_sides, v.qkv_line[1])
    v.down_chip, down_places = chip_plane(down_low, down_sides, down_corners)
    v.gains = small_sum(grid, v.gains, "c")
    v.close()

    v.qkv_column = jnp.stack(v.qkv_line)
    v.qkv_sides = plane_sides(grid, v.qkv_column)
    out_line = z_pieces(grid, v.out_low, False)
    v.out_column = jnp.stack(out_line)
    v.gains = small_sum(grid, after(v.gains, *out_line), "z")
    v.grad_feed = out_grad.astype(jnp.bfloat16)
    v.drop("qkv_line", "out_low")
    v.close()

    v.qkv_corners = plane_corners(grid, v.qkv_sides)
    v.gate_up_moved = {hops: grid.shift(v.gate_up_low, "z", hops) for hops in (1, 3)}
    v.qkv_column_swapped = grid.shift(v.qkv_column, "c", 1)
    v.gains = small_sum(grid, after(v.gains, v.qkv_corners), "x")
    v.close()

    v.out_sides = plane_sides(grid, v.out_column)
    half = gate_rows // 2
    first_half = grid.shift(v.gate_up_low[:half], "z", 2)
    second_half = grid.shift(after(v.gate_up_low[half:], first_half), "z", 2)
    v.gate_up_moved[2] = jnp.concatenate([first_half, second_half], axis=0)
    v.qkv_sides_swapped = swap_tree(grid, v.qkv_sides)
    v.qkv_corners_swapped = swap_tree(grid, after_tree(v.qkv_corners, v.qkv_sides_swapped))
    v.out_corners = plane_corners(grid, v.out_sides)
    v.gains = small_sum(grid, after(v.gains, v.out_corners), "y")
    v.out_column_swapped = grid.shift(after(v.out_column, v.qkv_corners_swapped), "c", 1)
    v.close()

    gain_one, gain_two = v.gains[:, :D], v.gains[:, D : 2 * D]
    gain_query = v.gains[:, 2 * D : 2 * D + HEAD_WIDTH]
    gain_key = v.gains[:, 2 * D + HEAD_WIDTH :]
    normed_one = (activations * scale_one * gain_one).astype(jnp.bfloat16)
    every = tuple(range(size["z"]))
    middle_plane = size["z"] // 2
    gate_up_line = [v.gate_up_low, *[v.gate_up_moved[hops] for hops in grid.hops("z")]]
    v.near_column = jnp.stack(gate_up_line[:middle_plane])
    v.far_column = jnp.stack(gate_up_line[middle_plane:])
    v.near_sides = plane_sides(grid, v.near_column)
    v.down_moved = {1: grid.shift(v.down_chip, "z", 1)}
    v.out_sides_swapped = swap_tree(grid, v.out_sides)
    qkv_full = assemble(
        grid,
        plane_pieces(every, v.qkv_column, v.qkv_sides, v.qkv_corners),
        plane_pieces(every, v.qkv_column_swapped, v.qkv_sides_swapped, v.qkv_corners_swapped),
    )
    grad_feed = v.grad_feed
    v.drop("qkv_column", "qkv_sides", "qkv_corners", "gate_up_low", "gate_up_moved", "gains")
    v.drop("grad_feed")
    v.drop("qkv_column_swapped", "qkv_sides_swapped", "qkv_corners_swapped")
    parts = []

    def attention_part(part, context):
        *kept, context = attention(
            after(normed_one, *flat(context)),
            qkv_full,
            tables,
            gain_query,
            gain_key,
            context,
            part * heads_of,
            heads_of,
        )
        parts.append(kept)
        return context

    v.context = attention_part(0, None)
    v.close()

    v.far_sides = plane_sides(grid, v.far_column)
    v.down_moved[3] = grid.shift(v.down_chip, "z", 3)
    v.out_corners_swapped = swap_tree(grid, v.out_corners)
    context = attention_part(1, v.context)
    v.near_column_swapped = grid.shift(
        after(v.near_column, context, v.out_corners_swapped), "c", 1
    )
    v.far_column_swapped = grid.shift(after(v.far_column, context, v.out_corners_swapped), "c", 1)
    v.context = attention_part(2, context)
    v.close()

    v.gate_up_corners = plane_corners(grid, (v.near_sides[0], v.far_sides[1]), halved=False)
    low, high = (0, down_rows // 2), (down_rows // 2, down_rows)
    v.down_moved[2] = [grid.shift(v.down_chip[:, : low[1]], "z", 2)]
    v.near_sides_swapped = swap_tree(grid, v.near_sides)
    context = attention_part(3, v.context)
    v.far_sides_swapped = swap_tree(
        grid, after_tree(v.far_sides, context, v.near_sides_swapped)
    )
    out_full = assemble(
        grid,
        plane_pieces(every, v.out_column, v.out_sides, v.out_corners),
        plane_pieces(every, v.out_column_swapped, v.out_sides_swapped, v.out_corners_swapped),
    )
    middle, v.normed_two = project(context, out_full, activations, gain_two)
    v.drop("out_column", "out_sides", "out_corners", "context")
    v.drop("out_column_swapped", "out_sides_swapped", "out_corners_swapped")
    v.close()

    normed_two = v.normed_two
    v.down_moved[2] = v.down_moved[2] + [grid.shift(v.down_chip[:, high[0] :], "z", 2)]
    corners_swapped = swap_tree(grid, v.gate_up_corners)
    near, far = every[:middle_plane], every[middle_plane:]
    gate_up_full = assemble(
        grid,
        plane_pieces(near, v.near_column, v.near_sides, {})
        + plane_pieces(far, v.far_column, v.far_sides, {})
        + corner_pieces(every, v.gate_up_corners),
        plane_pieces(near, v.near_column_swapped, v.near_sides_swapped, {})
        + plane_pieces(far, v.far_column_swapped, v.far_sides_swapped, {})
        + corner_pieces(every, corners_swapped),
    )
    v.hidden, v.slope, v.lift = feed(normed_two, gate_up_full)
    v.drop("near_column", "far_column", "near_sides", "far_sides", "gate_up_corners", "normed_two")
    v.drop("near_column_swapped", "far_column_swapped", "near_sides_swapped", "far_sides_swapped")
    v.close()

    hidden, slope, lift = v.hidden, v.slope, v.lift
    v.down_line = [v.down_chip, v.down_moved[1], v.down_moved[3], *v.down_moved[2]]
    v.down_swapped = swap_tree(grid, v.down_line)
    v.down_parts = outer(grad_feed, hidden, down_rows)
    v.drop("down_chip", "down_moved", "hidden", "slope", "lift")
    v.close()

    places = {
        (axis, hops): grid.ahead(axis, hops) for axis in "zyx" for hops in range(size[axis])
    }

    def here(axis, hops):
        return places[axis, hops]

    def in_planes(pair):
        return [
            part.reshape(-1, size["y"], size["x"], *part.shape[-2:]) for part in pair
        ]

    v.down_terms = swapped(grid, in_planes(v.down_parts))
    down_full = assemble(
        grid, down_pieces(v.down_line, down_places), down_pieces(v.down_swapped, down_places)
    )

    def feed_part(half, total):
        *pair, total = feed_backward(
            grad_feed, down_full, slope, lift, normed_two, gate_up_full, total, half, gate_rows
        )
        return pair, total

    v.even_parts, v.total = feed_part(0, None)
    v.drop("down_line", "down_swapped", "down_parts")
    v.close()

    merge = Merge(grid)
    down_one = line(merge, here, [(v.down_terms, every)], 1, lead=2)
    made = merge.run()
    v.down_moved = [Source(down_one(made))]
    v.even = swapped(grid, in_planes(v.even_parts))
    v.odd_parts, v.total = feed_part(1, v.total)
    v.drop("even_parts")
    v.close()

    merge = Merge(grid)
    even_corners = corners(merge, here, v.even)
    down_three = line(merge, here, [(v.down_terms, every)], 3, lead=2)
    made = merge.run()
    v.even_corners = even_corners(made)
    v.down_moved.append(Source(down_three(made)))
    v.odd = swapped(grid, in_planes(v.odd_parts))
    *v.out_parts, v.grad_context, v.grad_middle, v.gain_two_part = project_backward(
        v.total, middle, out_grad, gain_two, context, out_full, out_rows
    )
    v.drop("odd_parts", "total")
    v.close()

    grad_context, grad_middle, gain_two_part = v.grad_context, v.grad_middle, v.gain_two_part
    v.drop("grad_context", "grad_middle", "gain_two_part")
    merge = Merge(grid)
    even_sides = sides(merge, here, v.even, v.even_corners)
    down_two = line(merge, here, [(v.down_terms, every)], 2, rows=low, lead=2)
    made = merge.run()
    v.even = even_sides(made)
    v.down_moved.append(Source(down_two(made)))
    v.out_terms = swapped(grid, in_planes(v.out_parts))
    v.gain_terms = []

    def backward_part(part, rows, total):
        *v.rows, v.total, terms_q, terms_k = attention_backward(
            *parts[part],
            grad_context,
            tables,
            gain_query,
            gain_key,
            normed_one,
            qkv_full,
            total,
            rows,
            part * heads_of,
            qkv_rows,
        )
        v.gain_terms = v.gain_terms + [(terms_q, terms_k)]

    backward_part(0, [], None)
    v.drop("out_parts", "even_corners")
    v.close()

    merge = Merge(grid)
    odd_corners = corners(merge, here, v.odd)
    out_corners = corners(merge, here, v.out_terms)
    down_two = line(merge, here, [(v.down_terms, every)], 2, rows=high, lead=2)
    down_own = line(merge, here, [(v.down_terms, every)], 0, lead=2)
    made = merge.run()
    v.odd_corners = odd_corners(made)
    v.out_corners = out_corners(made)
    v.down_moved += [Source(down_two(made), high[0]), Source(down_own(made))]
    backward_part(1, v.rows, v.total)
    v.drop("down_terms")
    v.close()

    merge = Merge(grid)
    odd_sides = sides(merge, here, v.odd, v.odd_corners)
    down_corners = corners(merge, here, v.down_moved, lead=0)
    made = merge.run()
    v.odd = odd_sides(made)
    v.down_corners = down_corners(made)
    v.first = swapped(grid, in_planes(v.rows[:2]))
    backward_part(2, v.rows[2:], v.total)
    v.drop("odd_corners")
    v.close()

    gate_up_groups = [(v.even, (0, 2)), (v.odd, (1, 3))]
    merge = Merge(grid)
    out_sides = sides(merge, here, v.out_terms, v.out_corners)
    first_corners = corners(merge, here, v.first)
    gate_up_one = line(merge, here, gate_up_groups, 1)
    made = merge.run()
    v.out_terms = out_sides(made)
    v.first_corners = first_corners(made)
    v.gate_up_moved = [gate_up_one(made)]
    backward_part(3, v.rows, v.total)
    v.drop("out_corners")
    v.close()

    gate_up_groups = [(v.even, (0, 2)), (v.odd, (1, 3))]
    v.last = swapped(grid, in_planes(v.rows))
    merge = Merge(grid)
    first_sides = sides(merge, here, v.first, v.first_corners)
    gate_up_two = line(merge, here, gate_up_groups, 2)
    gate_up_own = line(merge, here, gate_up_groups, 0)
    made = merge.run()
    v.first = first_sides(made)
    v.gate_up_moved += [gate_up_two(made), gate_up_own(made)]
    grad_block, gain_one_terms = norm_backward(activations, scale_one, gain_one, v.total)
    v.input_grad = grad_middle + grad_block
    v.gains_part = jnp.concatenate(
        [
            jnp.sum(gain_one_terms, axis=0, keepdims=True),
            gain_two_part,
            sum(terms for terms, _ in v.gain_terms),
            sum(terms for _, terms in v.gain_terms),
        ],
        axis=1,
    )
    v.drop("rows", "total", "gain_terms", "first_corners")
    v.close()

    gate_up_groups = [(v.even, (0, 2)), (v.odd, (1, 3))]
    merge = Merge(grid)
    last_corners = corners(merge, here, v.last)
    down_sides = sides(merge, here, v.down_moved, v.down_corners, lead=0)
    gate_up_three = line(merge, here, gate_up_groups, 3)
    made = merge.run()
    v.last_corners = last_corners(made)
    v.down_terms = down_sides(made)
    v.gate_up_moved.append(gate_up_three(made))
    v.gains_part = small_sum(grid, v.gains_part, "c")
    v.layer_output = finish(hidden, down_full, middle)
    v.drop("down_corners", "down_moved", "even", "odd")
    v.close()

    merge = Merge(grid)
    last_sides = sides(merge, here, v.last, v.last_corners)
    out_lines = [line(merge, here, [(v.out_terms, every)], hops) for hops in range(size["z"])]
    made = merge.run()
    v.last = last_sides(made)
    v.out_moved = [go(made) for go in out_lines]
    v.gains_part = small_sum(grid, after(v.gains_part, v.out_moved), "xy")
    v.gate_up_new = adamw(
        gate_up_weight, gate_up_first, gate_up_second, total_of(*v.gate_up_moved), 0.06, 0.1
    )
    down_total = total_of(*[term.array for term in v.down_terms])
    v.down_new = adamw(down_weight, down_first, down_second, down_total, 0.04, 0.1)
    v.drop("last_corners", "gate_up_moved", "down_terms", "out_terms")
    v.close()

    qkv_groups = [(v.first, (0,)), (v.last, (1, 2, 3))]
    merge = Merge(grid)
    qkv_lines = [line(merge, here, qkv_groups, hops) for hops in range(size["z"])]
    made = merge.run()
    qkv_total = total_of(*[go(made) for go in qkv_lines])
    gains_total = small_sum(grid, v.gains_part, "z")
    out_new = adamw(out_weight, out_first, out_second, total_of(*v.out_moved), 0.25, 0.1)
    gains_total = lax.dynamic_slice(gains_total, (0, gain_start), (1, gain_count))[0]

    return (
        v.layer_output,
        v.input_grad,
        *adamw(qkv_weight, qkv_first, qkv_second, qkv_total, 0.06, 0.1),
        *out_new,
        *v.gate_up_new,
        *v.down_new,
        *adamw(norm_gains, gains_first, gains_second, gains_total, 0.3, 0.0),
    )


def solution(mesh):
    return jax.shard_map(
        functools.partial(per_device, Grid(mesh.shape["dp"])),
        mesh=mesh,
        in_specs=(
            P("dp", None),
            P("dp", None),
            P("dp", None),
            P("dp", None),
            P("dp", None),
            P("dp", None),
            P("dp", None),
            P("dp", None),
            P("dp", None),
            P("dp", None),
            P("dp", None),
            P("dp", None),
            P("dp", None),
            P("dp", None),
            P("dp", None),
            P("dp"),
            P("dp"),
            P("dp"),
        ),
        out_specs=(
            P("dp", None),
            P("dp", None),
            P("dp", None),
            P("dp", None),
            P("dp", None),
            P("dp", None),
            P("dp", None),
            P("dp", None),
            P("dp", None),
            P("dp", None),
            P("dp", None),
            P("dp", None),
            P("dp", None),
            P("dp", None),
            P("dp"),
            P("dp"),
            P("dp"),
        ),
        check_vma=False,
    )
```

```python
import functools
import itertools
import math

import jax
import jax.numpy as jnp
from jax import lax
from jax.experimental import pallas as pl
from jax.experimental.pallas import tpu as pltpu
from jax.sharding import PartitionSpec as P

D = 1024
QUERY_HEADS = 16
KEY_VALUE_HEADS = 8
HEAD_WIDTH = 128
FF = 3072
STEP = 10


NORM_EPS = 1e-06
ROPE_BASE = 1000000.0
BETA_ONE = 0.9
BETA_TWO = 0.95
ADAM_EPS = 1e-08


def contract_last(left_side, right_side):
    return lax.dot_general(
        left_side, right_side, (((1,), (1,)), ((), ())), preferred_element_type=jnp.float32
    )


def contract_first(left_side, right_side):
    return lax.dot_general(
        left_side, right_side, (((0,), (0,)), ((), ())), preferred_element_type=jnp.float32
    )


def plain_product(left_side, right_side):
    return jnp.dot(left_side, right_side, preferred_element_type=jnp.float32)


def rms_scale(values):
    return lax.rsqrt(jnp.mean(values * values, axis=-1, keepdims=True) + NORM_EPS)


class Grid:
    def __init__(self, count):
        chips = count // 2
        flat = 2 if chips <= 16 else 4
        self.size = {"z": chips // (flat * flat), "y": flat, "x": flat, "c": 2}
        self.step = {"z": 2 * flat * flat, "y": 2 * flat, "x": 2, "c": 1}
        self.count = count

    def at(self, axis):
        return (lax.axis_index("dp") // self.step[axis]) % self.size[axis]

    def ahead(self, axis, hops):
        return (self.at(axis) + hops) % self.size[axis]

    def hops(self, axis):
        return range(1, self.size[axis])

    def shift(self, value, axis, hops):
        size, step = self.size[axis], self.step[axis]
        pairs = []
        for device in range(self.count):
            here = (device // step) % size
            pairs.append((device, device + ((here + hops) % size - here) * step))
        return lax.ppermute(value, "dp", pairs)


def after(value, *others):
    return lax.optimization_barrier((value, *jax.tree.leaves(others)))[0]


GROUP = QUERY_HEADS // KEY_VALUE_HEADS
SCORE_SCALE = HEAD_WIDTH ** (-0.5)
EXP2_SCALE = SCORE_SCALE * math.log2(math.e)
VMEM_BYTES = 60 * 1024 * 1024
VMEM_LESS = 50 * 1024 * 1024


def norm_backward(values, scale_rows, gain, grad_out):
    scaled = gain * grad_out
    grad_in = scale_rows * scaled - values * scale_rows**3 * jnp.mean(
        scaled * values, axis=-1, keepdims=True
    )
    return (grad_in, grad_out * values * scale_rows)


def z_pieces(grid, shard, chained, *dependencies):
    moved = [shard]
    for hops in grid.hops("z"):
        moved.append(grid.shift(after(shard, *dependencies) if dependencies else shard, "z", hops))
        if chained:
            dependencies = (moved[-1],)
    return moved


def swap_tree(grid, buffers):
    return jax.tree.map(lambda buffer: grid.shift(buffer, "c", 1), buffers)


def swap_together(grid, buffers):
    leaves, shape = jax.tree.flatten(buffers)
    moved = grid.shift(jnp.concatenate(leaves, axis=0), "c", 1)
    starts = itertools.accumulate([0] + [leaf.shape[0] for leaf in leaves])
    return jax.tree.unflatten(
        shape, [Part(moved, start, leaf.shape[0]) for start, leaf in zip(starts, leaves)]
    )


@jax.tree_util.register_pytree_node_class
class Part:
    def __init__(self, array, start, count):
        self.array, self.start, self.count = array, start, count

    def tree_flatten(self):
        return (self.array,), (self.start, self.count)

    @classmethod
    def tree_unflatten(cls, held, leaves):
        return cls(*leaves, *held)


def plane_sides(grid, column, *dependencies):
    sent = after(column, *dependencies) if dependencies else column
    from_x = {hops: grid.shift(sent, "x", hops) for hops in grid.hops("x")}
    from_y = {hops: grid.shift(sent, "y", hops) for hops in grid.hops("y")}
    return from_x, from_y


def plane_corners(grid, sides, *dependencies, halved=True, cut_at=None):
    from_x, from_y = sides
    half = from_x[1].shape[0] // 2 if cut_at is None else cut_at
    corners = {}
    for j in from_x:
        for l in from_y:
            first, second = from_x[j], from_y[l]
            if halved:
                first, second = first[:half], second[half:]
            if dependencies:
                first, second = after(first, *dependencies), after(second, *dependencies)
            corners[j, l] = (grid.shift(first, "y", l), grid.shift(second, "x", j))
    return corners


def corner_pieces(planes, corners):
    half = len(planes) // 2
    pieces = []
    for (j, l), (first, second) in corners.items():
        pieces.append((first, [{"z": hops, "x": j, "y": l} for hops in planes[:half]]))
        pieces.append((second, [{"z": hops, "x": j, "y": l} for hops in planes[half:]]))
    return pieces


def plane_pieces(planes, column, sides, corners):
    from_x, from_y = sides
    pieces = [(column, [{"z": hops} for hops in planes])]
    pieces += [(from_x[j], [{"z": hops, "x": j} for hops in planes]) for j in from_x]
    pieces += [(from_y[l], [{"z": hops, "y": l} for hops in planes]) for l in from_y]
    return pieces + corner_pieces(planes, corners)


def after_tree(tree, *dependencies):
    leaves, shape = jax.tree.flatten(tree)
    tied = lax.optimization_barrier((*leaves, *flat(dependencies)))
    return jax.tree.unflatten(shape, tied[: len(leaves)])


def flat(*groups):
    return [leaf for leaf in jax.tree.leaves(groups)]


def rows_of_gains(gains, width):
    rows = -(-gains.shape[1] // width)
    block = jnp.pad(gains, ((0, 0), (0, rows * width - gains.shape[1]))).reshape(rows, width)
    return jnp.pad(block, ((0, 16 - rows), (0, 0)))


def chip_plane(block, sides_received, corners_received, rows):
    from_x, from_y = sides_received
    blocks = [block, *from_x.values(), *from_y.values()]
    shards = [part[:rows] for part in blocks]
    below = [part[rows:] for part in blocks]
    places = [{}] + [{"x": j} for j in from_x] + [{"y": l} for l in from_y]
    for (j, l), (shard, rest) in corners_received.items():
        shards.append(shard)
        below.append(rest)
        places.append({"x": j, "y": l})
    return jnp.stack(shards), sum(below), places


def assemble_kernel(grid, places_of, *refs):
    pieces, (out, held, came, went) = refs[:-4], refs[-4:]
    moves = []
    for which, first, places in places_of:
        piece = pieces[which]
        for slot, place in enumerate(places, first):
            index = 0
            for axis in ("z", "y", "x", "c"):
                size = grid.size[axis]
                index = index + (grid.at(axis) + size - place.get(axis, 0)) % size * grid.step[axis]
            number = len(moves)
            moves.append(
                (
                    pltpu.make_async_copy(piece.at[slot], held.at[index], came.at[number]),
                    pltpu.make_async_copy(held.at[index], out.at[index], went.at[number]),
                )
            )
    for arrive, _ in moves:
        arrive.start()
    for arrive, leave in moves:
        arrive.wait()
        leave.start()
    for _, leave in moves:
        leave.wait()


def line_pieces(line, places):
    return [
        (buffer, [dict(place, z=hops) for place in places]) for hops, buffer in enumerate(line)
    ]


def assemble(grid, own_pieces, swapped_pieces):
    pieces = own_pieces + [
        (buffer, [dict(place, c=1) for place in places]) for buffer, places in swapped_pieces
    ]
    arrays, places_of = [], []
    for buffer, places in pieces:
        array, first = (buffer.array, buffer.start) if isinstance(buffer, Part) else (buffer, 0)
        which = next((at for at, known in enumerate(arrays) if known is array), len(arrays))
        if which == len(arrays):
            arrays.append(array)
        places_of.append((which, first, places))
    rows, width = arrays[0].shape[1:]
    dims = (grid.count, rows, width)
    moves = sum(len(places) for _, places in pieces)
    gathered = pl.pallas_call(
        functools.partial(assemble_kernel, grid, places_of),
        out_shape=jax.ShapeDtypeStruct(dims, jnp.bfloat16),
        in_specs=[pl.BlockSpec(memory_space=pl.ANY)] * len(arrays),
        out_specs=pl.BlockSpec(memory_space=pl.ANY),
        scratch_shapes=[
            pltpu.VMEM(dims, jnp.bfloat16),
            pltpu.SemaphoreType.DMA((moves,)),
            pltpu.SemaphoreType.DMA((moves,)),
        ],
        compiler_params=pltpu.CompilerParams(vmem_limit_bytes=VMEM_BYTES),
        cost_estimate=LITTLE,
        name="assemble",
    )(*arrays)
    return gathered.reshape(grid.count * rows, width)


@jax.tree_util.register_pytree_node_class
class Source:
    def __init__(self, array, first=0):
        self.array, self.first = array, first

    def tree_flatten(self):
        return (self.array,), self.first

    @classmethod
    def tree_unflatten(cls, first, leaves):
        return cls(*leaves, first)


class Place:
    def __init__(self, slot, table=None):
        self.slot, self.table = slot, table

    def of(self, numbers):
        here = numbers[self.slot]
        if self.table is None:
            return here
        return sum(jnp.where(here == at, entry, 0) for at, entry in enumerate(self.table))

    def __eq__(self, other):
        return isinstance(other, Place) and (self.slot, self.table) == (other.slot, other.table)

    def __hash__(self):
        return hash((self.slot, self.table))


class Merge:
    STRIP = 16
    STEPS = 2

    def __init__(self, grid, numbers):
        self.grid, self.numbers = grid, numbers
        self.inputs, self.outputs, self.keys = [], [], {}

    def cut(self, array, places):
        key = (id(array), places)
        if key not in self.keys:
            self.keys[key] = len(self.inputs)
            self.inputs.append((array, places))
        return self.keys[key]

    def terms(self, sources, places, low, high):
        found = []
        for source in sources:
            first = source.first
            if first <= low and high <= first + source.array.shape[-2]:
                found.append((self.cut(source.array, places), low - first, high - first))
        return found

    def add(self, *options, chosen=None):
        self.outputs.append((options, chosen))
        return len(self.outputs) - 1

    def shape(self, options):
        array, places = self.inputs[options[0][0][0][0]]
        lead = [size for size, place in zip(array.shape, places) if place is None]
        rows = sum(segment[0][2] - segment[0][1] for segment in options[0])
        return (*lead, rows, array.shape[-1])

    def run(self):
        edges = [
            edge
            for options, _ in self.outputs
            for segments in options
            for segment in segments
            for term in segment
            for edge in term[1:]
        ]
        if any(edge % self.STRIP for edge in edges):
            return self.run_plain()
        shapes = [self.shape(options) for options, _ in self.outputs]
        def spec(array, places):
            block = [
                None if place is not None else size for size, place in zip(array.shape, places)
            ]
            return pl.BlockSpec(
                (*block, array.shape[-2], array.shape[-1] // self.STEPS),
                lambda step, held: (
                    *[0 if place is None else place.of(held) for place in places], 0, step
                ),
            )

        return pl.pallas_call(
            self.kernel,
            grid_spec=pltpu.PrefetchScalarGridSpec(
                num_scalar_prefetch=1,
                grid=(self.STEPS,),
                in_specs=[spec(*pair) for pair in self.inputs],
                out_specs=[
                    pl.BlockSpec(
                        (*dims[:-1], dims[-1] // self.STEPS),
                        lambda step, held, axes=len(dims): (0,) * (axes - 1) + (step,),
                    )
                    for dims in shapes
                ],
            ),
            out_shape=[jax.ShapeDtypeStruct(dims, jnp.bfloat16) for dims in shapes],
            compiler_params=pltpu.CompilerParams(vmem_limit_bytes=VMEM_LESS),
            cost_estimate=LITTLE,
            name="merge",
        )(self.numbers, *[array for array, _ in self.inputs])

    def kernel(self, held, *refs):
        inputs, outputs = refs[: len(self.inputs)], refs[len(self.inputs) :]
        for out, (options, chosen) in zip(outputs, self.outputs):
            for number, segments in enumerate(options):
                write = functools.partial(self.write, out, segments, inputs)
                if chosen is None:
                    write()
                else:
                    pl.when(chosen.of(held) == number)(write)

    def write(self, out, segments, inputs):
        start = 0
        for segment in segments:
            count = segment[0][2] - segment[0][1]
            strips = count // self.STRIP
            unroll = max(part for part in range(1, 9) if strips % part == 0)
            for lead in itertools.product(*[range(size) for size in out.shape[:-2]]):

                @pl.loop(0, strips, unroll=unroll)
                def _(strip, start=start, lead=lead, segment=segment):
                    def rows(first):
                        at = pl.multiple_of(first + strip * self.STRIP, self.STRIP)
                        return (*lead, pl.ds(at, self.STRIP), slice(None))

                    added = sum(inputs[k][rows(low)].astype(jnp.float32) for k, low, _ in segment)
                    out[rows(start)] = added.astype(jnp.bfloat16)

            start += count

    def run_plain(self):
        def part(term):
            array, places = self.inputs[term[0]]
            axis = 0
            for place in places:
                if place is None:
                    axis += 1
                else:
                    array = lax.dynamic_index_in_dim(
                        array, place.of(self.numbers), axis, keepdims=False
                    )
            return lax.slice_in_dim(array, term[1], term[2], axis=-2 + array.ndim)

        results = []
        for options, chosen in self.outputs:
            made = []
            for segments in options:
                sums = [
                    sum(part(term).astype(jnp.float32) for term in segment).astype(jnp.bfloat16)
                    for segment in segments
                ]
                made.append(jnp.concatenate(sums, axis=-2) if len(sums) > 1 else sums[0])
            results.append(made[0])
            for number in range(1, len(made)):
                results[-1] = jnp.where(chosen.of(self.numbers) == number, made[number], results[-1])
        return results


def swapped(grid, kept_and_sent):
    kept, sent = kept_and_sent
    return [Source(kept), Source(grid.shift(sent, "c", 1))]


def halves_of(sources):
    rows = sources[0].array.shape[-2]
    return (0, rows // 2), (rows // 2, rows)


def corners(merge, here, sources, lead=1):
    low, high = halves_of(sources)
    grid, whole_axes = merge.grid, (None,) * lead
    slots = {}
    for j in grid.hops("x"):
        for l in grid.hops("y"):
            place = (*whole_axes, here("y", l), here("x", j))
            slots[j, l] = (
                merge.add([merge.terms(sources, place, *low)]),
                merge.add([merge.terms(sources, place, *high)]),
            )

    def go(made):
        return {
            (j, l): (grid.shift(made[first], "x", j), grid.shift(made[second], "y", l))
            for (j, l), (first, second) in slots.items()
        }

    return go


def sides(merge, here, sources, crossed, lead=1):
    low, high = halves_of(sources)
    grid, whole_axes = merge.grid, (None,) * lead
    own_place = (*whole_axes, here("y", 0), here("x", 0))
    bare = (None,) * lead
    own = merge.add([merge.terms(sources, own_place, *half) for half in (low, high)])
    to_x, to_y = {}, {}
    for j in grid.hops("x"):
        place = (*whole_axes, here("y", 0), here("x", j))
        received = [Source(crossed[j, l][1], high[0]) for l in grid.hops("y")]
        to_x[j] = merge.add(
            [
                merge.terms(sources, place, *low),
                merge.terms(sources, place, *high) + merge.terms(received, bare, *high),
            ]
        )
    for l in grid.hops("y"):
        place = (*whole_axes, here("y", l), here("x", 0))
        received = [Source(crossed[j, l][0]) for j in grid.hops("x")]
        to_y[l] = merge.add(
            [
                merge.terms(sources, place, *low) + merge.terms(received, bare, *low),
                merge.terms(sources, place, *high),
            ]
        )

    def go(made):
        terms = [made[own]]
        terms += [grid.shift(made[to_x[j]], "x", j) for j in to_x]
        terms += [grid.shift(made[to_y[l]], "y", l) for l in to_y]
        return [Source(term) for term in terms]

    return go


def line(merge, here, groups, hops, rows=None, lead=0):
    grid = merge.grid
    plane = here("z", hops)
    owner = {
        number: (group, at)
        for group, (_, planes) in enumerate(groups)
        for at, number in enumerate(planes)
    }
    numbers = range(grid.size["z"])
    options = []
    for group, (sources, _) in enumerate(groups):
        index = Place(
            plane.slot, tuple(owner[n][1] if owner[n][0] == group else 0 for n in numbers)
        )
        place = (index, *(None,) * lead)
        parts = halves_of(sources) if rows is None else (rows,)
        options.append([merge.terms(sources, place, *part) for part in parts])
    chosen = Place(plane.slot, tuple(owner[n][0] for n in numbers)) if len(groups) > 1 else None
    slot = merge.add(*options, chosen=chosen)
    return lambda made: grid.shift(made[slot], "z", hops) if hops else made[slot]


def total_of(*terms):
    return sum(term.astype(jnp.float32) for term in terms)


class Steps:
    def __init__(self, **live):
        self.__dict__.update(live)

    def close(self):
        self.__dict__.update(after_tree(dict(self.__dict__)))

    def drop(self, *names):
        for name in names:
            del self.__dict__[name]


def small_sum(grid, value, axes):
    for axis in axes:
        value = value + sum(grid.shift(value, axis, hops) for hops in grid.hops(axis))
    return value


LITTLE = pl.CostEstimate(flops=1, bytes_accessed=1, transcendentals=0)


def whole(array):
    return pl.BlockSpec(array.shape, lambda *k: (0,) * array.ndim)


def in_vmem(array):
    return pl.BlockSpec(memory_space=pltpu.VMEM)


def kernel_call(
    body, name, grid, in_specs, out_shape, out_specs, scratch=(), aliases=None, vmem=VMEM_BYTES
):
    return pl.pallas_call(
        body,
        grid=grid,
        in_specs=in_specs,
        out_shape=out_shape,
        out_specs=out_specs,
        scratch_shapes=scratch,
        input_output_aliases=aliases or {},
        compiler_params=pltpu.CompilerParams(vmem_limit_bytes=vmem),
        cost_estimate=LITTLE,
        name=name,
    )


def shape_of(dims, dtype):
    return jax.ShapeDtypeStruct(dims, dtype)


TRIO = (GROUP + 1) * HEAD_WIDTH


def lanes_of(head):
    return slice(head * HEAD_WIDTH, (head + 1) * HEAD_WIDTH)


def turned(values):
    return pltpu.roll(values, HEAD_WIDTH // 2, 1)


def stacked(values, rows, heads=GROUP):
    return jnp.concatenate([values[rows, lanes_of(g)] for g in range(heads)], axis=0)


def query_blocks(micro_rows):
    half = micro_rows // 2
    return [(0, half), (half, micro_rows)]


def powers_of(queries, keys, bias):
    return jnp.exp2(contract_last(queries, keys) * EXP2_SCALE + bias)


def group_bias(bias, micro, begin, end):
    return jnp.concatenate([bias[micro, begin:end, :end]] * GROUP, axis=0)


def attention_kernel(normed, wq, wk, wv, cosine, sine, bias, gain_q, gain_k, *outputs):
    norms, scales, turns, value, context = outputs[-5:]
    norms[:, : GROUP * HEAD_WIDTH] = contract_last(normed[...], wq[...])
    both = contract_last(normed[...], jnp.concatenate([wk[...], wv[...]], axis=0))
    norms[:, GROUP * HEAD_WIDTH :] = both[:, :HEAD_WIDTH]
    value[...] = both[:, HEAD_WIDTH:].astype(jnp.bfloat16)
    micro_count, micro_rows, _ = bias.shape
    for micro in range(micro_count):
        start = micro * micro_rows
        rows = slice(start, start + micro_rows)
        for head in range(GROUP + 1):
            raw = norms[rows, lanes_of(head)]
            scale = lax.rsqrt(jnp.mean(raw * raw, axis=-1, keepdims=True) + NORM_EPS)
            scale = jnp.broadcast_to(scale, raw.shape)
            normal = raw * scale
            gained = normal * (gain_q[...] if head < GROUP else gain_k[...])
            norms[rows, lanes_of(head)] = normal
            scales[rows, lanes_of(head)] = scale
            turns[rows, lanes_of(head)] = (
                gained * cosine[rows, :] + turned(gained) * sine[rows, :]
            ).astype(jnp.bfloat16)
        keys = turns[rows, lanes_of(GROUP)]
        for begin, end in query_blocks(micro_rows):
            block = slice(start + begin, start + end)
            count = end - begin
            powers = powers_of(
                stacked(turns, block), keys[:end], group_bias(bias, micro, begin, end)
            )
            inverse = 1.0 / jnp.sum(powers, axis=-1, keepdims=True)
            probs = (powers * inverse).astype(jnp.bfloat16)
            mixed = plain_product(probs, value[start : start + end, :]).astype(jnp.bfloat16)
            for g in range(GROUP):
                context[block, lanes_of(g)] = mixed[g * count : (g + 1) * count, :]


def with_turn(values):
    return jnp.concatenate([values, turned(values)], axis=1)


def head_backward(normal, scale, gain, grad, cos, sin):
    grad_normed = (grad[:, :HEAD_WIDTH] * cos - grad[:, HEAD_WIDTH:] * sin) * SCORE_SCALE
    scaled = gain * grad_normed
    terms = grad_normed * normal
    mean = jnp.mean(scaled * normal, axis=-1, keepdims=True)
    grad_raw = scale * (scaled - normal * mean)
    return grad_raw.astype(jnp.bfloat16), jnp.sum(terms, axis=0, keepdims=True)


def put_by_core(rows_per_device, result, part, at, plane, kept, sent, sems, sem):
    rows = result.shape[0]
    if rows >= 2 * rows_per_device:
        chips = rows // (2 * rows_per_device)
        part[0], part[1] = by_core(rows_per_device, result)
        stretch = pl.ds(at * chips, chips)
        return [
            pltpu.make_async_copy(part.at[0], kept.at[plane, stretch], sems.at[sem]),
            pltpu.make_async_copy(part.at[1], sent.at[plane, stretch], sems.at[sem + 1]),
        ]
    part[0, 0] = result
    mine = (at + lax.axis_index("dp")) % 2 == 0
    return [
        Either(
            mine,
            pltpu.make_async_copy(part.at[0, 0], kept.at[plane, at // 2], sems.at[sem]),
            pltpu.make_async_copy(part.at[0, 0], sent.at[plane, at // 2], sems.at[sem + 1]),
        )
    ]


class Either:
    def __init__(self, first_one, first, second):
        self.first_one, self.first, self.second = first_one, first, second

    def start(self):
        pl.when(self.first_one)(self.first.start)
        pl.when(jnp.logical_not(self.first_one))(self.second.start)

    def wait(self):
        pl.when(self.first_one)(self.first.wait)
        pl.when(jnp.logical_not(self.first_one))(self.second.wait)


def attention_backward_kernel(
    first, rows_per_device, held, norms, scales, turns, value, grad_context, cosine, sine, bias,
    gain_q, gain_k, normed, wq, wk, wv, *others,
):
    grad_raw_all, part_q, part_k, part_v, sems = others[-5:]
    kv_kept, kv_sent, total, terms_q, terms_k = others[-10:-5]

    @pl.when(pl.program_id(0) == 0)
    def _():
        terms_q[...] = jnp.zeros_like(terms_q)
        terms_k[...] = jnp.zeros_like(terms_k)
        if held:
            total[...] = others[0][...]
        else:
            total[...] = jnp.zeros_like(total)

    micro_count, micro_rows, _ = bias.shape
    for micro in range(micro_count):
        start = micro * micro_rows
        rows = slice(start, start + micro_rows)
        keys = turns[rows, lanes_of(GROUP)]
        both_keys = with_turn(keys)
        grad_values, grad_keys = 0.0, 0.0
        for begin, end in query_blocks(micro_rows):
            block = slice(start + begin, start + end)
            count = end - begin
            cos, sin = cosine[block, :], sine[block, :]
            queries = stacked(turns, block)
            powers = powers_of(queries, keys[:end], group_bias(bias, micro, begin, end))
            probs = powers * (1.0 / jnp.sum(powers, axis=-1, keepdims=True))
            grads = stacked(grad_context, block)
            grad_probs = contract_last(grads, value[start : start + end, :])
            weighted = probs * grad_probs
            centre = jnp.sum(weighted, axis=-1, keepdims=True)
            grad_scores = (weighted - probs * centre).astype(jnp.bfloat16)
            pad = ((0, micro_rows - end), (0, 0))
            grad_values += jnp.pad(contract_first(probs.astype(jnp.bfloat16), grads), pad)
            grad_keys += jnp.pad(contract_first(grad_scores, with_turn(queries)), pad)
            grad_queries = plain_product(grad_scores, both_keys[:end])
            for g in range(GROUP):
                grad_raw, terms = head_backward(
                    norms[block, lanes_of(g)],
                    scales[block, lanes_of(g)],
                    gain_q[...],
                    grad_queries[g * count : (g + 1) * count, :],
                    cos,
                    sin,
                )
                grad_raw_all[block, lanes_of(g)] = grad_raw
                terms_q[...] += terms
        grad_raw_all[rows, lanes_of(GROUP + 1)] = grad_values.astype(jnp.bfloat16)
        grad_raw, terms = head_backward(
            norms[rows, lanes_of(GROUP)],
            scales[rows, lanes_of(GROUP)],
            gain_k[...],
            grad_keys,
            cosine[rows, :],
            sine[rows, :],
        )
        grad_raw_all[rows, lanes_of(GROUP)] = grad_raw
        terms_k[...] += terms
    head = first + pl.program_id(0)
    half = KEY_VALUE_HEADS // 2
    queries_kept, queries_sent = (kv_kept, kv_sent) if first >= half else others[-12:-10]
    wide = GROUP * HEAD_WIDTH
    result = contract_first(grad_raw_all[...], normed[...]).astype(jnp.bfloat16)
    result_q, result_k, result_v = (
        result[:wide, :],
        result[wide : wide + HEAD_WIDTH, :],
        result[wide + HEAD_WIDTH :, :],
    )
    copies = [
        *put_by_core(
            rows_per_device, result_q, part_q, head % half, 0, queries_kept, queries_sent, sems, 0
        ),
        *put_by_core(rows_per_device, result_k, part_k, head, 1, kv_kept, kv_sent, sems, 2),
        *put_by_core(rows_per_device, result_v, part_v, head, 2, kv_kept, kv_sent, sems, 4),
    ]
    for copy in copies:
        copy.start()
    weights = jnp.concatenate([wq[...], wk[...], wv[...]], axis=0)
    total[...] += plain_product(grad_raw_all[...], weights)
    for copy in copies:
        copy.wait()


def by_core(rows_per_device, part):
    pairs = part.reshape(-1, 2, rows_per_device, part.shape[-1])
    here = lax.axis_index("dp") % 2 == 0
    first, second = pairs[:, 0], pairs[:, 1]
    return jnp.where(here, first, second), jnp.where(here, second, first)


def heads(rows, width, first=0):
    return pl.BlockSpec((rows, width), lambda k: (0, first + k))


def head_rows(heads_in, depth, first):
    return pl.BlockSpec((heads_in * HEAD_WIDTH, depth), lambda k: (first + k, 0))


def qkv_rows_of(depth, first):
    return [
        head_rows(GROUP, depth, first),
        head_rows(1, depth, QUERY_HEADS + first),
        head_rows(1, depth, QUERY_HEADS + KEY_VALUE_HEADS + first),
    ]


def attention(normed, qkv_full, tables, gain_q, gain_k, context, first, count):
    tokens, depth = normed.shape
    wide = GROUP * HEAD_WIDTH
    whole_context = shape_of((tokens, QUERY_HEADS * HEAD_WIDTH), jnp.bfloat16)
    held = [] if context is None else [context]
    return kernel_call(
        attention_kernel,
        "attention",
        (count,),
        [
            in_vmem(normed),
            *qkv_rows_of(depth, first),
            *[in_vmem(table) for table in tables],
            in_vmem(gain_q),
            in_vmem(gain_k),
            *[pl.BlockSpec(memory_space=pl.ANY)] * len(held),
        ],
        (
            shape_of((tokens, count * TRIO), jnp.float32),
            shape_of((tokens, count * TRIO), jnp.float32),
            shape_of((tokens, count * TRIO), jnp.bfloat16),
            shape_of((tokens, count * HEAD_WIDTH), jnp.bfloat16),
            whole_context,
        ),
        (
            heads(tokens, TRIO),
            heads(tokens, TRIO),
            heads(tokens, TRIO),
            heads(tokens, HEAD_WIDTH),
            heads(tokens, wide, first),
        ),
        aliases={9: 4} if held else None,
        vmem=VMEM_LESS,
    )(normed, qkv_full, qkv_full, qkv_full, *tables, gain_q, gain_k, *held)


def attention_backward(
    norms, scales, turns, value, grad_context, tables, gain_q, gain_k,
    normed, qkv_full, total, parts, first, rows_per_device,
):
    tokens, depth = normed.shape
    wide = GROUP * HEAD_WIDTH
    count = value.shape[1] // HEAD_WIDTH
    half = KEY_VALUE_HEADS // 2
    stretch = half * wide // (2 * rows_per_device)
    early = shape_of((1, stretch, rows_per_device, depth), jnp.bfloat16)
    late = shape_of((3, stretch, rows_per_device, depth), jnp.bfloat16)
    shapes = [late, late] if first >= half else [early, early, late, late]
    held = [] if total is None else [total, *parts]

    def part_scratch(rows):
        chips = max(rows // (2 * rows_per_device), 1)
        height = min(rows, rows_per_device)
        return pltpu.VMEM((2, chips, height, depth), jnp.bfloat16)

    anywhere = pl.BlockSpec(memory_space=pl.ANY)
    return kernel_call(
        functools.partial(attention_backward_kernel, first, rows_per_device, len(held)),
        "attention_backward",
        (count,),
        [
            heads(tokens, TRIO),
            heads(tokens, TRIO),
            heads(tokens, TRIO),
            heads(tokens, HEAD_WIDTH),
            heads(tokens, wide, first),
            *[in_vmem(table) for table in tables],
            in_vmem(gain_q),
            in_vmem(gain_k),
            in_vmem(normed),
            *qkv_rows_of(depth, first),
            *[in_vmem(total)] * min(len(held), 1),
            *[anywhere] * max(len(held) - 1, 0),
        ],
        (
            *shapes,
            shape_of((tokens, depth), jnp.float32),
            shape_of(gain_q.shape, jnp.float32),
            shape_of(gain_k.shape, jnp.float32),
        ),
        (*[anywhere] * len(shapes), in_vmem(normed), in_vmem(gain_q), in_vmem(gain_k)),
        scratch=[
            pltpu.VMEM((tokens, TRIO + HEAD_WIDTH), jnp.bfloat16),
            part_scratch(wide),
            part_scratch(HEAD_WIDTH),
            part_scratch(HEAD_WIDTH),
            pltpu.SemaphoreType.DMA((6,)),
        ],
        aliases={15 + slot: slot for slot in range(len(shapes))} if held else None,
        vmem=VMEM_LESS,
    )(
        norms, scales, turns, value, grad_context, *tables, gain_q, gain_k,
        normed, qkv_full, qkv_full, qkv_full, *held,
    )


ROW_TILE = 256
FF_TILE = 512
BACK_TILE = 384
STRIP = 64


def project_kernel(context, weight, residual, gain, middle, normed):
    middle[...] = residual[...] + contract_last(context[...], weight[...])

    @pl.loop(0, middle.shape[0] // STRIP)
    def _(strip):
        rows = pl.ds(pl.multiple_of(strip * STRIP, STRIP), STRIP)
        values = middle[rows, :]
        normed[rows, :] = (values * rms_scale(values) * gain[...]).astype(jnp.bfloat16)


def rows_of(array, tile):
    return pl.BlockSpec((tile, array.shape[1]), lambda k: (k, 0))


def project(context, weight, residual, gain):
    return kernel_call(
        project_kernel,
        "project",
        (residual.shape[0] // ROW_TILE,),
        [rows_of(context, ROW_TILE), whole(weight), rows_of(residual, ROW_TILE), whole(gain)],
        (shape_of(residual.shape, jnp.float32), shape_of(residual.shape, jnp.bfloat16)),
        (rows_of(residual, ROW_TILE), rows_of(residual, ROW_TILE)),
    )(context, weight, residual, gain)


def feed_kernel(normed, weights, hidden, slope, lift):
    tile = hidden.shape[1]
    both = contract_last(normed[...], weights[...].reshape(2 * tile, -1))
    gate, upward = both[:, :tile], both[:, tile:]
    sigma = jax.nn.sigmoid(gate)
    lifted = gate * sigma
    lift[...] = lifted.astype(jnp.bfloat16)
    slope[...] = (upward * sigma * (1.0 + gate * (1.0 - sigma))).astype(jnp.bfloat16)
    hidden[...] = (lifted * upward).astype(jnp.bfloat16)


def columns_of(rows, tile, first=0):
    return pl.BlockSpec((rows, tile), lambda k: (0, first + k))


def gate_and_up(tile, depth, first=0):
    return pl.BlockSpec((2, tile, depth), lambda k: (0, first + k, 0))


def feed(normed, weight):
    tokens, depth = normed.shape
    columns = columns_of(tokens, FF_TILE)
    tiles = FF // FF_TILE
    return kernel_call(
        feed_kernel,
        "feed",
        (tiles,),
        [whole(normed), gate_and_up(FF_TILE, depth)],
        (
            shape_of((tokens, FF), jnp.bfloat16),
            shape_of((tokens, FF), jnp.bfloat16),
            shape_of((tokens, FF), jnp.bfloat16),
        ),
        (columns, columns, columns),
    )(normed, weight.reshape(2, FF, depth))


def finish_kernel(hidden, weight, residual, output):
    output[...] = residual[...] + contract_last(hidden[...], weight[...])


def finish(hidden, weight, residual):
    return kernel_call(
        finish_kernel,
        "finish",
        (residual.shape[0] // ROW_TILE,),
        [rows_of(hidden, ROW_TILE), whole(weight), rows_of(residual, ROW_TILE)],
        shape_of(residual.shape, jnp.float32),
        rows_of(residual, ROW_TILE),
    )(hidden, weight, residual)


def outer_kernel(rows_per_device, left, right, kept, sent, turned_left):
    @pl.when(pl.program_id(0) == 0)
    def _():
        turned_left[...] = left[...].T

    part = plain_product(turned_left[...], right[...]).astype(jnp.bfloat16)
    kept[...], sent[...] = by_core(rows_per_device, part)


def chip_columns(chips, rows, width):
    return pl.BlockSpec((chips, rows, width), lambda k: (0, 0, k))


def outer(left, right, rows_per_device):
    chips = left.shape[1] // (2 * rows_per_device)
    shape = shape_of((chips, rows_per_device, right.shape[1]), jnp.bfloat16)
    block = chip_columns(chips, rows_per_device, FF_TILE)
    return kernel_call(
        functools.partial(outer_kernel, rows_per_device),
        "outer",
        (right.shape[1] // FF_TILE,),
        [whole(left), columns_of(right.shape[0], FF_TILE)],
        (shape, shape),
        (block, block),
        scratch=[pltpu.VMEM((left.shape[1], left.shape[0]), jnp.bfloat16)],
    )(left, right)


def feed_backward_kernel(
    rows_per_device, grad_feed, down, slope, lift, normed, weights, *others
):
    kept, sent, total = others[-3:]

    @pl.when(pl.program_id(0) == 0)
    def _():
        total[...] = others[0][...] if len(others) > 3 else jnp.zeros_like(total)

    grad_hidden = plain_product(grad_feed[...], down[...])
    grads = jnp.concatenate(
        [
            (grad_hidden * slope[...].astype(jnp.float32)).astype(jnp.bfloat16),
            (grad_hidden * lift[...].astype(jnp.float32)).astype(jnp.bfloat16),
        ],
        axis=1,
    )
    tile = grad_hidden.shape[1]
    part = contract_first(grads, normed[...]).astype(jnp.bfloat16)
    for plane in range(2):
        kept[plane], sent[plane] = by_core(
            rows_per_device, part[plane * tile : (plane + 1) * tile, :]
        )
    total[...] += plain_product(grads, weights[...].reshape(2 * tile, -1))


def feed_backward(grad_feed, down, slope, lift, normed, weight, total, half, rows_per_device):
    tokens, depth = normed.shape
    tiles = FF // BACK_TILE
    count = tiles // 2
    first = half * count
    held = [] if total is None else [total]
    chips = BACK_TILE // (2 * rows_per_device)
    shape = shape_of((2, count * chips, rows_per_device, depth), jnp.bfloat16)
    block = pl.BlockSpec((2, chips, rows_per_device, depth), lambda k: (0, k, 0, 0))
    return kernel_call(
        functools.partial(feed_backward_kernel, rows_per_device),
        "feed_backward",
        (count,),
        [
            whole(grad_feed),
            columns_of(depth, BACK_TILE, first),
            columns_of(tokens, BACK_TILE, first),
            columns_of(tokens, BACK_TILE, first),
            whole(normed),
            gate_and_up(BACK_TILE, depth, first),
            *[whole(total) for total in held],
        ],
        (shape, shape, shape_of((tokens, depth), jnp.float32)),
        (block, block, pl.BlockSpec((tokens, depth), lambda k: (0, 0))),
    )(grad_feed, down, slope, lift, normed, weight.reshape(2, FF, depth), *held)


def project_backward_kernel(
    rows_per_device, grad_normed, middle, out_grad, gain, context, weight,
    kept, sent, grad_context, grad_middle, gain_terms, branch, turned_branch,
):
    step = pl.program_id(0)
    row_steps = branch.shape[0] // ROW_TILE

    @pl.when(step == 0)
    def _():
        gain_terms[...] = jnp.zeros_like(gain_terms)

    @pl.when(step < row_steps)
    def _():
        start = pl.multiple_of(step * ROW_TILE, ROW_TILE)

        @pl.loop(0, ROW_TILE // STRIP)
        def _(strip):
            rows = pl.ds(pl.multiple_of(strip * STRIP, STRIP), STRIP)
            values = middle[rows, :]
            grad, terms = norm_backward(values, rms_scale(values), gain[...], grad_normed[rows, :])
            grad = out_grad[rows, :] + grad
            grad_middle[rows, :] = grad
            branch[pl.ds(pl.multiple_of(start + strip * STRIP, STRIP), STRIP), :] = grad.astype(
                jnp.bfloat16
            )
            gain_terms[...] += jnp.sum(terms, axis=0, keepdims=True)

    @pl.when(step == row_steps)
    def _():
        turned_branch[...] = branch[...].T

    @pl.when(step >= row_steps)
    def _():
        part = plain_product(turned_branch[...], context[...]).astype(jnp.bfloat16)
        kept[...], sent[...] = by_core(rows_per_device, part)
        grad_context[...] = plain_product(branch[...], weight[...]).astype(jnp.bfloat16)


def project_backward(grad_normed, middle, out_grad, gain, context, weight, rows_per_device):
    tokens, depth = middle.shape
    width = context.shape[1]
    chips = depth // (2 * rows_per_device)
    shape = shape_of((chips, rows_per_device, width), jnp.bfloat16)
    row_steps = tokens // ROW_TILE

    def column(k):
        return jnp.maximum(k - row_steps, 0)

    def row_block(k):
        return (jnp.minimum(k, row_steps - 1), 0)

    rows = pl.BlockSpec((ROW_TILE, depth), row_block)
    block = pl.BlockSpec((chips, rows_per_device, FF_TILE), lambda k: (0, 0, column(k)))

    def columns(count):
        return pl.BlockSpec((count, FF_TILE), lambda k: (0, column(k)))

    return kernel_call(
        functools.partial(project_backward_kernel, rows_per_device),
        "project_backward",
        (row_steps + width // FF_TILE,),
        [rows, rows, rows, whole(gain), columns(tokens), columns(depth)],
        (
            shape,
            shape,
            shape_of((tokens, width), jnp.bfloat16),
            shape_of((tokens, depth), jnp.float32),
            shape_of(gain.shape, jnp.float32),
        ),
        (block, block, columns(tokens), rows, whole(gain)),
        scratch=[
            pltpu.VMEM((tokens, depth), jnp.bfloat16),
            pltpu.VMEM((depth, tokens), jnp.bfloat16),
        ],
    )(grad_normed, middle, out_grad, gain, context, weight)


def position_tables(segment_ids):
    _, micro_rows = segment_ids.shape
    order = jnp.arange(micro_rows, dtype=jnp.int32)
    same = segment_ids[:, :, None] == segment_ids[:, None, :]
    earlier = order[None, :] < order[:, None]
    positions = jnp.sum(jnp.where(same & earlier[None], 1, 0), axis=2).astype(jnp.int32)
    half_size = HEAD_WIDTH // 2
    frequency = ROPE_BASE ** (-(jnp.arange(half_size, dtype=jnp.float32) * (2.0 / HEAD_WIDTH)))
    angles = positions.reshape(-1, 1).astype(jnp.float32) * frequency[None, :]
    cosine, sine = jnp.cos(angles), jnp.sin(angles)
    allowed = same & (earlier | (order[None, :] == order[:, None]))[None]
    return (
        jnp.concatenate([cosine, cosine], axis=-1),
        jnp.concatenate([-sine, sine], axis=-1),
        jnp.where(allowed, 0.0, -1e30).astype(jnp.float32),
    )


def adamw(weight, first, second, grad, rate, decay):
    first_new = BETA_ONE * first + (1.0 - BETA_ONE) * grad
    second_new = BETA_TWO * second + (1.0 - BETA_TWO) * grad * grad
    corrected = (
        first_new
        / (1.0 - BETA_ONE**STEP)
        / (jnp.sqrt(second_new / (1.0 - BETA_TWO**STEP)) + ADAM_EPS)
    )
    return (weight - rate * (corrected + decay * weight), first_new, second_new)


def per_device(
    grid,
    activations,
    segment_ids,
    out_grad,
    qkv_weight,
    qkv_first,
    qkv_second,
    out_weight,
    out_first,
    out_second,
    gate_up_weight,
    gate_up_first,
    gate_up_second,
    down_weight,
    down_first,
    down_second,
    norm_gains,
    gains_first,
    gains_second,
):
    qkv_low = qkv_weight.astype(jnp.bfloat16)
    out_low = out_weight.astype(jnp.bfloat16)
    gate_up_low = gate_up_weight.astype(jnp.bfloat16)
    down_low = down_weight.astype(jnp.bfloat16)

    gain_count = norm_gains.shape[0]
    gain_start = lax.axis_index("dp") * gain_count
    all_gains = jnp.zeros((1, gain_count * grid.count), jnp.bfloat16)
    all_gains = lax.dynamic_update_slice(
        all_gains, norm_gains.astype(jnp.bfloat16)[None], (0, gain_start)
    )
    size = grid.size
    heads_of = KEY_VALUE_HEADS // 4
    out_rows, gate_rows = out_low.shape[0], gate_up_low.shape[0]
    qkv_rows, down_rows = qkv_low.shape[0], down_low.shape[0]

    tables = position_tables(segment_ids)
    scale_one = rms_scale(activations)
    v = Steps(out_low=out_low, gate_up_low=gate_up_low)
    v.qkv_line = z_pieces(grid, qkv_low, False)
    down_block = jnp.concatenate([down_low, rows_of_gains(all_gains, down_low.shape[1])], axis=0)
    down_sides = plane_sides(grid, down_block)
    down_corners = plane_corners(grid, down_sides, v.qkv_line[1], cut_at=down_rows)
    v.down_chip, v.gains, down_places = chip_plane(down_block, down_sides, down_corners, down_rows)
    v.close()

    v.qkv_column = jnp.stack(v.qkv_line)
    v.qkv_sides = plane_sides(grid, v.qkv_column)
    all_gains = v.gains.reshape(1, -1)[:, : gain_count * grid.count]
    out_block = jnp.concatenate([v.out_low, rows_of_gains(all_gains, out_low.shape[1])], axis=0)
    v.out_line = z_pieces(grid, out_block, False)
    v.grad_feed = out_grad.astype(jnp.bfloat16)
    v.drop("qkv_line", "out_low", "gains")
    v.close()

    grad_feed = v.grad_feed
    v.out_column = jnp.stack([piece[:out_rows] for piece in v.out_line])
    gains = sum(piece[out_rows:].astype(jnp.float32) for piece in v.out_line)
    gains = gains.reshape(1, -1)[:, : gain_count * grid.count]
    v.gains = gains
    v.qkv_corners = plane_corners(grid, v.qkv_sides)
    v.gate_up_moved = {1: grid.shift(v.gate_up_low, "z", 1)}
    v.qkv_sides_swapped = swap_tree(grid, v.qkv_sides)
    v.drop("grad_feed", "out_line")
    v.close()

    every = tuple(range(size["z"]))
    middle_plane = size["z"] // 2
    gains = small_sum(grid, v.gains, "c")
    gain_one, gain_two = gains[:, :D], gains[:, D : 2 * D]
    gain_query = gains[:, 2 * D : 2 * D + HEAD_WIDTH]
    gain_key = gains[:, 2 * D + HEAD_WIDTH :]
    normed_one = (activations * scale_one * gain_one).astype(jnp.bfloat16)
    qkv_column_swapped, qkv_corners_swapped = swap_tree(grid, (v.qkv_column, v.qkv_corners))
    v.out_sides = plane_sides(grid, v.out_column)
    v.near_column = jnp.stack([v.gate_up_low, v.gate_up_moved[1]])
    v.near_sides = plane_sides(grid, v.near_column)
    v.gate_up_moved[2] = grid.shift(v.gate_up_low, "z", 2)
    qkv_full = assemble(
        grid,
        plane_pieces(every, v.qkv_column, v.qkv_sides, v.qkv_corners),
        plane_pieces(every, qkv_column_swapped, v.qkv_sides_swapped, qkv_corners_swapped),
    )
    v.drop("qkv_column", "qkv_sides", "qkv_corners", "gate_up_low", "gains")
    v.drop("qkv_sides_swapped")
    parts = []

    def attention_part(part, context):
        *kept, context = attention(
            after(normed_one, *flat(context)),
            qkv_full,
            tables,
            gain_query,
            gain_key,
            context,
            part * heads_of,
            heads_of,
        )
        parts.append(kept)
        return context

    context = attention_part(0, None)
    v.gate_up_moved[3] = grid.shift(
        after(gate_up_low, context, v.gate_up_moved[2]), "z", 3
    )
    v.context = attention_part(1, context)
    v.close()

    v.far_column = jnp.stack([v.gate_up_moved[2], v.gate_up_moved[3]])
    v.out_corners = plane_corners(grid, v.out_sides)
    v.far_sides = plane_sides(grid, v.far_column)
    v.down_moved = {1: grid.shift(v.down_chip, "z", 1)}
    v.context = attention_part(3, attention_part(2, v.context))
    v.drop("gate_up_moved")
    v.close()

    v.gate_up_corners = plane_corners(grid, (v.near_sides[0], v.far_sides[1]), halved=False)
    v.down_moved[3] = grid.shift(v.down_chip, "z", 3)
    out_swapped = swap_together(grid, (v.out_column, v.out_sides, v.out_corners))
    v.near_sides_swapped = swap_tree(grid, after_tree(v.near_sides, out_swapped))
    out_full = assemble(
        grid,
        plane_pieces(every, v.out_column, v.out_sides, v.out_corners),
        plane_pieces(every, *out_swapped),
    )
    v.far_sides_swapped = swap_tree(
        grid, after_tree(v.far_sides, out_full, v.near_sides_swapped)
    )
    middle, v.normed_two = project(v.context, out_full, activations, gain_two)
    context = v.context
    v.drop("out_column", "out_sides", "out_corners", "context")
    v.close()

    normed_two = v.normed_two
    corners_swapped = swap_tree(grid, v.gate_up_corners)
    columns_swapped = swap_tree(grid, (v.near_column, v.far_column))
    v.down_moved[2] = grid.shift(v.down_chip, "z", 2)
    near, far = every[:middle_plane], every[middle_plane:]
    gate_up_full = assemble(
        grid,
        plane_pieces(near, v.near_column, v.near_sides, {})
        + plane_pieces(far, v.far_column, v.far_sides, {})
        + corner_pieces(every, v.gate_up_corners),
        plane_pieces(near, columns_swapped[0], v.near_sides_swapped, {})
        + plane_pieces(far, columns_swapped[1], v.far_sides_swapped, {})
        + corner_pieces(every, corners_swapped),
    )
    v.hidden, v.slope, v.lift = feed(normed_two, gate_up_full)
    v.drop("near_column", "far_column", "near_sides", "far_sides", "gate_up_corners", "normed_two")
    v.drop("near_sides_swapped", "far_sides_swapped")
    v.close()

    hidden, slope, lift = v.hidden, v.slope, v.lift
    v.down_line = [v.down_chip, *[v.down_moved[hops] for hops in grid.hops("z")]]
    v.down_swapped = swap_tree(grid, v.down_line)
    v.down_parts = outer(grad_feed, hidden, down_rows)
    v.drop("down_chip", "down_moved", "hidden", "slope", "lift")
    v.close()

    slots = [(axis, hops) for axis in "zyx" for hops in range(size[axis])]
    numbers = jnp.stack([grid.ahead(axis, hops) for axis, hops in slots]).astype(jnp.int32)

    def here(axis, hops):
        return Place(slots.index((axis, hops)))

    def in_planes(pair):
        return [
            part.reshape(-1, size["y"], size["x"], *part.shape[-2:]) for part in pair
        ]

    v.down_terms = swapped(grid, in_planes(v.down_parts))
    down_full = assemble(
        grid, line_pieces(v.down_line, down_places), line_pieces(v.down_swapped, down_places)
    )

    def feed_part(half, total):
        *pair, total = feed_backward(
            grad_feed, down_full, slope, lift, normed_two, gate_up_full, total, half, gate_rows
        )
        return pair, total

    v.even_parts, v.total = feed_part(0, None)
    v.drop("down_line", "down_swapped", "down_parts")
    v.close()

    merge = Merge(grid, numbers)
    down_one = line(merge, here, [(v.down_terms, every)], 1, lead=2)
    made = merge.run()
    v.down_moved = [Source(down_one(made))]
    v.even = swapped(grid, in_planes(v.even_parts))
    v.odd_parts, v.total = feed_part(1, v.total)
    v.drop("even_parts")
    v.close()

    merge = Merge(grid, numbers)
    even_corners = corners(merge, here, v.even)
    down_three = line(merge, here, [(v.down_terms, every)], 3, lead=2)
    made = merge.run()
    v.even_corners = even_corners(made)
    v.down_moved.append(Source(down_three(made)))
    v.odd = swapped(grid, in_planes(v.odd_parts))
    *v.out_parts, v.grad_context, v.grad_middle, v.gain_two_part = project_backward(
        v.total, middle, out_grad, gain_two, context, out_full, out_rows
    )
    v.drop("odd_parts", "total")
    v.close()

    low, high = halves_of(v.down_terms)
    grad_context, grad_middle, gain_two_part = v.grad_context, v.grad_middle, v.gain_two_part
    v.drop("grad_context", "grad_middle", "gain_two_part")
    merge = Merge(grid, numbers)
    even_sides = sides(merge, here, v.even, v.even_corners)
    down_two = line(merge, here, [(v.down_terms, every)], 2, rows=low, lead=2)
    made = merge.run()
    v.even = even_sides(made)
    v.down_moved.append(Source(down_two(made)))
    v.out_terms = swapped(grid, in_planes(v.out_parts))
    v.gain_terms = []

    def backward_part(part, rows, total):
        *v.rows, v.total, terms_q, terms_k = attention_backward(
            *parts[part],
            grad_context,
            tables,
            gain_query,
            gain_key,
            normed_one,
            qkv_full,
            total,
            rows,
            part * heads_of,
            qkv_rows,
        )
        v.gain_terms = v.gain_terms + [(terms_q, terms_k)]

    backward_part(0, [], None)
    v.drop("out_parts", "even_corners")
    v.close()

    merge = Merge(grid, numbers)
    odd_corners = corners(merge, here, v.odd)
    out_corners = corners(merge, here, v.out_terms)
    down_two = line(merge, here, [(v.down_terms, every)], 2, rows=high, lead=2)
    down_own = line(merge, here, [(v.down_terms, every)], 0, lead=2)
    made = merge.run()
    v.odd_corners = odd_corners(made)
    v.out_corners = out_corners(made)
    v.down_moved += [Source(down_two(made), high[0]), Source(down_own(made))]
    backward_part(1, v.rows, v.total)
    v.drop("down_terms")
    v.close()

    merge = Merge(grid, numbers)
    odd_sides = sides(merge, here, v.odd, v.odd_corners)
    down_corners = corners(merge, here, v.down_moved, lead=0)
    made = merge.run()
    v.odd = odd_sides(made)
    v.down_corners = down_corners(made)
    v.first = swapped(grid, in_planes(v.rows[:2]))
    backward_part(2, v.rows[2:], v.total)
    v.drop("odd_corners")
    v.close()

    gate_up_groups = [(v.even, (0, 2)), (v.odd, (1, 3))]
    merge = Merge(grid, numbers)
    out_sides = sides(merge, here, v.out_terms, v.out_corners)
    down_sides = sides(merge, here, v.down_moved, v.down_corners, lead=0)
    gate_up_lines = [line(merge, here, gate_up_groups, hops) for hops in (1, 0)]
    made = merge.run()
    v.out_terms = out_sides(made)
    v.down_terms = down_sides(made)
    v.gate_up_moved = [go(made) for go in gate_up_lines]
    backward_part(3, v.rows, v.total)
    v.drop("out_corners", "down_moved", "down_corners")
    v.close()

    gate_up_groups = [(v.even, (0, 2)), (v.odd, (1, 3))]
    v.last = swapped(grid, in_planes(v.rows))
    merge = Merge(grid, numbers)
    first_corners = corners(merge, here, v.first)
    gate_up_three = line(merge, here, gate_up_groups, 3)
    made = merge.run()
    v.first_corners = first_corners(made)
    v.gate_up_moved.append(gate_up_three(made))
    grad_block, gain_one_terms = norm_backward(activations, scale_one, gain_one, v.total)
    gains_part = jnp.concatenate(
        [
            jnp.sum(gain_one_terms, axis=0, keepdims=True),
            gain_two_part,
            sum(terms for terms, _ in v.gain_terms),
            sum(terms for _, terms in v.gain_terms),
        ],
        axis=1,
    )
    v.input_grad = grad_middle + grad_block
    v.gains_part = gains_part
    v.drop("rows", "total", "gain_terms")
    v.close()

    gate_up_groups = [(v.even, (0, 2)), (v.odd, (1, 3))]
    merge = Merge(grid, numbers)
    last_corners = corners(merge, here, v.last)
    first_sides = sides(merge, here, v.first, v.first_corners)
    gate_up_two = line(merge, here, gate_up_groups, 2)
    made = merge.run()
    v.last_corners = last_corners(made)
    v.first = first_sides(made)
    v.gate_up_moved.append(gate_up_two(made))
    v.gains_part = small_sum(grid, v.gains_part, "c")
    v.layer_output = finish(hidden, down_full, middle)
    v.drop("even", "odd", "first_corners")
    v.close()

    merge = Merge(grid, numbers)
    last_sides = sides(merge, here, v.last, v.last_corners)
    out_lines = [line(merge, here, [(v.out_terms, every)], hops) for hops in range(size["z"])]
    made = merge.run()
    v.last = last_sides(made)
    v.out_moved = [go(made) for go in out_lines]
    v.gate_up_new = adamw(
        gate_up_weight, gate_up_first, gate_up_second, total_of(*v.gate_up_moved), 0.06, 0.1
    )
    down_total = total_of(*[term.array for term in v.down_terms])
    v.down_new = adamw(down_weight, down_first, down_second, down_total, 0.04, 0.1)
    v.drop("last_corners", "gate_up_moved", "down_terms", "out_terms")
    v.close()

    gains_total = small_sum(grid, v.gains_part, "z")
    v.last = after_tree(v.last, gains_total)
    qkv_groups = [(v.first, (0,)), (v.last, (1, 2, 3))]
    merge = Merge(grid, numbers)
    qkv_lines = [line(merge, here, qkv_groups, hops) for hops in range(size["z"])]
    made = merge.run()
    qkv_total = total_of(*[go(made) for go in qkv_lines])
    out_new = adamw(out_weight, out_first, out_second, total_of(*v.out_moved), 0.25, 0.1)
    gains_total = small_sum(grid, gains_total, "xy")
    gains_total = lax.dynamic_slice(gains_total, (0, gain_start), (1, gain_count))[0]

    return (
        v.layer_output,
        v.input_grad,
        *adamw(qkv_weight, qkv_first, qkv_second, qkv_total, 0.06, 0.1),
        *out_new,
        *v.gate_up_new,
        *v.down_new,
        *adamw(norm_gains, gains_first, gains_second, gains_total, 0.3, 0.0),
    )


def solution(mesh):
    return jax.shard_map(
        functools.partial(per_device, Grid(mesh.shape["dp"])),
        mesh=mesh,
        in_specs=(
            P("dp", None),
            P("dp", None),
            P("dp", None),
            P("dp", None),
            P("dp", None),
            P("dp", None),
            P("dp", None),
            P("dp", None),
            P("dp", None),
            P("dp", None),
            P("dp", None),
            P("dp", None),
            P("dp", None),
            P("dp", None),
            P("dp", None),
            P("dp"),
            P("dp"),
            P("dp"),
        ),
        out_specs=(
            P("dp", None),
            P("dp", None),
            P("dp", None),
            P("dp", None),
            P("dp", None),
            P("dp", None),
            P("dp", None),
            P("dp", None),
            P("dp", None),
            P("dp", None),
            P("dp", None),
            P("dp", None),
            P("dp", None),
            P("dp", None),
            P("dp"),
            P("dp"),
            P("dp"),
        ),
        check_vma=False,
    )
```

```python
import functools
import itertools
import math

import jax
import jax.numpy as jnp
from jax import lax
from jax.experimental import pallas as pl
from jax.experimental.pallas import tpu as pltpu
from jax.sharding import PartitionSpec as P

D = 1024
QUERY_HEADS = 16
KEY_VALUE_HEADS = 8
HEAD_WIDTH = 128
FF = 3072
STEP = 10


NORM_EPS = 1e-06
ROPE_BASE = 1000000.0
BETA_ONE = 0.9
BETA_TWO = 0.95
ADAM_EPS = 1e-08


def contract_last(left_side, right_side):
    return lax.dot_general(
        left_side, right_side, (((1,), (1,)), ((), ())), preferred_element_type=jnp.float32
    )


def contract_first(left_side, right_side):
    return lax.dot_general(
        left_side, right_side, (((0,), (0,)), ((), ())), preferred_element_type=jnp.float32
    )


def plain_product(left_side, right_side):
    return jnp.dot(left_side, right_side, preferred_element_type=jnp.float32)


def rms_scale(values):
    return lax.rsqrt(jnp.mean(values * values, axis=-1, keepdims=True) + NORM_EPS)


class Grid:
    def __init__(self, count):
        chips = count // 2
        flat = 2 if chips <= 16 else 4
        self.size = {"z": chips // (flat * flat), "y": flat, "x": flat, "c": 2}
        self.step = {"z": 2 * flat * flat, "y": 2 * flat, "x": 2, "c": 1}
        self.count = count

    def at(self, axis):
        return (lax.axis_index("dp") // self.step[axis]) % self.size[axis]

    def ahead(self, axis, hops):
        return (self.at(axis) + hops) % self.size[axis]

    def hops(self, axis):
        return range(1, self.size[axis])

    def shift(self, value, axis, hops):
        size, step = self.size[axis], self.step[axis]
        pairs = []
        for device in range(self.count):
            here = (device // step) % size
            pairs.append((device, device + ((here + hops) % size - here) * step))
        return lax.ppermute(value, "dp", pairs)


def after(value, *others):
    return lax.optimization_barrier((value, *jax.tree.leaves(others)))[0]


GROUP = QUERY_HEADS // KEY_VALUE_HEADS
SCORE_SCALE = HEAD_WIDTH ** (-0.5)
EXP2_SCALE = SCORE_SCALE * math.log2(math.e)
VMEM_BYTES = 60 * 1024 * 1024
VMEM_LESS = 50 * 1024 * 1024
VMEM_OF = {name: 46 * 1024 * 1024 for name in ("finish", "outer", "project")}


def norm_backward(values, scale_rows, gain, grad_out):
    scaled = gain * grad_out
    grad_in = scale_rows * scaled - values * scale_rows**3 * jnp.mean(
        scaled * values, axis=-1, keepdims=True
    )
    return (grad_in, grad_out * values * scale_rows)


def z_pieces(grid, shard, chained, *dependencies):
    moved = [shard]
    for hops in grid.hops("z"):
        moved.append(grid.shift(after(shard, *dependencies) if dependencies else shard, "z", hops))
        if chained:
            dependencies = (moved[-1],)
    return moved


def swap_tree(grid, buffers):
    return jax.tree.map(lambda buffer: grid.shift(buffer, "c", 1), buffers)


def swap_together(grid, buffers):
    leaves, shape = jax.tree.flatten(buffers)
    moved = grid.shift(jnp.concatenate(leaves, axis=0), "c", 1)
    starts = itertools.accumulate([0] + [leaf.shape[0] for leaf in leaves])
    return jax.tree.unflatten(
        shape, [Part(moved, start, leaf.shape[0]) for start, leaf in zip(starts, leaves)]
    )


@jax.tree_util.register_pytree_node_class
class Part:
    def __init__(self, array, start, count):
        self.array, self.start, self.count = array, start, count

    def tree_flatten(self):
        return (self.array,), (self.start, self.count)

    @classmethod
    def tree_unflatten(cls, held, leaves):
        return cls(*leaves, *held)


def plane_sides(grid, column, *dependencies):
    sent = after(column, *dependencies) if dependencies else column
    from_x = {hops: grid.shift(sent, "x", hops) for hops in grid.hops("x")}
    from_y = {hops: grid.shift(sent, "y", hops) for hops in grid.hops("y")}
    return from_x, from_y


def plane_corners(grid, sides, *dependencies, halved=True, cut_at=None):
    from_x, from_y = sides
    half = from_x[1].shape[0] // 2 if cut_at is None else cut_at
    corners = {}
    for j in from_x:
        for l in from_y:
            first, second = from_x[j], from_y[l]
            if halved:
                first, second = first[:half], second[half:]
            if dependencies:
                first, second = after(first, *dependencies), after(second, *dependencies)
            corners[j, l] = (grid.shift(first, "y", l), grid.shift(second, "x", j))
    return corners


def corner_pieces(planes, corners):
    half = len(planes) // 2
    pieces = []
    for (j, l), (first, second) in corners.items():
        pieces.append((first, [{"z": hops, "x": j, "y": l} for hops in planes[:half]]))
        pieces.append((second, [{"z": hops, "x": j, "y": l} for hops in planes[half:]]))
    return pieces


def plane_pieces(planes, column, sides, corners):
    from_x, from_y = sides
    pieces = [(column, [{"z": hops} for hops in planes])]
    pieces += [(from_x[j], [{"z": hops, "x": j} for hops in planes]) for j in from_x]
    pieces += [(from_y[l], [{"z": hops, "y": l} for hops in planes]) for l in from_y]
    return pieces + corner_pieces(planes, corners)


def after_tree(tree, *dependencies):
    leaves, shape = jax.tree.flatten(tree)
    tied = lax.optimization_barrier((*leaves, *flat(dependencies)))
    return jax.tree.unflatten(shape, tied[: len(leaves)])


def flat(*groups):
    return [leaf for leaf in jax.tree.leaves(groups)]


def rows_of_gains(gains, width):
    rows = -(-gains.shape[1] // width)
    block = jnp.pad(gains, ((0, 0), (0, rows * width - gains.shape[1]))).reshape(rows, width)
    return jnp.pad(block, ((0, 16 - rows), (0, 0)))


def chip_plane(block, sides_received, corners_received, rows):
    from_x, from_y = sides_received
    blocks = [block, *from_x.values(), *from_y.values()]
    shards = [part[:rows] for part in blocks]
    below = [part[rows:] for part in blocks]
    places = [{}] + [{"x": j} for j in from_x] + [{"y": l} for l in from_y]
    for (j, l), (shard, rest) in corners_received.items():
        shards.append(shard)
        below.append(rest)
        places.append({"x": j, "y": l})
    return jnp.stack(shards), sum(below), places


def arrivals(grid, places_of, pieces, held, came):
    copies = []
    for which, first, places in places_of:
        for slot, place in enumerate(places, first):
            index = 0
            for axis in ("z", "y", "x", "c"):
                size = grid.size[axis]
                index = index + (grid.at(axis) + size - place.get(axis, 0)) % size * grid.step[axis]
            copies.append(
                pltpu.make_async_copy(pieces[which].at[slot], held.at[index], came.at[index])
            )
    return copies


def arrived(held, device, came):
    return pltpu.make_async_copy(held.at[device], held.at[device], came.at[device])


def leaving(held, device, out, went):
    return pltpu.make_async_copy(held.at[device], out.at[device], went.at[device])


def assemble_kernel(grid, places_of, *refs):
    pieces, (out, held, came, went) = refs[:-4], refs[-4:]
    for copy in arrivals(grid, places_of, pieces, held, came):
        copy.start()
    for device in range(grid.count):
        arrived(held, device, came).wait()
        leaving(held, device, out, went).start()
    for device in range(grid.count):
        leaving(held, device, out, went).wait()


def line_pieces(line, places):
    return [
        (buffer, [dict(place, z=hops) for place in places]) for hops, buffer in enumerate(line)
    ]


def gather_plan(own_pieces, swapped_pieces):
    pieces = own_pieces + [
        (buffer, [dict(place, c=1) for place in places]) for buffer, places in swapped_pieces
    ]
    arrays, places_of = [], []
    for buffer, places in pieces:
        array, first = (buffer.array, buffer.start) if isinstance(buffer, Part) else (buffer, 0)
        which = next((at for at, known in enumerate(arrays) if known is array), len(arrays))
        if which == len(arrays):
            arrays.append(array)
        places_of.append((which, first, places))
    return arrays, places_of


def assemble(grid, own_pieces, swapped_pieces):
    arrays, places_of = gather_plan(own_pieces, swapped_pieces)
    rows, width = arrays[0].shape[1:]
    dims = (grid.count, rows, width)
    gathered = pl.pallas_call(
        functools.partial(assemble_kernel, grid, places_of),
        out_shape=jax.ShapeDtypeStruct(dims, jnp.bfloat16),
        in_specs=[pl.BlockSpec(memory_space=pl.ANY)] * len(arrays),
        out_specs=pl.BlockSpec(memory_space=pl.ANY),
        scratch_shapes=[
            pltpu.VMEM(dims, jnp.bfloat16),
            pltpu.SemaphoreType.DMA((grid.count,)),
            pltpu.SemaphoreType.DMA((grid.count,)),
        ],
        compiler_params=pltpu.CompilerParams(vmem_limit_bytes=VMEM_BYTES),
        cost_estimate=LITTLE,
        name="assemble",
    )(*arrays)
    return gathered.reshape(grid.count * rows, width)


@jax.tree_util.register_pytree_node_class
class Source:
    def __init__(self, array, first=0):
        self.array, self.first = array, first

    def tree_flatten(self):
        return (self.array,), self.first

    @classmethod
    def tree_unflatten(cls, first, leaves):
        return cls(*leaves, first)


class Place:
    def __init__(self, slot, table=None):
        self.slot, self.table = slot, table

    def of(self, numbers):
        here = numbers[self.slot]
        if self.table is None:
            return here
        return sum(jnp.where(here == at, entry, 0) for at, entry in enumerate(self.table))

    def __eq__(self, other):
        return isinstance(other, Place) and (self.slot, self.table) == (other.slot, other.table)

    def __hash__(self):
        return hash((self.slot, self.table))


class Merge:
    STRIP = 16
    STEPS = 2

    def __init__(self, grid, numbers):
        self.grid, self.numbers = grid, numbers
        self.inputs, self.outputs, self.keys = [], [], {}

    def cut(self, array, places):
        key = (id(array), places)
        if key not in self.keys:
            self.keys[key] = len(self.inputs)
            self.inputs.append((array, places))
        return self.keys[key]

    def terms(self, sources, places, low, high):
        found = []
        for source in sources:
            first = source.first
            if first <= low and high <= first + source.array.shape[-2]:
                found.append((self.cut(source.array, places), low - first, high - first))
        return found

    def add(self, *options, chosen=None):
        self.outputs.append((options, chosen))
        return len(self.outputs) - 1

    def shape(self, options):
        array, places = self.inputs[options[0][0][0][0]]
        lead = [size for size, place in zip(array.shape, places) if place is None]
        rows = sum(segment[0][2] - segment[0][1] for segment in options[0])
        return (*lead, rows, array.shape[-1])

    def run(self):
        edges = [
            edge
            for options, _ in self.outputs
            for segments in options
            for segment in segments
            for term in segment
            for edge in term[1:]
        ]
        if any(edge % self.STRIP for edge in edges):
            return self.run_plain()
        shapes = [self.shape(options) for options, _ in self.outputs]
        def spec(array, places):
            block = [
                None if place is not None else size for size, place in zip(array.shape, places)
            ]
            return pl.BlockSpec(
                (*block, array.shape[-2], array.shape[-1] // self.STEPS),
                lambda step, held: (
                    *[0 if place is None else place.of(held) for place in places], 0, step
                ),
            )

        return pl.pallas_call(
            self.kernel,
            grid_spec=pltpu.PrefetchScalarGridSpec(
                num_scalar_prefetch=1,
                grid=(self.STEPS,),
                in_specs=[spec(*pair) for pair in self.inputs],
                out_specs=[
                    pl.BlockSpec(
                        (*dims[:-1], dims[-1] // self.STEPS),
                        lambda step, held, axes=len(dims): (0,) * (axes - 1) + (step,),
                    )
                    for dims in shapes
                ],
            ),
            out_shape=[jax.ShapeDtypeStruct(dims, jnp.bfloat16) for dims in shapes],
            compiler_params=pltpu.CompilerParams(vmem_limit_bytes=VMEM_LESS),
            cost_estimate=LITTLE,
            name="merge",
        )(self.numbers, *[array for array, _ in self.inputs])

    def kernel(self, held, *refs):
        inputs, outputs = refs[: len(self.inputs)], refs[len(self.inputs) :]
        for out, (options, chosen) in zip(outputs, self.outputs):
            for number, segments in enumerate(options):
                write = functools.partial(self.write, out, segments, inputs)
                if chosen is None:
                    write()
                else:
                    pl.when(chosen.of(held) == number)(write)

    def write(self, out, segments, inputs):
        start = 0
        for segment in segments:
            count = segment[0][2] - segment[0][1]
            strips = count // self.STRIP
            unroll = max(part for part in range(1, 9) if strips % part == 0)
            for lead in itertools.product(*[range(size) for size in out.shape[:-2]]):

                @pl.loop(0, strips, unroll=unroll)
                def _(strip, start=start, lead=lead, segment=segment):
                    def rows(first):
                        at = pl.multiple_of(first + strip * self.STRIP, self.STRIP)
                        return (*lead, pl.ds(at, self.STRIP), slice(None))

                    added = sum(inputs[k][rows(low)].astype(jnp.float32) for k, low, _ in segment)
                    out[rows(start)] = added.astype(jnp.bfloat16)

            start += count

    def run_plain(self):
        def part(term):
            array, places = self.inputs[term[0]]
            axis = 0
            for place in places:
                if place is None:
                    axis += 1
                else:
                    array = lax.dynamic_index_in_dim(
                        array, place.of(self.numbers), axis, keepdims=False
                    )
            return lax.slice_in_dim(array, term[1], term[2], axis=-2 + array.ndim)

        results = []
        for options, chosen in self.outputs:
            made = []
            for segments in options:
                sums = [
                    sum(part(term).astype(jnp.float32) for term in segment).astype(jnp.bfloat16)
                    for segment in segments
                ]
                made.append(jnp.concatenate(sums, axis=-2) if len(sums) > 1 else sums[0])
            results.append(made[0])
            for number in range(1, len(made)):
                results[-1] = jnp.where(chosen.of(self.numbers) == number, made[number], results[-1])
        return results


def swapped(grid, kept_and_sent):
    kept, sent = kept_and_sent
    return [Source(kept), Source(grid.shift(sent, "c", 1))]


def halves_of(sources):
    rows = sources[0].array.shape[-2]
    return (0, rows // 2), (rows // 2, rows)


def corners(merge, here, sources, lead=1):
    low, high = halves_of(sources)
    grid, whole_axes = merge.grid, (None,) * lead
    slots = {}
    for j in grid.hops("x"):
        for l in grid.hops("y"):
            place = (*whole_axes, here("y", l), here("x", j))
            slots[j, l] = (
                merge.add([merge.terms(sources, place, *low)]),
                merge.add([merge.terms(sources, place, *high)]),
            )

    def go(made):
        return {
            (j, l): (grid.shift(made[first], "x", j), grid.shift(made[second], "y", l))
            for (j, l), (first, second) in slots.items()
        }

    return go


def sides(merge, here, sources, crossed, lead=1):
    low, high = halves_of(sources)
    grid, whole_axes = merge.grid, (None,) * lead
    own_place = (*whole_axes, here("y", 0), here("x", 0))
    bare = (None,) * lead
    own = merge.add([merge.terms(sources, own_place, *half) for half in (low, high)])
    to_x, to_y = {}, {}
    for j in grid.hops("x"):
        place = (*whole_axes, here("y", 0), here("x", j))
        received = [Source(crossed[j, l][1], high[0]) for l in grid.hops("y")]
        to_x[j] = merge.add(
            [
                merge.terms(sources, place, *low),
                merge.terms(sources, place, *high) + merge.terms(received, bare, *high),
            ]
        )
    for l in grid.hops("y"):
        place = (*whole_axes, here("y", l), here("x", 0))
        received = [Source(crossed[j, l][0]) for j in grid.hops("x")]
        to_y[l] = merge.add(
            [
                merge.terms(sources, place, *low) + merge.terms(received, bare, *low),
                merge.terms(sources, place, *high),
            ]
        )

    def go(made):
        terms = [made[own]]
        terms += [grid.shift(made[to_x[j]], "x", j) for j in to_x]
        terms += [grid.shift(made[to_y[l]], "y", l) for l in to_y]
        return [Source(term) for term in terms]

    return go


def line(merge, here, groups, hops, rows=None, lead=0):
    grid = merge.grid
    plane = here("z", hops)
    owner = {
        number: (group, at)
        for group, (_, planes) in enumerate(groups)
        for at, number in enumerate(planes)
    }
    numbers = range(grid.size["z"])
    options = []
    for group, (sources, _) in enumerate(groups):
        index = Place(
            plane.slot, tuple(owner[n][1] if owner[n][0] == group else 0 for n in numbers)
        )
        place = (index, *(None,) * lead)
        parts = halves_of(sources) if rows is None else (rows,)
        options.append([merge.terms(sources, place, *part) for part in parts])
    chosen = Place(plane.slot, tuple(owner[n][0] for n in numbers)) if len(groups) > 1 else None
    slot = merge.add(*options, chosen=chosen)
    return lambda made: grid.shift(made[slot], "z", hops) if hops else made[slot]


def total_of(*terms):
    return sum(term.astype(jnp.float32) for term in terms)


class Steps:
    def __init__(self, **live):
        self.__dict__.update(live)

    def close(self):
        self.__dict__.update(after_tree(dict(self.__dict__)))

    def drop(self, *names):
        for name in names:
            del self.__dict__[name]


def small_sum(grid, value, axes):
    for axis in axes:
        value = value + sum(grid.shift(value, axis, hops) for hops in grid.hops(axis))
    return value


LITTLE = pl.CostEstimate(flops=1, bytes_accessed=1, transcendentals=0)


def whole(array):
    return pl.BlockSpec(array.shape, lambda *k: (0,) * array.ndim)


def in_vmem(array):
    return pl.BlockSpec(memory_space=pltpu.VMEM)


def kernel_call(
    body, name, grid, in_specs, out_shape, out_specs, scratch=(), aliases=None, vmem=VMEM_BYTES
):
    return pl.pallas_call(
        body,
        grid=grid,
        in_specs=in_specs,
        out_shape=out_shape,
        out_specs=out_specs,
        scratch_shapes=scratch,
        input_output_aliases=aliases or {},
        compiler_params=pltpu.CompilerParams(vmem_limit_bytes=VMEM_OF.get(name, vmem)),
        cost_estimate=LITTLE,
        name=name,
    )


def shape_of(dims, dtype):
    return jax.ShapeDtypeStruct(dims, dtype)


TRIO = (GROUP + 1) * HEAD_WIDTH


def lanes_of(head):
    return slice(head * HEAD_WIDTH, (head + 1) * HEAD_WIDTH)


def turned(values):
    return pltpu.roll(values, HEAD_WIDTH // 2, 1)


def stacked(values, rows, heads=GROUP):
    return jnp.concatenate([values[rows, lanes_of(g)] for g in range(heads)], axis=0)


def query_blocks(micro_rows):
    half = micro_rows // 2
    return [(0, half), (half, micro_rows)]


def powers_of(queries, keys, bias):
    return jnp.exp2(contract_last(queries, keys) * EXP2_SCALE + bias)


def group_bias(bias, micro, begin, end):
    return jnp.concatenate([bias[micro, begin:end, :end]] * GROUP, axis=0)


def attention_kernel(normed, wq, wk, wv, cosine, sine, bias, gain_q, gain_k, *outputs):
    norms, scales, turns, value, context, held = outputs[-6:]
    held[:, : GROUP * HEAD_WIDTH] = contract_last(normed[...], wq[...])
    both = contract_last(normed[...], jnp.concatenate([wk[...], wv[...]], axis=0))
    held[:, GROUP * HEAD_WIDTH :] = both[:, :HEAD_WIDTH]
    value[...] = both[:, HEAD_WIDTH:].astype(jnp.bfloat16)
    micro_count, micro_rows, _ = bias.shape
    for micro in range(micro_count):
        start = micro * micro_rows
        rows = slice(start, start + micro_rows)
        for head in range(GROUP + 1):
            raw = held[rows, lanes_of(head)]
            scale = lax.rsqrt(jnp.mean(raw * raw, axis=-1, keepdims=True) + NORM_EPS)
            scale = jnp.broadcast_to(scale, raw.shape)
            normal = raw * scale
            gained = normal * (gain_q[...] if head < GROUP else gain_k[...])
            norms[rows, lanes_of(head)] = normal.astype(jnp.bfloat16)
            scales[rows, lanes_of(head)] = scale.astype(jnp.bfloat16)
            turns[rows, lanes_of(head)] = (
                gained * cosine[rows, :] + turned(gained) * sine[rows, :]
            ).astype(jnp.bfloat16)
        keys = turns[rows, lanes_of(GROUP)]
        for begin, end in query_blocks(micro_rows):
            block = slice(start + begin, start + end)
            count = end - begin
            powers = powers_of(
                stacked(turns, block), keys[:end], group_bias(bias, micro, begin, end)
            )
            inverse = 1.0 / jnp.sum(powers, axis=-1, keepdims=True)
            probs = (powers * inverse).astype(jnp.bfloat16)
            mixed = plain_product(probs, value[start : start + end, :]).astype(jnp.bfloat16)
            for g in range(GROUP):
                context[block, lanes_of(g)] = mixed[g * count : (g + 1) * count, :]


def with_turn(values):
    return jnp.concatenate([values, turned(values)], axis=1)


def head_backward(normal, scale, gain, grad, cos, sin):
    normal, scale = normal.astype(jnp.float32), scale.astype(jnp.float32)
    grad_normed = (grad[:, :HEAD_WIDTH] * cos - grad[:, HEAD_WIDTH:] * sin) * SCORE_SCALE
    scaled = gain * grad_normed
    terms = grad_normed * normal
    mean = jnp.mean(scaled * normal, axis=-1, keepdims=True)
    grad_raw = scale * (scaled - normal * mean)
    return grad_raw.astype(jnp.bfloat16), jnp.sum(terms, axis=0, keepdims=True)


def put_by_core(rows_per_device, result, part, at, plane, kept, sent, sems, sem):
    rows = result.shape[0]
    if rows >= 2 * rows_per_device:
        chips = rows // (2 * rows_per_device)
        part[0], part[1] = by_core(rows_per_device, result)
        stretch = pl.ds(at * chips, chips)
        return [
            pltpu.make_async_copy(part.at[0], kept.at[plane, stretch], sems.at[sem]),
            pltpu.make_async_copy(part.at[1], sent.at[plane, stretch], sems.at[sem + 1]),
        ]
    part[0, 0] = result
    mine = (at + lax.axis_index("dp")) % 2 == 0
    return [
        Either(
            mine,
            pltpu.make_async_copy(part.at[0, 0], kept.at[plane, at // 2], sems.at[sem]),
            pltpu.make_async_copy(part.at[0, 0], sent.at[plane, at // 2], sems.at[sem + 1]),
        )
    ]


class Either:
    def __init__(self, first_one, first, second):
        self.first_one, self.first, self.second = first_one, first, second

    def start(self):
        pl.when(self.first_one)(self.first.start)
        pl.when(jnp.logical_not(self.first_one))(self.second.start)

    def wait(self):
        pl.when(self.first_one)(self.first.wait)
        pl.when(jnp.logical_not(self.first_one))(self.second.wait)


def attention_backward_kernel(
    first, rows_per_device, held, norms, scales, turns, value, grad_context, cosine, sine, bias,
    gain_q, gain_k, normed, wq, wk, wv, *others,
):
    grad_raw_all, part_q, part_k, part_v, sems = others[-5:]
    kv_kept, kv_sent, total, terms_q, terms_k = others[-10:-5]

    @pl.when(pl.program_id(0) == 0)
    def _():
        terms_q[...] = jnp.zeros_like(terms_q)
        terms_k[...] = jnp.zeros_like(terms_k)
        if held:
            total[...] = others[0][...]
        else:
            total[...] = jnp.zeros_like(total)

    micro_count, micro_rows, _ = bias.shape
    for micro in range(micro_count):
        start = micro * micro_rows
        rows = slice(start, start + micro_rows)
        keys = turns[rows, lanes_of(GROUP)]
        both_keys = with_turn(keys)
        grad_values, grad_keys = 0.0, 0.0
        for begin, end in query_blocks(micro_rows):
            block = slice(start + begin, start + end)
            count = end - begin
            cos, sin = cosine[block, :], sine[block, :]
            queries = stacked(turns, block)
            powers = powers_of(queries, keys[:end], group_bias(bias, micro, begin, end))
            probs = powers * (1.0 / jnp.sum(powers, axis=-1, keepdims=True))
            grads = stacked(grad_context, block)
            grad_probs = contract_last(grads, value[start : start + end, :])
            weighted = probs * grad_probs
            centre = jnp.sum(weighted, axis=-1, keepdims=True)
            grad_scores = (weighted - probs * centre).astype(jnp.bfloat16)
            pad = ((0, micro_rows - end), (0, 0))
            grad_values += jnp.pad(contract_first(probs.astype(jnp.bfloat16), grads), pad)
            grad_keys += jnp.pad(contract_first(grad_scores, with_turn(queries)), pad)
            grad_queries = plain_product(grad_scores, both_keys[:end])
            for g in range(GROUP):
                grad_raw, terms = head_backward(
                    norms[block, lanes_of(g)],
                    scales[block, lanes_of(g)],
                    gain_q[...],
                    grad_queries[g * count : (g + 1) * count, :],
                    cos,
                    sin,
                )
                grad_raw_all[block, lanes_of(g)] = grad_raw
                terms_q[...] += terms
        grad_raw_all[rows, lanes_of(GROUP + 1)] = grad_values.astype(jnp.bfloat16)
        grad_raw, terms = head_backward(
            norms[rows, lanes_of(GROUP)],
            scales[rows, lanes_of(GROUP)],
            gain_k[...],
            grad_keys,
            cosine[rows, :],
            sine[rows, :],
        )
        grad_raw_all[rows, lanes_of(GROUP)] = grad_raw
        terms_k[...] += terms
    head = first + pl.program_id(0)
    half = KEY_VALUE_HEADS // 2
    queries_kept, queries_sent = (kv_kept, kv_sent) if first >= half else others[-12:-10]
    wide = GROUP * HEAD_WIDTH
    result = contract_first(grad_raw_all[...], normed[...]).astype(jnp.bfloat16)
    result_q, result_k, result_v = (
        result[:wide, :],
        result[wide : wide + HEAD_WIDTH, :],
        result[wide + HEAD_WIDTH :, :],
    )
    copies = [
        *put_by_core(
            rows_per_device, result_q, part_q, head % half, 0, queries_kept, queries_sent, sems, 0
        ),
        *put_by_core(rows_per_device, result_k, part_k, head, 1, kv_kept, kv_sent, sems, 2),
        *put_by_core(rows_per_device, result_v, part_v, head, 2, kv_kept, kv_sent, sems, 4),
    ]
    for copy in copies:
        copy.start()
    weights = jnp.concatenate([wq[...], wk[...], wv[...]], axis=0)
    total[...] += plain_product(grad_raw_all[...], weights)
    for copy in copies:
        copy.wait()


def by_core(rows_per_device, part):
    pairs = part.reshape(-1, 2, rows_per_device, part.shape[-1])
    here = lax.axis_index("dp") % 2 == 0
    first, second = pairs[:, 0], pairs[:, 1]
    return jnp.where(here, first, second), jnp.where(here, second, first)


def heads(rows, width, first=0):
    return pl.BlockSpec((rows, width), lambda k: (0, first + k))


def head_rows(heads_in, depth, first):
    return pl.BlockSpec((heads_in * HEAD_WIDTH, depth), lambda k: (first + k, 0))


def qkv_rows_of(depth, first):
    return [
        head_rows(GROUP, depth, first),
        head_rows(1, depth, QUERY_HEADS + first),
        head_rows(1, depth, QUERY_HEADS + KEY_VALUE_HEADS + first),
    ]


def attention(normed, qkv_full, tables, gain_q, gain_k, context, first, count):
    tokens, depth = normed.shape
    wide = GROUP * HEAD_WIDTH
    whole_context = shape_of((tokens, QUERY_HEADS * HEAD_WIDTH), jnp.bfloat16)
    held = [] if context is None else [context]
    return kernel_call(
        attention_kernel,
        "attention",
        (count,),
        [
            in_vmem(normed),
            *qkv_rows_of(depth, first),
            *[in_vmem(table) for table in tables],
            in_vmem(gain_q),
            in_vmem(gain_k),
            *[pl.BlockSpec(memory_space=pl.ANY)] * len(held),
        ],
        (
            shape_of((tokens, count * TRIO), jnp.bfloat16),
            shape_of((tokens, count * TRIO), jnp.bfloat16),
            shape_of((tokens, count * TRIO), jnp.bfloat16),
            shape_of((tokens, count * HEAD_WIDTH), jnp.bfloat16),
            whole_context,
        ),
        (
            heads(tokens, TRIO),
            heads(tokens, TRIO),
            heads(tokens, TRIO),
            heads(tokens, HEAD_WIDTH),
            heads(tokens, wide, first),
        ),
        scratch=[pltpu.VMEM((tokens, TRIO), jnp.float32)],
        aliases={9: 4} if held else None,
        vmem=VMEM_LESS,
    )(normed, qkv_full, qkv_full, qkv_full, *tables, gain_q, gain_k, *held)


def attention_backward(
    norms, scales, turns, value, grad_context, tables, gain_q, gain_k,
    normed, qkv_full, total, parts, first, rows_per_device,
):
    tokens, depth = normed.shape
    wide = GROUP * HEAD_WIDTH
    count = value.shape[1] // HEAD_WIDTH
    half = KEY_VALUE_HEADS // 2
    stretch = half * wide // (2 * rows_per_device)
    early = shape_of((1, stretch, rows_per_device, depth), jnp.bfloat16)
    late = shape_of((3, stretch, rows_per_device, depth), jnp.bfloat16)
    shapes = [late, late] if first >= half else [early, early, late, late]
    held = [] if total is None else [total, *parts]

    def part_scratch(rows):
        chips = max(rows // (2 * rows_per_device), 1)
        height = min(rows, rows_per_device)
        return pltpu.VMEM((2, chips, height, depth), jnp.bfloat16)

    anywhere = pl.BlockSpec(memory_space=pl.ANY)
    return kernel_call(
        functools.partial(attention_backward_kernel, first, rows_per_device, len(held)),
        "attention_backward",
        (count,),
        [
            heads(tokens, TRIO),
            heads(tokens, TRIO),
            heads(tokens, TRIO),
            heads(tokens, HEAD_WIDTH),
            heads(tokens, wide, first),
            *[in_vmem(table) for table in tables],
            in_vmem(gain_q),
            in_vmem(gain_k),
            in_vmem(normed),
            *qkv_rows_of(depth, first),
            *[in_vmem(total)] * min(len(held), 1),
            *[anywhere] * max(len(held) - 1, 0),
        ],
        (
            *shapes,
            shape_of((tokens, depth), jnp.float32),
            shape_of(gain_q.shape, jnp.float32),
            shape_of(gain_k.shape, jnp.float32),
        ),
        (*[anywhere] * len(shapes), in_vmem(normed), in_vmem(gain_q), in_vmem(gain_k)),
        scratch=[
            pltpu.VMEM((tokens, TRIO + HEAD_WIDTH), jnp.bfloat16),
            part_scratch(wide),
            part_scratch(HEAD_WIDTH),
            part_scratch(HEAD_WIDTH),
            pltpu.SemaphoreType.DMA((6,)),
        ],
        aliases={15 + slot: slot for slot in range(len(shapes))} if held else None,
        vmem=VMEM_LESS,
    )(
        norms, scales, turns, value, grad_context, *tables, gain_q, gain_k,
        normed, qkv_full, qkv_full, qkv_full, *held,
    )


ROW_TILE = 256
FF_TILE = 512
BACK_TILE = 384
STRIP = 64


def project_kernel(context, weight, residual, gain, middle, normed):
    middle[...] = residual[...] + contract_last(context[...], weight[...])

    @pl.loop(0, middle.shape[0] // STRIP)
    def _(strip):
        rows = pl.ds(pl.multiple_of(strip * STRIP, STRIP), STRIP)
        values = middle[rows, :]
        normed[rows, :] = (values * rms_scale(values) * gain[...]).astype(jnp.bfloat16)


def rows_of(array, tile):
    return pl.BlockSpec((tile, array.shape[1]), lambda k: (k, 0))


def project(context, weight, residual, gain):
    return kernel_call(
        project_kernel,
        "project",
        (residual.shape[0] // ROW_TILE,),
        [rows_of(context, ROW_TILE), whole(weight), rows_of(residual, ROW_TILE), whole(gain)],
        (shape_of(residual.shape, jnp.float32), shape_of(residual.shape, jnp.bfloat16)),
        (rows_of(residual, ROW_TILE), rows_of(residual, ROW_TILE)),
    )(context, weight, residual, gain)


def feed_kernel(grid, places_of, pieces_count, *refs):
    pieces, normed = refs[:pieces_count], refs[pieces_count]
    hidden, slope, lift, out, held, came, went = refs[pieces_count + 1 :]
    step = pl.program_id(0)
    rows = held.shape[1]
    tile = hidden.shape[1]
    each = tile // rows
    half = grid.count // 2

    @pl.when(step == 0)
    def _():
        for copy in arrivals(grid, places_of, pieces, held, came):
            copy.start()

    for number in range(each):
        for first in (0, half):
            device = first + step * each + number
            arrived(held, device, came).wait()
            leaving(held, device, out, went).start()
    weights = jnp.concatenate(
        [held[pl.ds(first + step * each, each)].reshape(tile, -1) for first in (0, half)], axis=0
    )
    both = contract_last(normed[...], weights)
    gate, upward = both[:, :tile], both[:, tile:]
    sigma = jax.nn.sigmoid(gate)
    lifted = gate * sigma
    lift[...] = lifted.astype(jnp.bfloat16)
    slope[...] = (upward * sigma * (1.0 + gate * (1.0 - sigma))).astype(jnp.bfloat16)
    hidden[...] = (lifted * upward).astype(jnp.bfloat16)

    @pl.when(step == pl.num_programs(0) - 1)
    def _():
        for device in range(grid.count):
            leaving(held, device, out, went).wait()


def columns_of(rows, tile, first=0):
    return pl.BlockSpec((rows, tile), lambda k: (0, first + k))


def gate_and_up(tile, depth, first=0):
    return pl.BlockSpec((2, tile, depth), lambda k: (0, first + k, 0))


def feed(grid, normed, own_pieces, swapped_pieces):
    arrays, places_of = gather_plan(own_pieces, swapped_pieces)
    tokens, depth = normed.shape
    rows = arrays[0].shape[1]
    columns = columns_of(tokens, BACK_TILE)
    anywhere = pl.BlockSpec(memory_space=pl.ANY)
    dims = (grid.count, rows, depth)
    hidden, slope, lift, weight = kernel_call(
        functools.partial(feed_kernel, grid, places_of, len(arrays)),
        "feed",
        (FF // BACK_TILE,),
        [*[anywhere] * len(arrays), whole(normed)],
        (
            shape_of((tokens, FF), jnp.bfloat16),
            shape_of((tokens, FF), jnp.bfloat16),
            shape_of((tokens, FF), jnp.bfloat16),
            shape_of(dims, jnp.bfloat16),
        ),
        (columns, columns, columns, anywhere),
        scratch=[
            pltpu.VMEM(dims, jnp.bfloat16),
            pltpu.SemaphoreType.DMA((grid.count,)),
            pltpu.SemaphoreType.DMA((grid.count,)),
        ],
    )(*arrays, normed)
    return hidden, slope, lift, weight.reshape(grid.count * rows, depth)


def finish_kernel(hidden, weight, residual, output):
    output[...] = residual[...] + contract_last(hidden[...], weight[...])


def finish(hidden, weight, residual):
    return kernel_call(
        finish_kernel,
        "finish",
        (residual.shape[0] // ROW_TILE,),
        [rows_of(hidden, ROW_TILE), whole(weight), rows_of(residual, ROW_TILE)],
        shape_of(residual.shape, jnp.float32),
        rows_of(residual, ROW_TILE),
    )(hidden, weight, residual)


def outer_kernel(rows_per_device, left, right, kept, sent, turned_left):
    @pl.when(pl.program_id(0) == 0)
    def _():
        turned_left[...] = left[...].T

    part = plain_product(turned_left[...], right[...]).astype(jnp.bfloat16)
    kept[...], sent[...] = by_core(rows_per_device, part)


def chip_columns(chips, rows, width):
    return pl.BlockSpec((chips, rows, width), lambda k: (0, 0, k))


def outer(left, right, rows_per_device):
    chips = left.shape[1] // (2 * rows_per_device)
    shape = shape_of((chips, rows_per_device, right.shape[1]), jnp.bfloat16)
    block = chip_columns(chips, rows_per_device, FF_TILE)
    return kernel_call(
        functools.partial(outer_kernel, rows_per_device),
        "outer",
        (right.shape[1] // FF_TILE,),
        [whole(left), columns_of(right.shape[0], FF_TILE)],
        (shape, shape),
        (block, block),
        scratch=[pltpu.VMEM((left.shape[1], left.shape[0]), jnp.bfloat16)],
    )(left, right)


def feed_backward_kernel(
    rows_per_device, grad_feed, down, slope, lift, normed, weights, *others
):
    kept, sent, total = others[-3:]

    @pl.when(pl.program_id(0) == 0)
    def _():
        total[...] = others[0][...] if len(others) > 3 else jnp.zeros_like(total)

    grad_hidden = plain_product(grad_feed[...], down[...])
    grads = jnp.concatenate(
        [
            (grad_hidden * slope[...].astype(jnp.float32)).astype(jnp.bfloat16),
            (grad_hidden * lift[...].astype(jnp.float32)).astype(jnp.bfloat16),
        ],
        axis=1,
    )
    tile = grad_hidden.shape[1]
    part = contract_first(grads, normed[...]).astype(jnp.bfloat16)
    for plane in range(2):
        kept[plane], sent[plane] = by_core(
            rows_per_device, part[plane * tile : (plane + 1) * tile, :]
        )
    total[...] += plain_product(grads, weights[...].reshape(2 * tile, -1))


def feed_backward(grad_feed, down, slope, lift, normed, weight, total, half, rows_per_device):
    tokens, depth = normed.shape
    tiles = FF // BACK_TILE
    count = tiles // 2
    first = half * count
    held = [] if total is None else [total]
    chips = BACK_TILE // (2 * rows_per_device)
    shape = shape_of((2, count * chips, rows_per_device, depth), jnp.bfloat16)
    block = pl.BlockSpec((2, chips, rows_per_device, depth), lambda k: (0, k, 0, 0))
    return kernel_call(
        functools.partial(feed_backward_kernel, rows_per_device),
        "feed_backward",
        (count,),
        [
            whole(grad_feed),
            columns_of(depth, BACK_TILE, first),
            columns_of(tokens, BACK_TILE, first),
            columns_of(tokens, BACK_TILE, first),
            whole(normed),
            gate_and_up(BACK_TILE, depth, first),
            *[whole(total) for total in held],
        ],
        (shape, shape, shape_of((tokens, depth), jnp.float32)),
        (block, block, pl.BlockSpec((tokens, depth), lambda k: (0, 0))),
    )(grad_feed, down, slope, lift, normed, weight.reshape(2, FF, depth), *held)


def project_backward_kernel(
    rows_per_device, grad_normed, middle, out_grad, gain, context, weight,
    kept, sent, grad_context, grad_middle, gain_terms, branch, turned_branch,
):
    step = pl.program_id(0)
    row_steps = branch.shape[0] // ROW_TILE

    @pl.when(step == 0)
    def _():
        gain_terms[...] = jnp.zeros_like(gain_terms)

    @pl.when(step < row_steps)
    def _():
        start = pl.multiple_of(step * ROW_TILE, ROW_TILE)

        @pl.loop(0, ROW_TILE // STRIP)
        def _(strip):
            rows = pl.ds(pl.multiple_of(strip * STRIP, STRIP), STRIP)
            values = middle[rows, :]
            grad, terms = norm_backward(values, rms_scale(values), gain[...], grad_normed[rows, :])
            grad = out_grad[rows, :] + grad
            grad_middle[rows, :] = grad
            branch[pl.ds(pl.multiple_of(start + strip * STRIP, STRIP), STRIP), :] = grad.astype(
                jnp.bfloat16
            )
            gain_terms[...] += jnp.sum(terms, axis=0, keepdims=True)

    @pl.when(step == row_steps)
    def _():
        turned_branch[...] = branch[...].T

    @pl.when(step >= row_steps)
    def _():
        part = plain_product(turned_branch[...], context[...]).astype(jnp.bfloat16)
        kept[...], sent[...] = by_core(rows_per_device, part)
        grad_context[...] = plain_product(branch[...], weight[...]).astype(jnp.bfloat16)


def project_backward(grad_normed, middle, out_grad, gain, context, weight, rows_per_device):
    tokens, depth = middle.shape
    width = context.shape[1]
    chips = depth // (2 * rows_per_device)
    shape = shape_of((chips, rows_per_device, width), jnp.bfloat16)
    row_steps = tokens // ROW_TILE

    def column(k):
        return jnp.maximum(k - row_steps, 0)

    def row_block(k):
        return (jnp.minimum(k, row_steps - 1), 0)

    rows = pl.BlockSpec((ROW_TILE, depth), row_block)
    block = pl.BlockSpec((chips, rows_per_device, FF_TILE), lambda k: (0, 0, column(k)))

    def columns(count):
        return pl.BlockSpec((count, FF_TILE), lambda k: (0, column(k)))

    return kernel_call(
        functools.partial(project_backward_kernel, rows_per_device),
        "project_backward",
        (row_steps + width // FF_TILE,),
        [rows, rows, rows, whole(gain), columns(tokens), columns(depth)],
        (
            shape,
            shape,
            shape_of((tokens, width), jnp.bfloat16),
            shape_of((tokens, depth), jnp.float32),
            shape_of(gain.shape, jnp.float32),
        ),
        (block, block, columns(tokens), rows, whole(gain)),
        scratch=[
            pltpu.VMEM((tokens, depth), jnp.bfloat16),
            pltpu.VMEM((depth, tokens), jnp.bfloat16),
        ],
    )(grad_normed, middle, out_grad, gain, context, weight)


def position_tables(segment_ids):
    _, micro_rows = segment_ids.shape
    order = jnp.arange(micro_rows, dtype=jnp.int32)
    same = segment_ids[:, :, None] == segment_ids[:, None, :]
    earlier = order[None, :] < order[:, None]
    positions = jnp.sum(jnp.where(same & earlier[None], 1, 0), axis=2).astype(jnp.int32)
    half_size = HEAD_WIDTH // 2
    frequency = ROPE_BASE ** (-(jnp.arange(half_size, dtype=jnp.float32) * (2.0 / HEAD_WIDTH)))
    angles = positions.reshape(-1, 1).astype(jnp.float32) * frequency[None, :]
    cosine, sine = jnp.cos(angles), jnp.sin(angles)
    allowed = same & (earlier | (order[None, :] == order[:, None]))[None]
    return (
        jnp.concatenate([cosine, cosine], axis=-1),
        jnp.concatenate([-sine, sine], axis=-1),
        jnp.where(allowed, 0.0, -1e30).astype(jnp.float32),
    )


def adamw(weight, first, second, grad, rate, decay):
    first_new = BETA_ONE * first + (1.0 - BETA_ONE) * grad
    second_new = BETA_TWO * second + (1.0 - BETA_TWO) * grad * grad
    corrected = (
        first_new
        / (1.0 - BETA_ONE**STEP)
        / (jnp.sqrt(second_new / (1.0 - BETA_TWO**STEP)) + ADAM_EPS)
    )
    return (weight - rate * (corrected + decay * weight), first_new, second_new)


def per_device(
    grid,
    activations,
    segment_ids,
    out_grad,
    qkv_weight,
    qkv_first,
    qkv_second,
    out_weight,
    out_first,
    out_second,
    gate_up_weight,
    gate_up_first,
    gate_up_second,
    down_weight,
    down_first,
    down_second,
    norm_gains,
    gains_first,
    gains_second,
):
    qkv_low = qkv_weight.astype(jnp.bfloat16)
    out_low = out_weight.astype(jnp.bfloat16)
    gate_up_low = gate_up_weight.astype(jnp.bfloat16)
    down_low = down_weight.astype(jnp.bfloat16)

    gain_count = norm_gains.shape[0]
    gain_start = lax.axis_index("dp") * gain_count
    all_gains = jnp.zeros((1, gain_count * grid.count), jnp.bfloat16)
    all_gains = lax.dynamic_update_slice(
        all_gains, norm_gains.astype(jnp.bfloat16)[None], (0, gain_start)
    )
    size = grid.size
    heads_of = KEY_VALUE_HEADS // 4
    out_rows, gate_rows = out_low.shape[0], gate_up_low.shape[0]
    qkv_rows, down_rows = qkv_low.shape[0], down_low.shape[0]

    tables = position_tables(segment_ids)
    scale_one = rms_scale(activations)
    v = Steps(out_low=out_low, gate_up_low=gate_up_low)
    v.qkv_line = z_pieces(grid, qkv_low, False)
    down_block = jnp.concatenate([down_low, rows_of_gains(all_gains, down_low.shape[1])], axis=0)
    down_sides = plane_sides(grid, down_block)
    down_corners = plane_corners(grid, down_sides, cut_at=down_rows)
    v.down_chip, v.gains, down_places = chip_plane(down_block, down_sides, down_corners, down_rows)
    v.close()

    v.qkv_column = jnp.stack(v.qkv_line)
    v.qkv_sides = plane_sides(grid, v.qkv_column)
    all_gains = v.gains.reshape(1, -1)[:, : gain_count * grid.count]
    out_block = jnp.concatenate([v.out_low, rows_of_gains(all_gains, out_low.shape[1])], axis=0)
    v.out_line = z_pieces(grid, out_block, False)
    v.grad_feed = out_grad.astype(jnp.bfloat16)
    v.drop("qkv_line", "out_low", "gains")
    v.close()

    grad_feed = v.grad_feed
    v.out_column = jnp.stack([piece[:out_rows] for piece in v.out_line])
    gains = sum(piece[out_rows:].astype(jnp.float32) for piece in v.out_line)
    gains = gains.reshape(1, -1)[:, : gain_count * grid.count]
    v.gains = gains
    v.qkv_corners = plane_corners(grid, v.qkv_sides)
    v.gate_up_moved = {1: grid.shift(v.gate_up_low, "z", 1)}
    v.qkv_sides_swapped = swap_tree(grid, v.qkv_sides)
    v.drop("grad_feed", "out_line")
    v.close()

    every = tuple(range(size["z"]))
    middle_plane = size["z"] // 2
    gains = small_sum(grid, v.gains, "c")
    gain_one, gain_two = gains[:, :D], gains[:, D : 2 * D]
    gain_query = gains[:, 2 * D : 2 * D + HEAD_WIDTH]
    gain_key = gains[:, 2 * D + HEAD_WIDTH :]
    normed_one = (activations * scale_one * gain_one).astype(jnp.bfloat16)
    qkv_column_swapped, qkv_corners_swapped = swap_tree(grid, (v.qkv_column, v.qkv_corners))
    v.out_sides = plane_sides(grid, v.out_column)
    v.near_column = jnp.stack([v.gate_up_low, v.gate_up_moved[1]])
    v.near_sides = plane_sides(grid, v.near_column)
    v.gate_up_moved[2] = grid.shift(v.gate_up_low, "z", 2)
    qkv_full = assemble(
        grid,
        plane_pieces(every, v.qkv_column, v.qkv_sides, v.qkv_corners),
        plane_pieces(every, qkv_column_swapped, v.qkv_sides_swapped, qkv_corners_swapped),
    )
    v.drop("qkv_column", "qkv_sides", "qkv_corners", "gate_up_low", "gains")
    v.drop("qkv_sides_swapped")
    parts = []

    def attention_part(part, context):
        *kept, context = attention(
            after(normed_one, *flat(context)),
            qkv_full,
            tables,
            gain_query,
            gain_key,
            context,
            part * heads_of,
            heads_of,
        )
        parts.append(kept)
        return context

    context = attention_part(0, None)
    v.gate_up_moved[3] = grid.shift(
        after(gate_up_low, context, v.gate_up_moved[2]), "z", 3
    )
    v.context = attention_part(1, context)
    v.close()

    v.far_column = jnp.stack([v.gate_up_moved[2], v.gate_up_moved[3]])
    v.out_corners = plane_corners(grid, v.out_sides)
    v.far_sides = plane_sides(grid, v.far_column)
    v.down_moved = {1: grid.shift(v.down_chip, "z", 1)}
    v.context = attention_part(3, attention_part(2, v.context))
    v.drop("gate_up_moved")
    v.close()

    v.gate_up_corners = plane_corners(grid, (v.near_sides[0], v.far_sides[1]), halved=False)
    v.down_moved[3] = grid.shift(v.down_chip, "z", 3)
    out_swapped = swap_together(grid, (v.out_column, v.out_sides, v.out_corners))
    v.near_sides_swapped = swap_tree(grid, after_tree(v.near_sides, out_swapped))
    out_full = assemble(
        grid,
        plane_pieces(every, v.out_column, v.out_sides, v.out_corners),
        plane_pieces(every, *out_swapped),
    )
    v.far_sides_swapped = swap_tree(
        grid, after_tree(v.far_sides, out_full, v.near_sides_swapped)
    )
    middle, v.normed_two = project(v.context, out_full, activations, gain_two)
    context = v.context
    v.drop("out_column", "out_sides", "out_corners", "context")
    v.close()

    normed_two = v.normed_two
    corners_swapped = swap_tree(grid, v.gate_up_corners)
    columns_swapped = swap_tree(grid, (v.near_column, v.far_column))
    v.down_moved[2] = grid.shift(v.down_chip, "z", 2)
    near, far = every[:middle_plane], every[middle_plane:]
    v.hidden, v.slope, v.lift, gate_up_full = feed(
        grid,
        normed_two,
        plane_pieces(near, v.near_column, v.near_sides, {})
        + plane_pieces(far, v.far_column, v.far_sides, {})
        + corner_pieces(every, v.gate_up_corners),
        plane_pieces(near, columns_swapped[0], v.near_sides_swapped, {})
        + plane_pieces(far, columns_swapped[1], v.far_sides_swapped, {})
        + corner_pieces(every, corners_swapped),
    )
    early = after_tree(
        [v.down_chip, v.down_moved[1], v.down_moved[3]], corners_swapped, columns_swapped
    )
    v.down_swapped = swap_tree(grid, early)
    v.down_parts = outer(grad_feed, v.hidden, down_rows)
    v.drop("near_column", "far_column", "near_sides", "far_sides", "gate_up_corners", "normed_two")
    v.drop("near_sides_swapped", "far_sides_swapped")
    v.close()

    hidden, slope, lift = v.hidden, v.slope, v.lift
    down_line = [v.down_chip, *[v.down_moved[hops] for hops in grid.hops("z")]]
    own_swapped, one_swapped, three_swapped = v.down_swapped
    two_swapped = grid.shift(v.down_moved[2], "c", 1)
    down_line_swapped = [own_swapped, one_swapped, two_swapped, three_swapped]
    slots = [(axis, hops) for axis in "zyx" for hops in range(size[axis])]
    numbers = jnp.stack([grid.ahead(axis, hops) for axis, hops in slots]).astype(jnp.int32)

    def here(axis, hops):
        return Place(slots.index((axis, hops)))

    def in_planes(pair):
        return [
            part.reshape(-1, size["y"], size["x"], *part.shape[-2:]) for part in pair
        ]

    down_full = assemble(
        grid, line_pieces(down_line, down_places), line_pieces(down_line_swapped, down_places)
    )

    v.down_terms = swapped(grid, in_planes(after_tree(v.down_parts, two_swapped)))

    def feed_part(half, total):
        *pair, total = feed_backward(
            grad_feed, down_full, slope, lift, normed_two, gate_up_full, total, half, gate_rows
        )
        return pair, total

    v.even_parts, v.total = feed_part(0, None)
    v.drop("down_chip", "down_moved", "down_swapped", "down_parts", "hidden", "slope", "lift")
    v.close()

    merge = Merge(grid, numbers)
    down_one = line(merge, here, [(v.down_terms, every)], 1, lead=2)
    made = merge.run()
    v.down_moved = [Source(down_one(made))]
    v.even = swapped(grid, in_planes(v.even_parts))
    v.odd_parts, v.total = feed_part(1, v.total)
    v.drop("even_parts")
    v.close()

    merge = Merge(grid, numbers)
    even_corners = corners(merge, here, v.even)
    down_three = line(merge, here, [(v.down_terms, every)], 3, lead=2)
    made = merge.run()
    v.even_corners = even_corners(made)
    v.down_moved.append(Source(down_three(made)))
    v.odd = swapped(grid, in_planes(v.odd_parts))
    *v.out_parts, v.grad_context, v.grad_middle, v.gain_two_part = project_backward(
        v.total, middle, out_grad, gain_two, context, out_full, out_rows
    )
    v.drop("odd_parts", "total")
    v.close()

    low, high = halves_of(v.down_terms)
    grad_context, grad_middle, gain_two_part = v.grad_context, v.grad_middle, v.gain_two_part
    v.drop("grad_context", "grad_middle", "gain_two_part")
    merge = Merge(grid, numbers)
    even_sides = sides(merge, here, v.even, v.even_corners)
    down_two = line(merge, here, [(v.down_terms, every)], 2, rows=low, lead=2)
    made = merge.run()
    v.even = even_sides(made)
    v.down_moved.append(Source(down_two(made)))
    v.out_terms = swapped(grid, in_planes(v.out_parts))
    v.gain_terms = []

    def backward_part(part, rows, total):
        *v.rows, v.total, terms_q, terms_k = attention_backward(
            *parts[part],
            grad_context,
            tables,
            gain_query,
            gain_key,
            normed_one,
            qkv_full,
            total,
            rows,
            part * heads_of,
            qkv_rows,
        )
        v.gain_terms = v.gain_terms + [(terms_q, terms_k)]

    backward_part(0, [], None)
    v.drop("out_parts", "even_corners")
    v.close()

    merge = Merge(grid, numbers)
    odd_corners = corners(merge, here, v.odd)
    out_corners = corners(merge, here, v.out_terms)
    down_two = line(merge, here, [(v.down_terms, every)], 2, rows=high, lead=2)
    down_own = line(merge, here, [(v.down_terms, every)], 0, lead=2)
    made = merge.run()
    v.odd_corners = odd_corners(made)
    v.out_corners = out_corners(made)
    v.down_moved += [Source(down_two(made), high[0]), Source(down_own(made))]
    backward_part(1, v.rows, v.total)
    v.drop("down_terms")
    v.close()

    merge = Merge(grid, numbers)
    odd_sides = sides(merge, here, v.odd, v.odd_corners)
    down_corners = corners(merge, here, v.down_moved, lead=0)
    made = merge.run()
    v.odd = odd_sides(made)
    v.down_corners = down_corners(made)
    v.first = swapped(grid, in_planes(v.rows[:2]))
    backward_part(2, v.rows[2:], v.total)
    v.drop("odd_corners")
    v.close()

    gate_up_groups = [(v.even, (0, 2)), (v.odd, (1, 3))]
    merge = Merge(grid, numbers)
    out_sides = sides(merge, here, v.out_terms, v.out_corners)
    gate_up_lines = [line(merge, here, gate_up_groups, hops) for hops in (1, 3, 0)]
    made = merge.run()
    v.out_terms = out_sides(made)
    v.gate_up_moved = [go(made) for go in gate_up_lines]
    backward_part(3, v.rows, v.total)
    v.drop("out_corners")
    v.close()

    v.last = swapped(grid, in_planes(v.rows))
    merge = Merge(grid, numbers)
    first_corners = corners(merge, here, v.first)
    down_sides = sides(merge, here, v.down_moved, v.down_corners, lead=0)
    made = merge.run()
    v.first_corners = first_corners(made)
    v.down_terms = down_sides(made)
    total, gain_terms = v.total, v.gain_terms
    v.drop("rows", "total", "gain_terms", "down_moved", "down_corners")
    v.close()

    gate_up_groups = [(v.even, (0, 2)), (v.odd, (1, 3))]
    merge = Merge(grid, numbers)
    last_corners = corners(merge, here, v.last)
    first_sides = sides(merge, here, v.first, v.first_corners)
    gate_up_two = line(merge, here, gate_up_groups, 2)
    made = merge.run()
    v.last_corners = last_corners(made)
    v.first = first_sides(made)
    v.gate_up_moved.append(gate_up_two(made))
    v.layer_output = finish(after(hidden, made), down_full, middle)
    total = after(total, v.layer_output)
    grad_block, gain_one_terms = norm_backward(activations, scale_one, gain_one, total)
    v.gains_part = jnp.concatenate(
        [
            jnp.sum(gain_one_terms, axis=0, keepdims=True),
            gain_two_part,
            sum(terms for terms, _ in gain_terms),
            sum(terms for _, terms in gain_terms),
        ],
        axis=1,
    )
    v.total = total
    v.drop("even", "odd", "first_corners")
    v.close()

    merge = Merge(grid, numbers)
    last_sides = sides(merge, here, v.last, v.last_corners)
    out_lines = [line(merge, here, [(v.out_terms, every)], hops) for hops in range(size["z"])]
    made = merge.run()
    v.last = last_sides(made)
    v.out_moved = [go(made) for go in out_lines]
    v.gains_part = small_sum(grid, after(v.gains_part, v.out_moved), "z")
    v.gate_up_new = adamw(
        gate_up_weight, gate_up_first, gate_up_second, total_of(*v.gate_up_moved), 0.06, 0.1
    )
    down_total = total_of(*[term.array for term in v.down_terms])
    v.down_new = adamw(down_weight, down_first, down_second, down_total, 0.04, 0.1)
    grad_block, _ = norm_backward(activations, scale_one, gain_one, after(v.total, made))
    v.input_grad = grad_middle + grad_block
    v.drop("last_corners", "gate_up_moved", "down_terms", "out_terms", "total")
    v.close()

    qkv_groups = [(v.first, (0,)), (v.last, (1, 2, 3))]
    merge = Merge(grid, numbers)
    qkv_lines = [line(merge, here, qkv_groups, hops) for hops in range(size["z"])]
    made = merge.run()
    qkv_total = total_of(*[go(made) for go in qkv_lines])
    out_new = adamw(out_weight, out_first, out_second, total_of(*v.out_moved), 0.25, 0.1)
    gains_total = small_sum(grid, v.gains_part, "xyc")
    gains_total = lax.dynamic_slice(gains_total, (0, gain_start), (1, gain_count))[0]

    return (
        v.layer_output,
        v.input_grad,
        *adamw(qkv_weight, qkv_first, qkv_second, qkv_total, 0.06, 0.1),
        *out_new,
        *v.gate_up_new,
        *v.down_new,
        *adamw(norm_gains, gains_first, gains_second, gains_total, 0.3, 0.0),
    )


def solution(mesh):
    return jax.shard_map(
        functools.partial(per_device, Grid(mesh.shape["dp"])),
        mesh=mesh,
        in_specs=(
            P("dp", None),
            P("dp", None),
            P("dp", None),
            P("dp", None),
            P("dp", None),
            P("dp", None),
            P("dp", None),
            P("dp", None),
            P("dp", None),
            P("dp", None),
            P("dp", None),
            P("dp", None),
            P("dp", None),
            P("dp", None),
            P("dp", None),
            P("dp"),
            P("dp"),
            P("dp"),
        ),
        out_specs=(
            P("dp", None),
            P("dp", None),
            P("dp", None),
            P("dp", None),
            P("dp", None),
            P("dp", None),
            P("dp", None),
            P("dp", None),
            P("dp", None),
            P("dp", None),
            P("dp", None),
            P("dp", None),
            P("dp", None),
            P("dp", None),
            P("dp"),
            P("dp"),
            P("dp"),
        ),
        check_vma=False,
    )
```

```python
import functools
import itertools
import math

import jax
import jax.numpy as jnp
from jax import lax
from jax.experimental import pallas as pl
from jax.experimental.pallas import tpu as pltpu
from jax.sharding import PartitionSpec as P

D = 1024
QUERY_HEADS = 16
KEY_VALUE_HEADS = 8
HEAD_WIDTH = 128
FF = 3072
STEP = 10


NORM_EPS = 1e-06
ROPE_BASE = 1000000.0
BETA_ONE = 0.9
BETA_TWO = 0.95
ADAM_EPS = 1e-08


def contract_last(left_side, right_side):
    return lax.dot_general(
        left_side, right_side, (((1,), (1,)), ((), ())), preferred_element_type=jnp.float32
    )


def contract_first(left_side, right_side):
    return lax.dot_general(
        left_side, right_side, (((0,), (0,)), ((), ())), preferred_element_type=jnp.float32
    )


def plain_product(left_side, right_side):
    return jnp.dot(left_side, right_side, preferred_element_type=jnp.float32)


def rms_scale(values):
    return lax.rsqrt(jnp.mean(values * values, axis=-1, keepdims=True) + NORM_EPS)


class Grid:
    def __init__(self, count):
        chips = count // 2
        flat = 2 if chips <= 16 else 4
        self.size = {"z": chips // (flat * flat), "y": flat, "x": flat, "c": 2}
        self.step = {"z": 2 * flat * flat, "y": 2 * flat, "x": 2, "c": 1}
        self.count = count

    def at(self, axis):
        return (lax.axis_index("dp") // self.step[axis]) % self.size[axis]

    def ahead(self, axis, hops):
        return (self.at(axis) + hops) % self.size[axis]

    def hops(self, axis):
        return range(1, self.size[axis])

    def shift(self, value, axis, hops):
        size, step = self.size[axis], self.step[axis]
        pairs = []
        for device in range(self.count):
            here = (device // step) % size
            pairs.append((device, device + ((here + hops) % size - here) * step))
        return lax.ppermute(value, "dp", pairs)


def after(value, *others):
    return lax.optimization_barrier((value, *jax.tree.leaves(others)))[0]


GROUP = QUERY_HEADS // KEY_VALUE_HEADS
SCORE_SCALE = HEAD_WIDTH ** (-0.5)
EXP2_SCALE = SCORE_SCALE * math.log2(math.e)
VMEM_BYTES = 60 * 1024 * 1024
VMEM_LESS = 50 * 1024 * 1024
VMEM_OF = {name: 46 * 1024 * 1024 for name in ("finish", "outer", "project")}


def norm_backward(values, scale_rows, gain, grad_out):
    scaled = gain * grad_out
    grad_in = scale_rows * scaled - values * scale_rows**3 * jnp.mean(
        scaled * values, axis=-1, keepdims=True
    )
    return (grad_in, grad_out * values * scale_rows)


def z_pieces(grid, shard, chained, *dependencies):
    moved = [shard]
    for hops in grid.hops("z"):
        moved.append(grid.shift(after(shard, *dependencies) if dependencies else shard, "z", hops))
        if chained:
            dependencies = (moved[-1],)
    return moved


def swap_tree(grid, buffers):
    return jax.tree.map(lambda buffer: grid.shift(buffer, "c", 1), buffers)


def swap_together(grid, buffers):
    leaves, shape = jax.tree.flatten(buffers)
    moved = grid.shift(jnp.concatenate(leaves, axis=0), "c", 1)
    starts = itertools.accumulate([0] + [leaf.shape[0] for leaf in leaves])
    return jax.tree.unflatten(
        shape, [Part(moved, start, leaf.shape[0]) for start, leaf in zip(starts, leaves)]
    )


@jax.tree_util.register_pytree_node_class
class Part:
    def __init__(self, array, start, count):
        self.array, self.start, self.count = array, start, count

    def tree_flatten(self):
        return (self.array,), (self.start, self.count)

    @classmethod
    def tree_unflatten(cls, held, leaves):
        return cls(*leaves, *held)


def plane_sides(grid, column, *dependencies):
    sent = after(column, *dependencies) if dependencies else column
    from_x = {hops: grid.shift(sent, "x", hops) for hops in grid.hops("x")}
    from_y = {hops: grid.shift(sent, "y", hops) for hops in grid.hops("y")}
    return from_x, from_y


def plane_corners(grid, sides, *dependencies, halved=True, cut_at=None):
    from_x, from_y = sides
    half = from_x[1].shape[0] // 2 if cut_at is None else cut_at
    corners = {}
    for j in from_x:
        for l in from_y:
            first, second = from_x[j], from_y[l]
            if halved:
                first, second = first[:half], second[half:]
            if dependencies:
                first, second = after(first, *dependencies), after(second, *dependencies)
            corners[j, l] = (grid.shift(first, "y", l), grid.shift(second, "x", j))
    return corners


def corner_pieces(planes, corners):
    half = len(planes) // 2
    pieces = []
    for (j, l), (first, second) in corners.items():
        pieces.append((first, [{"z": hops, "x": j, "y": l} for hops in planes[:half]]))
        pieces.append((second, [{"z": hops, "x": j, "y": l} for hops in planes[half:]]))
    return pieces


def plane_pieces(planes, column, sides, corners):
    from_x, from_y = sides
    pieces = [(column, [{"z": hops} for hops in planes])]
    pieces += [(from_x[j], [{"z": hops, "x": j} for hops in planes]) for j in from_x]
    pieces += [(from_y[l], [{"z": hops, "y": l} for hops in planes]) for l in from_y]
    return pieces + corner_pieces(planes, corners)


def after_tree(tree, *dependencies):
    leaves, shape = jax.tree.flatten(tree)
    tied = lax.optimization_barrier((*leaves, *flat(dependencies)))
    return jax.tree.unflatten(shape, tied[: len(leaves)])


def flat(*groups):
    return [leaf for leaf in jax.tree.leaves(groups)]


def rows_of_gains(gains, width):
    rows = -(-gains.shape[1] // width)
    block = jnp.pad(gains, ((0, 0), (0, rows * width - gains.shape[1]))).reshape(rows, width)
    return jnp.pad(block, ((0, 16 - rows), (0, 0)))


def chip_plane(block, sides_received, corners_received, rows):
    from_x, from_y = sides_received
    blocks = [block, *from_x.values(), *from_y.values()]
    shards = [part[:rows] for part in blocks]
    below = [part[rows:] for part in blocks]
    places = [{}] + [{"x": j} for j in from_x] + [{"y": l} for l in from_y]
    for (j, l), (shard, rest) in corners_received.items():
        shards.append(shard)
        below.append(rest)
        places.append({"x": j, "y": l})
    return jnp.stack(shards), sum(below), places


def arrivals(grid, places_of, pieces, held, came):
    copies = []
    for which, first, places in places_of:
        for slot, place in enumerate(places, first):
            index = 0
            for axis in ("z", "y", "x", "c"):
                size = grid.size[axis]
                index = index + (grid.at(axis) + size - place.get(axis, 0)) % size * grid.step[axis]
            copies.append(
                pltpu.make_async_copy(pieces[which].at[slot], held.at[index], came.at[index])
            )
    return copies


def arrived(held, device, came):
    return pltpu.make_async_copy(held.at[device], held.at[device], came.at[device])


def leaving(held, device, out, went):
    return pltpu.make_async_copy(held.at[device], out.at[device], went.at[device])


def assemble_kernel(grid, places_of, *refs):
    pieces, (out, held, came, went) = refs[:-4], refs[-4:]
    for copy in arrivals(grid, places_of, pieces, held, came):
        copy.start()
    for device in range(grid.count):
        arrived(held, device, came).wait()
        leaving(held, device, out, went).start()
    for device in range(grid.count):
        leaving(held, device, out, went).wait()


def line_pieces(line, places):
    return [
        (buffer, [dict(place, z=hops) for place in places]) for hops, buffer in enumerate(line)
    ]


def gather_plan(own_pieces, swapped_pieces):
    pieces = own_pieces + [
        (buffer, [dict(place, c=1) for place in places]) for buffer, places in swapped_pieces
    ]
    arrays, places_of = [], []
    for buffer, places in pieces:
        array, first = (buffer.array, buffer.start) if isinstance(buffer, Part) else (buffer, 0)
        which = next((at for at, known in enumerate(arrays) if known is array), len(arrays))
        if which == len(arrays):
            arrays.append(array)
        places_of.append((which, first, places))
    return arrays, places_of


def assemble(grid, own_pieces, swapped_pieces):
    arrays, places_of = gather_plan(own_pieces, swapped_pieces)
    rows, width = arrays[0].shape[1:]
    dims = (grid.count, rows, width)
    gathered = pl.pallas_call(
        functools.partial(assemble_kernel, grid, places_of),
        out_shape=jax.ShapeDtypeStruct(dims, jnp.bfloat16),
        in_specs=[pl.BlockSpec(memory_space=pl.ANY)] * len(arrays),
        out_specs=pl.BlockSpec(memory_space=pl.ANY),
        scratch_shapes=[
            pltpu.VMEM(dims, jnp.bfloat16),
            pltpu.SemaphoreType.DMA((grid.count,)),
            pltpu.SemaphoreType.DMA((grid.count,)),
        ],
        compiler_params=pltpu.CompilerParams(vmem_limit_bytes=VMEM_BYTES),
        cost_estimate=LITTLE,
        name="assemble",
    )(*arrays)
    return gathered.reshape(grid.count * rows, width)


@jax.tree_util.register_pytree_node_class
class Source:
    def __init__(self, array, first=0):
        self.array, self.first = array, first

    def tree_flatten(self):
        return (self.array,), self.first

    @classmethod
    def tree_unflatten(cls, first, leaves):
        return cls(*leaves, first)


class Place:
    def __init__(self, slot, table=None):
        self.slot, self.table = slot, table

    def of(self, numbers):
        here = numbers[self.slot]
        if self.table is None:
            return here
        return sum(jnp.where(here == at, entry, 0) for at, entry in enumerate(self.table))

    def __eq__(self, other):
        return isinstance(other, Place) and (self.slot, self.table) == (other.slot, other.table)

    def __hash__(self):
        return hash((self.slot, self.table))


class Merge:
    STRIP = 16
    STEPS = 2

    def __init__(self, grid, numbers):
        self.grid, self.numbers = grid, numbers
        self.inputs, self.outputs, self.keys = [], [], {}

    def cut(self, array, places):
        key = (id(array), places)
        if key not in self.keys:
            self.keys[key] = len(self.inputs)
            self.inputs.append((array, places))
        return self.keys[key]

    def terms(self, sources, places, low, high):
        found = []
        for source in sources:
            first = source.first
            if first <= low and high <= first + source.array.shape[-2]:
                found.append((self.cut(source.array, places), low - first, high - first))
        return found

    def add(self, *options, chosen=None):
        self.outputs.append((options, chosen))
        return len(self.outputs) - 1

    def shape(self, options):
        array, places = self.inputs[options[0][0][0][0]]
        lead = [size for size, place in zip(array.shape, places) if place is None]
        rows = sum(segment[0][2] - segment[0][1] for segment in options[0])
        return (*lead, rows, array.shape[-1])

    def run(self):
        edges = [
            edge
            for options, _ in self.outputs
            for segments in options
            for segment in segments
            for term in segment
            for edge in term[1:]
        ]
        if any(edge % self.STRIP for edge in edges):
            return self.run_plain()
        shapes = [self.shape(options) for options, _ in self.outputs]
        def spec(array, places):
            block = [
                None if place is not None else size for size, place in zip(array.shape, places)
            ]
            return pl.BlockSpec(
                (*block, array.shape[-2], array.shape[-1] // self.STEPS),
                lambda step, held: (
                    *[0 if place is None else place.of(held) for place in places], 0, step
                ),
            )

        return pl.pallas_call(
            self.kernel,
            grid_spec=pltpu.PrefetchScalarGridSpec(
                num_scalar_prefetch=1,
                grid=(self.STEPS,),
                in_specs=[spec(*pair) for pair in self.inputs],
                out_specs=[
                    pl.BlockSpec(
                        (*dims[:-1], dims[-1] // self.STEPS),
                        lambda step, held, axes=len(dims): (0,) * (axes - 1) + (step,),
                    )
                    for dims in shapes
                ],
            ),
            out_shape=[jax.ShapeDtypeStruct(dims, jnp.bfloat16) for dims in shapes],
            compiler_params=pltpu.CompilerParams(vmem_limit_bytes=VMEM_LESS),
            cost_estimate=LITTLE,
            name="merge",
        )(self.numbers, *[array for array, _ in self.inputs])

    def kernel(self, held, *refs):
        inputs, outputs = refs[: len(self.inputs)], refs[len(self.inputs) :]
        for out, (options, chosen) in zip(outputs, self.outputs):
            for number, segments in enumerate(options):
                write = functools.partial(self.write, out, segments, inputs)
                if chosen is None:
                    write()
                else:
                    pl.when(chosen.of(held) == number)(write)

    def write(self, out, segments, inputs):
        start = 0
        for segment in segments:
            count = segment[0][2] - segment[0][1]
            strips = count // self.STRIP
            unroll = max(part for part in range(1, 9) if strips % part == 0)
            for lead in itertools.product(*[range(size) for size in out.shape[:-2]]):

                @pl.loop(0, strips, unroll=unroll)
                def _(strip, start=start, lead=lead, segment=segment):
                    def rows(first):
                        at = pl.multiple_of(first + strip * self.STRIP, self.STRIP)
                        return (*lead, pl.ds(at, self.STRIP), slice(None))

                    added = sum(inputs[k][rows(low)].astype(jnp.float32) for k, low, _ in segment)
                    out[rows(start)] = added.astype(jnp.bfloat16)

            start += count

    def run_plain(self):
        def part(term):
            array, places = self.inputs[term[0]]
            axis = 0
            for place in places:
                if place is None:
                    axis += 1
                else:
                    array = lax.dynamic_index_in_dim(
                        array, place.of(self.numbers), axis, keepdims=False
                    )
            return lax.slice_in_dim(array, term[1], term[2], axis=-2 + array.ndim)

        results = []
        for options, chosen in self.outputs:
            made = []
            for segments in options:
                sums = [
                    sum(part(term).astype(jnp.float32) for term in segment).astype(jnp.bfloat16)
                    for segment in segments
                ]
                made.append(jnp.concatenate(sums, axis=-2) if len(sums) > 1 else sums[0])
            results.append(made[0])
            for number in range(1, len(made)):
                results[-1] = jnp.where(chosen.of(self.numbers) == number, made[number], results[-1])
        return results


def swapped(grid, kept_and_sent):
    kept, sent = kept_and_sent
    return [Source(kept), Source(grid.shift(sent, "c", 1))]


def halves_of(sources):
    rows = sources[0].array.shape[-2]
    return (0, rows // 2), (rows // 2, rows)


def corners(merge, here, sources, lead=1):
    low, high = halves_of(sources)
    grid, whole_axes = merge.grid, (None,) * lead
    slots = {}
    for j in grid.hops("x"):
        for l in grid.hops("y"):
            place = (*whole_axes, here("y", l), here("x", j))
            slots[j, l] = (
                merge.add([merge.terms(sources, place, *low)]),
                merge.add([merge.terms(sources, place, *high)]),
            )

    def go(made):
        return {
            (j, l): (grid.shift(made[first], "x", j), grid.shift(made[second], "y", l))
            for (j, l), (first, second) in slots.items()
        }

    return go


def sides(merge, here, sources, crossed, lead=1):
    low, high = halves_of(sources)
    grid, whole_axes = merge.grid, (None,) * lead
    own_place = (*whole_axes, here("y", 0), here("x", 0))
    bare = (None,) * lead
    own = merge.add([merge.terms(sources, own_place, *half) for half in (low, high)])
    to_x, to_y = {}, {}
    for j in grid.hops("x"):
        place = (*whole_axes, here("y", 0), here("x", j))
        received = [Source(crossed[j, l][1], high[0]) for l in grid.hops("y")]
        to_x[j] = merge.add(
            [
                merge.terms(sources, place, *low),
                merge.terms(sources, place, *high) + merge.terms(received, bare, *high),
            ]
        )
    for l in grid.hops("y"):
        place = (*whole_axes, here("y", l), here("x", 0))
        received = [Source(crossed[j, l][0]) for j in grid.hops("x")]
        to_y[l] = merge.add(
            [
                merge.terms(sources, place, *low) + merge.terms(received, bare, *low),
                merge.terms(sources, place, *high),
            ]
        )

    def go(made):
        terms = [made[own]]
        terms += [grid.shift(made[to_x[j]], "x", j) for j in to_x]
        terms += [grid.shift(made[to_y[l]], "y", l) for l in to_y]
        return [Source(term) for term in terms]

    return go


def line(merge, here, groups, hops, rows=None, lead=0):
    grid = merge.grid
    plane = here("z", hops)
    owner = {
        number: (group, at)
        for group, (_, planes) in enumerate(groups)
        for at, number in enumerate(planes)
    }
    numbers = range(grid.size["z"])
    options = []
    for group, (sources, _) in enumerate(groups):
        index = Place(
            plane.slot, tuple(owner[n][1] if owner[n][0] == group else 0 for n in numbers)
        )
        place = (index, *(None,) * lead)
        parts = halves_of(sources) if rows is None else (rows,)
        options.append([merge.terms(sources, place, *part) for part in parts])
    chosen = Place(plane.slot, tuple(owner[n][0] for n in numbers)) if len(groups) > 1 else None
    slot = merge.add(*options, chosen=chosen)
    return lambda made: grid.shift(made[slot], "z", hops) if hops else made[slot]


def total_of(*terms):
    return sum(term.astype(jnp.float32) for term in terms)


class Steps:
    def __init__(self, **live):
        self.__dict__.update(live)

    def close(self):
        self.__dict__.update(after_tree(dict(self.__dict__)))

    def drop(self, *names):
        for name in names:
            del self.__dict__[name]


def small_sum(grid, value, axes):
    for axis in axes:
        value = value + sum(grid.shift(value, axis, hops) for hops in grid.hops(axis))
    return value


LITTLE = pl.CostEstimate(flops=1, bytes_accessed=1, transcendentals=0)


def whole(array):
    return pl.BlockSpec(array.shape, lambda *k: (0,) * array.ndim)


def in_vmem(array):
    return pl.BlockSpec(memory_space=pltpu.VMEM)


def kernel_call(
    body, name, grid, in_specs, out_shape, out_specs, scratch=(), aliases=None, vmem=VMEM_BYTES
):
    return pl.pallas_call(
        body,
        grid=grid,
        in_specs=in_specs,
        out_shape=out_shape,
        out_specs=out_specs,
        scratch_shapes=scratch,
        input_output_aliases=aliases or {},
        compiler_params=pltpu.CompilerParams(vmem_limit_bytes=VMEM_OF.get(name, vmem)),
        cost_estimate=LITTLE,
        name=name,
    )


def shape_of(dims, dtype):
    return jax.ShapeDtypeStruct(dims, dtype)


TRIO = (GROUP + 1) * HEAD_WIDTH


def lanes_of(head):
    return slice(head * HEAD_WIDTH, (head + 1) * HEAD_WIDTH)


def turned(values):
    return pltpu.roll(values, HEAD_WIDTH // 2, 1)


def stacked(values, rows, heads=GROUP):
    return jnp.concatenate([values[rows, lanes_of(g)] for g in range(heads)], axis=0)


def query_blocks(micro_rows):
    half = micro_rows // 2
    return [(0, half), (half, micro_rows)]


def powers_of(queries, keys, bias):
    return jnp.exp2(contract_last(queries, keys) * EXP2_SCALE + bias)


def group_bias(bias, micro, begin, end):
    return jnp.concatenate([bias[micro, begin:end, :end]] * GROUP, axis=0)


def attention_kernel(normed, wq, wk, wv, cosine, sine, bias, gain_q, gain_k, *outputs):
    keys_values = jnp.concatenate([wk[...], wv[...]], axis=0)
    attend(normed, wq[...], keys_values, cosine, sine, bias, gain_q, gain_k, *outputs[-6:])


def first_attention_kernel(grid, places_of, pieces_count, head_count, *refs):
    pieces, (normed, *tables) = refs[:pieces_count], refs[pieces_count : pieces_count + 6]
    *outputs, out, raw, held, came, went = refs[pieces_count + 6 :]
    step = pl.program_id(0)
    rows = held.shape[1]
    stretches = [
        (0, GROUP * HEAD_WIDTH),
        (QUERY_HEADS * HEAD_WIDTH, HEAD_WIDTH),
        ((QUERY_HEADS + KEY_VALUE_HEADS) * HEAD_WIDTH, HEAD_WIDTH),
    ]

    @pl.when(step == 0)
    def _():
        for copy in arrivals(grid, places_of, pieces, held, came):
            copy.start()

    def pass_on(device):
        arrived(held, device, came).wait()
        leaving(held, device, out, went).start()

    weights, early = [], set()
    for first, count in stretches:
        each = count // rows
        device = first // rows + step * each
        for number in range(each):
            pass_on(device + number)
        weights.append(held[pl.ds(device, each)].reshape(count, held.shape[2]))
        early |= set(range(first // rows, first // rows + head_count * each))
    keys_values = jnp.concatenate(weights[1:], axis=0)
    attend(normed, weights[0], keys_values, *tables, *outputs, raw)

    @pl.when(step == head_count - 1)
    def _():
        for device in range(grid.count):
            if device not in early:
                pass_on(device)
        for device in range(grid.count):
            leaving(held, device, out, went).wait()


def attend(
    normed, wq, keys_values, cosine, sine, bias, gain_q, gain_k,
    norms, scales, turns, value, context, held,
):
    held[:, : GROUP * HEAD_WIDTH] = contract_last(normed[...], wq)
    both = contract_last(normed[...], keys_values)
    held[:, GROUP * HEAD_WIDTH :] = both[:, :HEAD_WIDTH]
    value[...] = both[:, HEAD_WIDTH:].astype(jnp.bfloat16)
    micro_count, micro_rows, _ = bias.shape
    for micro in range(micro_count):
        start = micro * micro_rows
        rows = slice(start, start + micro_rows)
        for head in range(GROUP + 1):
            raw = held[rows, lanes_of(head)]
            scale = lax.rsqrt(jnp.mean(raw * raw, axis=-1, keepdims=True) + NORM_EPS)
            scale = jnp.broadcast_to(scale, raw.shape)
            normal = raw * scale
            gained = normal * (gain_q[...] if head < GROUP else gain_k[...])
            norms[rows, lanes_of(head)] = normal.astype(jnp.bfloat16)
            scales[rows, lanes_of(head)] = scale.astype(jnp.bfloat16)
            turns[rows, lanes_of(head)] = (
                gained * cosine[rows, :] + turned(gained) * sine[rows, :]
            ).astype(jnp.bfloat16)
        keys = turns[rows, lanes_of(GROUP)]
        for begin, end in query_blocks(micro_rows):
            block = slice(start + begin, start + end)
            count = end - begin
            powers = powers_of(
                stacked(turns, block), keys[:end], group_bias(bias, micro, begin, end)
            )
            inverse = 1.0 / jnp.sum(powers, axis=-1, keepdims=True)
            probs = (powers * inverse).astype(jnp.bfloat16)
            mixed = plain_product(probs, value[start : start + end, :]).astype(jnp.bfloat16)
            for g in range(GROUP):
                context[block, lanes_of(g)] = mixed[g * count : (g + 1) * count, :]


def with_turn(values):
    return jnp.concatenate([values, turned(values)], axis=1)


def head_backward(normal, scale, gain, grad, cos, sin):
    normal, scale = normal.astype(jnp.float32), scale.astype(jnp.float32)
    grad_normed = (grad[:, :HEAD_WIDTH] * cos - grad[:, HEAD_WIDTH:] * sin) * SCORE_SCALE
    scaled = gain * grad_normed
    terms = grad_normed * normal
    mean = jnp.mean(scaled * normal, axis=-1, keepdims=True)
    grad_raw = scale * (scaled - normal * mean)
    return grad_raw.astype(jnp.bfloat16), jnp.sum(terms, axis=0, keepdims=True)


def put_by_core(rows_per_device, result, part, at, plane, kept, sent, sems, sem):
    rows = result.shape[0]
    if rows >= 2 * rows_per_device:
        chips = rows // (2 * rows_per_device)
        part[0], part[1] = by_core(rows_per_device, result)
        stretch = pl.ds(at * chips, chips)
        return [
            pltpu.make_async_copy(part.at[0], kept.at[plane, stretch], sems.at[sem]),
            pltpu.make_async_copy(part.at[1], sent.at[plane, stretch], sems.at[sem + 1]),
        ]
    part[0, 0] = result
    mine = (at + lax.axis_index("dp")) % 2 == 0
    return [
        Either(
            mine,
            pltpu.make_async_copy(part.at[0, 0], kept.at[plane, at // 2], sems.at[sem]),
            pltpu.make_async_copy(part.at[0, 0], sent.at[plane, at // 2], sems.at[sem + 1]),
        )
    ]


class Either:
    def __init__(self, first_one, first, second):
        self.first_one, self.first, self.second = first_one, first, second

    def start(self):
        pl.when(self.first_one)(self.first.start)
        pl.when(jnp.logical_not(self.first_one))(self.second.start)

    def wait(self):
        pl.when(self.first_one)(self.first.wait)
        pl.when(jnp.logical_not(self.first_one))(self.second.wait)


def attention_backward_kernel(
    first, rows_per_device, held, norms, scales, turns, value, grad_context, cosine, sine, bias,
    gain_q, gain_k, normed, wq, wk, wv, *others,
):
    grad_raw_all, part_q, part_k, part_v, sems = others[-5:]
    kv_kept, kv_sent, total, terms_q, terms_k = others[-10:-5]

    @pl.when(pl.program_id(0) == 0)
    def _():
        terms_q[...] = jnp.zeros_like(terms_q)
        terms_k[...] = jnp.zeros_like(terms_k)
        if held:
            total[...] = others[0][...]
        else:
            total[...] = jnp.zeros_like(total)

    micro_count, micro_rows, _ = bias.shape
    for micro in range(micro_count):
        start = micro * micro_rows
        rows = slice(start, start + micro_rows)
        keys = turns[rows, lanes_of(GROUP)]
        both_keys = with_turn(keys)
        grad_values, grad_keys = 0.0, 0.0
        for begin, end in query_blocks(micro_rows):
            block = slice(start + begin, start + end)
            count = end - begin
            cos, sin = cosine[block, :], sine[block, :]
            queries = stacked(turns, block)
            powers = powers_of(queries, keys[:end], group_bias(bias, micro, begin, end))
            probs = powers * (1.0 / jnp.sum(powers, axis=-1, keepdims=True))
            grads = stacked(grad_context, block)
            grad_probs = contract_last(grads, value[start : start + end, :])
            weighted = probs * grad_probs
            centre = jnp.sum(weighted, axis=-1, keepdims=True)
            grad_scores = (weighted - probs * centre).astype(jnp.bfloat16)
            pad = ((0, micro_rows - end), (0, 0))
            grad_values += jnp.pad(contract_first(probs.astype(jnp.bfloat16), grads), pad)
            grad_keys += jnp.pad(contract_first(grad_scores, with_turn(queries)), pad)
            grad_queries = plain_product(grad_scores, both_keys[:end])
            for g in range(GROUP):
                grad_raw, terms = head_backward(
                    norms[block, lanes_of(g)],
                    scales[block, lanes_of(g)],
                    gain_q[...],
                    grad_queries[g * count : (g + 1) * count, :],
                    cos,
                    sin,
                )
                grad_raw_all[block, lanes_of(g)] = grad_raw
                terms_q[...] += terms
        grad_raw_all[rows, lanes_of(GROUP + 1)] = grad_values.astype(jnp.bfloat16)
        grad_raw, terms = head_backward(
            norms[rows, lanes_of(GROUP)],
            scales[rows, lanes_of(GROUP)],
            gain_k[...],
            grad_keys,
            cosine[rows, :],
            sine[rows, :],
        )
        grad_raw_all[rows, lanes_of(GROUP)] = grad_raw
        terms_k[...] += terms
    head = first + pl.program_id(0)
    half = KEY_VALUE_HEADS // 2
    queries_kept, queries_sent = (kv_kept, kv_sent) if first >= half else others[-12:-10]
    wide = GROUP * HEAD_WIDTH
    result = contract_first(grad_raw_all[...], normed[...]).astype(jnp.bfloat16)
    result_q, result_k, result_v = (
        result[:wide, :],
        result[wide : wide + HEAD_WIDTH, :],
        result[wide + HEAD_WIDTH :, :],
    )
    copies = [
        *put_by_core(
            rows_per_device, result_q, part_q, head % half, 0, queries_kept, queries_sent, sems, 0
        ),
        *put_by_core(rows_per_device, result_k, part_k, head, 1, kv_kept, kv_sent, sems, 2),
        *put_by_core(rows_per_device, result_v, part_v, head, 2, kv_kept, kv_sent, sems, 4),
    ]
    for copy in copies:
        copy.start()
    weights = jnp.concatenate([wq[...], wk[...], wv[...]], axis=0)
    total[...] += plain_product(grad_raw_all[...], weights)
    for copy in copies:
        copy.wait()


def by_core(rows_per_device, part):
    pairs = part.reshape(-1, 2, rows_per_device, part.shape[-1])
    here = lax.axis_index("dp") % 2 == 0
    first, second = pairs[:, 0], pairs[:, 1]
    return jnp.where(here, first, second), jnp.where(here, second, first)


def heads(rows, width, first=0):
    return pl.BlockSpec((rows, width), lambda k: (0, first + k))


def head_rows(heads_in, depth, first):
    return pl.BlockSpec((heads_in * HEAD_WIDTH, depth), lambda k: (first + k, 0))


def qkv_rows_of(depth, first):
    return [
        head_rows(GROUP, depth, first),
        head_rows(1, depth, QUERY_HEADS + first),
        head_rows(1, depth, QUERY_HEADS + KEY_VALUE_HEADS + first),
    ]


def attention(normed, qkv_full, tables, gain_q, gain_k, context, first, count):
    tokens, depth = normed.shape
    wide = GROUP * HEAD_WIDTH
    whole_context = shape_of((tokens, QUERY_HEADS * HEAD_WIDTH), jnp.bfloat16)
    held = [] if context is None else [context]
    return kernel_call(
        attention_kernel,
        "attention",
        (count,),
        [
            in_vmem(normed),
            *qkv_rows_of(depth, first),
            *[in_vmem(table) for table in tables],
            in_vmem(gain_q),
            in_vmem(gain_k),
            *[pl.BlockSpec(memory_space=pl.ANY)] * len(held),
        ],
        (
            shape_of((tokens, count * TRIO), jnp.bfloat16),
            shape_of((tokens, count * TRIO), jnp.bfloat16),
            shape_of((tokens, count * TRIO), jnp.bfloat16),
            shape_of((tokens, count * HEAD_WIDTH), jnp.bfloat16),
            whole_context,
        ),
        (
            heads(tokens, TRIO),
            heads(tokens, TRIO),
            heads(tokens, TRIO),
            heads(tokens, HEAD_WIDTH),
            heads(tokens, wide, first),
        ),
        scratch=[pltpu.VMEM((tokens, TRIO), jnp.float32)],
        aliases={9: 4} if held else None,
        vmem=VMEM_LESS,
    )(normed, qkv_full, qkv_full, qkv_full, *tables, gain_q, gain_k, *held)


def first_attention(grid, normed, own_pieces, swapped_pieces, tables, gain_q, gain_k, count):
    arrays, places_of = gather_plan(own_pieces, swapped_pieces)
    tokens, depth = normed.shape
    rows = arrays[0].shape[1]
    dims = (grid.count, rows, depth)
    anywhere = pl.BlockSpec(memory_space=pl.ANY)
    trio = shape_of((tokens, count * TRIO), jnp.bfloat16)
    *kept, context, weight = kernel_call(
        functools.partial(first_attention_kernel, grid, places_of, len(arrays), count),
        "attention",
        (count,),
        [
            *[anywhere] * len(arrays),
            in_vmem(normed),
            *[in_vmem(table) for table in tables],
            in_vmem(gain_q),
            in_vmem(gain_k),
        ],
        (
            trio,
            trio,
            trio,
            shape_of((tokens, count * HEAD_WIDTH), jnp.bfloat16),
            shape_of((tokens, QUERY_HEADS * HEAD_WIDTH), jnp.bfloat16),
            shape_of(dims, jnp.bfloat16),
        ),
        (
            heads(tokens, TRIO),
            heads(tokens, TRIO),
            heads(tokens, TRIO),
            heads(tokens, HEAD_WIDTH),
            heads(tokens, GROUP * HEAD_WIDTH),
            anywhere,
        ),
        scratch=[
            pltpu.VMEM((tokens, TRIO), jnp.float32),
            pltpu.VMEM(dims, jnp.bfloat16),
            pltpu.SemaphoreType.DMA((grid.count,)),
            pltpu.SemaphoreType.DMA((grid.count,)),
        ],
        vmem=VMEM_LESS,
    )(*arrays, normed, *tables, gain_q, gain_k)
    return kept, context, weight.reshape(grid.count * rows, depth)


def attention_backward(
    norms, scales, turns, value, grad_context, tables, gain_q, gain_k,
    normed, qkv_full, total, parts, first, rows_per_device,
):
    tokens, depth = normed.shape
    wide = GROUP * HEAD_WIDTH
    count = value.shape[1] // HEAD_WIDTH
    half = KEY_VALUE_HEADS // 2
    stretch = half * wide // (2 * rows_per_device)
    early = shape_of((1, stretch, rows_per_device, depth), jnp.bfloat16)
    late = shape_of((3, stretch, rows_per_device, depth), jnp.bfloat16)
    shapes = [late, late] if first >= half else [early, early, late, late]
    held = [] if total is None else [total, *parts]

    def part_scratch(rows):
        chips = max(rows // (2 * rows_per_device), 1)
        height = min(rows, rows_per_device)
        return pltpu.VMEM((2, chips, height, depth), jnp.bfloat16)

    anywhere = pl.BlockSpec(memory_space=pl.ANY)
    return kernel_call(
        functools.partial(attention_backward_kernel, first, rows_per_device, len(held)),
        "attention_backward",
        (count,),
        [
            heads(tokens, TRIO),
            heads(tokens, TRIO),
            heads(tokens, TRIO),
            heads(tokens, HEAD_WIDTH),
            heads(tokens, wide, first),
            *[in_vmem(table) for table in tables],
            in_vmem(gain_q),
            in_vmem(gain_k),
            in_vmem(normed),
            *qkv_rows_of(depth, first),
            *[in_vmem(total)] * min(len(held), 1),
            *[anywhere] * max(len(held) - 1, 0),
        ],
        (
            *shapes,
            shape_of((tokens, depth), jnp.float32),
            shape_of(gain_q.shape, jnp.float32),
            shape_of(gain_k.shape, jnp.float32),
        ),
        (*[anywhere] * len(shapes), in_vmem(normed), in_vmem(gain_q), in_vmem(gain_k)),
        scratch=[
            pltpu.VMEM((tokens, TRIO + HEAD_WIDTH), jnp.bfloat16),
            part_scratch(wide),
            part_scratch(HEAD_WIDTH),
            part_scratch(HEAD_WIDTH),
            pltpu.SemaphoreType.DMA((6,)),
        ],
        aliases={15 + slot: slot for slot in range(len(shapes))} if held else None,
        vmem=VMEM_LESS,
    )(
        norms, scales, turns, value, grad_context, *tables, gain_q, gain_k,
        normed, qkv_full, qkv_full, qkv_full, *held,
    )


ROW_TILE = 256
FF_TILE = 512
BACK_TILE = 384
STRIP = 64


def project_kernel(context, weight, residual, gain, middle, normed):
    middle[...] = residual[...] + contract_last(context[...], weight[...])

    @pl.loop(0, middle.shape[0] // STRIP)
    def _(strip):
        rows = pl.ds(pl.multiple_of(strip * STRIP, STRIP), STRIP)
        values = middle[rows, :]
        normed[rows, :] = (values * rms_scale(values) * gain[...]).astype(jnp.bfloat16)


def rows_of(array, tile):
    return pl.BlockSpec((tile, array.shape[1]), lambda k: (k, 0))


def project(context, weight, residual, gain):
    return kernel_call(
        project_kernel,
        "project",
        (residual.shape[0] // ROW_TILE,),
        [rows_of(context, ROW_TILE), whole(weight), rows_of(residual, ROW_TILE), whole(gain)],
        (shape_of(residual.shape, jnp.float32), shape_of(residual.shape, jnp.bfloat16)),
        (rows_of(residual, ROW_TILE), rows_of(residual, ROW_TILE)),
    )(context, weight, residual, gain)


def feed_kernel(grid, places_of, pieces_count, *refs):
    pieces, normed = refs[:pieces_count], refs[pieces_count]
    hidden, slope, lift, out, held, came, went = refs[pieces_count + 1 :]
    step = pl.program_id(0)
    rows = held.shape[1]
    tile = hidden.shape[1]
    each = tile // rows
    half = grid.count // 2

    @pl.when(step == 0)
    def _():
        for copy in arrivals(grid, places_of, pieces, held, came):
            copy.start()

    for number in range(each):
        for first in (0, half):
            device = first + step * each + number
            arrived(held, device, came).wait()
            leaving(held, device, out, went).start()
    weights = jnp.concatenate(
        [held[pl.ds(first + step * each, each)].reshape(tile, -1) for first in (0, half)], axis=0
    )
    both = contract_last(normed[...], weights)
    gate, upward = both[:, :tile], both[:, tile:]
    sigma = jax.nn.sigmoid(gate)
    lifted = gate * sigma
    lift[...] = lifted.astype(jnp.bfloat16)
    slope[...] = (upward * sigma * (1.0 + gate * (1.0 - sigma))).astype(jnp.bfloat16)
    hidden[...] = (lifted * upward).astype(jnp.bfloat16)

    @pl.when(step == pl.num_programs(0) - 1)
    def _():
        for device in range(grid.count):
            leaving(held, device, out, went).wait()


def columns_of(rows, tile, first=0):
    return pl.BlockSpec((rows, tile), lambda k: (0, first + k))


def gate_and_up(tile, depth, first=0):
    return pl.BlockSpec((2, tile, depth), lambda k: (0, first + k, 0))


def feed(grid, normed, own_pieces, swapped_pieces):
    arrays, places_of = gather_plan(own_pieces, swapped_pieces)
    tokens, depth = normed.shape
    rows = arrays[0].shape[1]
    columns = columns_of(tokens, BACK_TILE)
    anywhere = pl.BlockSpec(memory_space=pl.ANY)
    dims = (grid.count, rows, depth)
    hidden, slope, lift, weight = kernel_call(
        functools.partial(feed_kernel, grid, places_of, len(arrays)),
        "feed",
        (FF // BACK_TILE,),
        [*[anywhere] * len(arrays), whole(normed)],
        (
            shape_of((tokens, FF), jnp.bfloat16),
            shape_of((tokens, FF), jnp.bfloat16),
            shape_of((tokens, FF), jnp.bfloat16),
            shape_of(dims, jnp.bfloat16),
        ),
        (columns, columns, columns, anywhere),
        scratch=[
            pltpu.VMEM(dims, jnp.bfloat16),
            pltpu.SemaphoreType.DMA((grid.count,)),
            pltpu.SemaphoreType.DMA((grid.count,)),
        ],
    )(*arrays, normed)
    return hidden, slope, lift, weight.reshape(grid.count * rows, depth)


def finish_kernel(hidden, weight, residual, output):
    output[...] = residual[...] + contract_last(hidden[...], weight[...])


def finish(hidden, weight, residual):
    return kernel_call(
        finish_kernel,
        "finish",
        (residual.shape[0] // ROW_TILE,),
        [rows_of(hidden, ROW_TILE), whole(weight), rows_of(residual, ROW_TILE)],
        shape_of(residual.shape, jnp.float32),
        rows_of(residual, ROW_TILE),
    )(hidden, weight, residual)


def outer_kernel(rows_per_device, left, right, kept, sent, turned_left):
    @pl.when(pl.program_id(0) == 0)
    def _():
        turned_left[...] = left[...].T

    part = plain_product(turned_left[...], right[...]).astype(jnp.bfloat16)
    kept[...], sent[...] = by_core(rows_per_device, part)


def chip_columns(chips, rows, width):
    return pl.BlockSpec((chips, rows, width), lambda k: (0, 0, k))


def outer(left, right, rows_per_device):
    chips = left.shape[1] // (2 * rows_per_device)
    shape = shape_of((chips, rows_per_device, right.shape[1]), jnp.bfloat16)
    block = chip_columns(chips, rows_per_device, FF_TILE)
    return kernel_call(
        functools.partial(outer_kernel, rows_per_device),
        "outer",
        (right.shape[1] // FF_TILE,),
        [whole(left), columns_of(right.shape[0], FF_TILE)],
        (shape, shape),
        (block, block),
        scratch=[pltpu.VMEM((left.shape[1], left.shape[0]), jnp.bfloat16)],
    )(left, right)


def feed_backward_kernel(
    rows_per_device, grad_feed, down, slope, lift, normed, weights, *others
):
    kept, sent, total = others[-3:]

    @pl.when(pl.program_id(0) == 0)
    def _():
        total[...] = others[0][...] if len(others) > 3 else jnp.zeros_like(total)

    grad_hidden = plain_product(grad_feed[...], down[...])
    grads = jnp.concatenate(
        [
            (grad_hidden * slope[...].astype(jnp.float32)).astype(jnp.bfloat16),
            (grad_hidden * lift[...].astype(jnp.float32)).astype(jnp.bfloat16),
        ],
        axis=1,
    )
    tile = grad_hidden.shape[1]
    part = contract_first(grads, normed[...]).astype(jnp.bfloat16)
    for plane in range(2):
        kept[plane], sent[plane] = by_core(
            rows_per_device, part[plane * tile : (plane + 1) * tile, :]
        )
    total[...] += plain_product(grads, weights[...].reshape(2 * tile, -1))


def feed_backward(grad_feed, down, slope, lift, normed, weight, total, half, rows_per_device):
    tokens, depth = normed.shape
    tiles = FF // BACK_TILE
    count = tiles // 2
    first = half * count
    held = [] if total is None else [total]
    chips = BACK_TILE // (2 * rows_per_device)
    shape = shape_of((2, count * chips, rows_per_device, depth), jnp.bfloat16)
    block = pl.BlockSpec((2, chips, rows_per_device, depth), lambda k: (0, k, 0, 0))
    return kernel_call(
        functools.partial(feed_backward_kernel, rows_per_device),
        "feed_backward",
        (count,),
        [
            whole(grad_feed),
            columns_of(depth, BACK_TILE, first),
            columns_of(tokens, BACK_TILE, first),
            columns_of(tokens, BACK_TILE, first),
            whole(normed),
            gate_and_up(BACK_TILE, depth, first),
            *[whole(total) for total in held],
        ],
        (shape, shape, shape_of((tokens, depth), jnp.float32)),
        (block, block, pl.BlockSpec((tokens, depth), lambda k: (0, 0))),
    )(grad_feed, down, slope, lift, normed, weight.reshape(2, FF, depth), *held)


def project_backward_kernel(
    rows_per_device, grad_normed, middle, out_grad, gain, context, weight,
    kept, sent, grad_context, grad_middle, gain_terms, branch, turned_branch,
):
    step = pl.program_id(0)
    row_steps = branch.shape[0] // ROW_TILE

    @pl.when(step == 0)
    def _():
        gain_terms[...] = jnp.zeros_like(gain_terms)

    @pl.when(step < row_steps)
    def _():
        start = pl.multiple_of(step * ROW_TILE, ROW_TILE)

        @pl.loop(0, ROW_TILE // STRIP)
        def _(strip):
            rows = pl.ds(pl.multiple_of(strip * STRIP, STRIP), STRIP)
            values = middle[rows, :]
            grad, terms = norm_backward(values, rms_scale(values), gain[...], grad_normed[rows, :])
            grad = out_grad[rows, :] + grad
            grad_middle[rows, :] = grad
            branch[pl.ds(pl.multiple_of(start + strip * STRIP, STRIP), STRIP), :] = grad.astype(
                jnp.bfloat16
            )
            gain_terms[...] += jnp.sum(terms, axis=0, keepdims=True)

    @pl.when(step == row_steps)
    def _():
        turned_branch[...] = branch[...].T

    @pl.when(step >= row_steps)
    def _():
        part = plain_product(turned_branch[...], context[...]).astype(jnp.bfloat16)
        kept[...], sent[...] = by_core(rows_per_device, part)
        grad_context[...] = plain_product(branch[...], weight[...]).astype(jnp.bfloat16)


def project_backward(grad_normed, middle, out_grad, gain, context, weight, rows_per_device):
    tokens, depth = middle.shape
    width = context.shape[1]
    chips = depth // (2 * rows_per_device)
    shape = shape_of((chips, rows_per_device, width), jnp.bfloat16)
    row_steps = tokens // ROW_TILE

    def column(k):
        return jnp.maximum(k - row_steps, 0)

    def row_block(k):
        return (jnp.minimum(k, row_steps - 1), 0)

    rows = pl.BlockSpec((ROW_TILE, depth), row_block)
    block = pl.BlockSpec((chips, rows_per_device, FF_TILE), lambda k: (0, 0, column(k)))

    def columns(count):
        return pl.BlockSpec((count, FF_TILE), lambda k: (0, column(k)))

    return kernel_call(
        functools.partial(project_backward_kernel, rows_per_device),
        "project_backward",
        (row_steps + width // FF_TILE,),
        [rows, rows, rows, whole(gain), columns(tokens), columns(depth)],
        (
            shape,
            shape,
            shape_of((tokens, width), jnp.bfloat16),
            shape_of((tokens, depth), jnp.float32),
            shape_of(gain.shape, jnp.float32),
        ),
        (block, block, columns(tokens), rows, whole(gain)),
        scratch=[
            pltpu.VMEM((tokens, depth), jnp.bfloat16),
            pltpu.VMEM((depth, tokens), jnp.bfloat16),
        ],
    )(grad_normed, middle, out_grad, gain, context, weight)


def position_tables(segment_ids):
    _, micro_rows = segment_ids.shape
    order = jnp.arange(micro_rows, dtype=jnp.int32)
    same = segment_ids[:, :, None] == segment_ids[:, None, :]
    earlier = order[None, :] < order[:, None]
    positions = jnp.sum(jnp.where(same & earlier[None], 1, 0), axis=2).astype(jnp.int32)
    half_size = HEAD_WIDTH // 2
    frequency = ROPE_BASE ** (-(jnp.arange(half_size, dtype=jnp.float32) * (2.0 / HEAD_WIDTH)))
    angles = positions.reshape(-1, 1).astype(jnp.float32) * frequency[None, :]
    cosine, sine = jnp.cos(angles), jnp.sin(angles)
    allowed = same & (earlier | (order[None, :] == order[:, None]))[None]
    return (
        jnp.concatenate([cosine, cosine], axis=-1),
        jnp.concatenate([-sine, sine], axis=-1),
        jnp.where(allowed, 0.0, -1e30).astype(jnp.float32),
    )


def adamw(weight, first, second, grad, rate, decay):
    first_new = BETA_ONE * first + (1.0 - BETA_ONE) * grad
    second_new = BETA_TWO * second + (1.0 - BETA_TWO) * grad * grad
    corrected = (
        first_new
        / (1.0 - BETA_ONE**STEP)
        / (jnp.sqrt(second_new / (1.0 - BETA_TWO**STEP)) + ADAM_EPS)
    )
    return (weight - rate * (corrected + decay * weight), first_new, second_new)


def per_device(
    grid,
    activations,
    segment_ids,
    out_grad,
    qkv_weight,
    qkv_first,
    qkv_second,
    out_weight,
    out_first,
    out_second,
    gate_up_weight,
    gate_up_first,
    gate_up_second,
    down_weight,
    down_first,
    down_second,
    norm_gains,
    gains_first,
    gains_second,
):
    qkv_low = qkv_weight.astype(jnp.bfloat16)
    out_low = out_weight.astype(jnp.bfloat16)
    gate_up_low = gate_up_weight.astype(jnp.bfloat16)
    down_low = down_weight.astype(jnp.bfloat16)

    gain_count = norm_gains.shape[0]
    gain_start = lax.axis_index("dp") * gain_count
    all_gains = jnp.zeros((1, gain_count * grid.count), jnp.bfloat16)
    all_gains = lax.dynamic_update_slice(
        all_gains, norm_gains.astype(jnp.bfloat16)[None], (0, gain_start)
    )
    size = grid.size
    heads_of = KEY_VALUE_HEADS // 4
    out_rows, gate_rows = out_low.shape[0], gate_up_low.shape[0]
    qkv_rows, down_rows = qkv_low.shape[0], down_low.shape[0]

    tables = position_tables(segment_ids)
    scale_one = rms_scale(activations)
    v = Steps(out_low=out_low, gate_up_low=gate_up_low)
    v.qkv_line = z_pieces(grid, qkv_low, False)
    down_block = jnp.concatenate([down_low, rows_of_gains(all_gains, down_low.shape[1])], axis=0)
    down_sides = plane_sides(grid, down_block)
    down_corners = plane_corners(grid, down_sides, cut_at=down_rows)
    v.down_chip, v.gains, down_places = chip_plane(down_block, down_sides, down_corners, down_rows)
    v.close()

    v.qkv_column = jnp.stack(v.qkv_line)
    v.qkv_sides = plane_sides(grid, v.qkv_column)
    all_gains = v.gains.reshape(1, -1)[:, : gain_count * grid.count]
    out_block = jnp.concatenate([v.out_low, rows_of_gains(all_gains, out_low.shape[1])], axis=0)
    v.out_line = z_pieces(grid, out_block, False)
    v.grad_feed = out_grad.astype(jnp.bfloat16)
    v.drop("qkv_line", "out_low", "gains")
    v.close()

    grad_feed = v.grad_feed
    v.out_column = jnp.stack([piece[:out_rows] for piece in v.out_line])
    gains = sum(piece[out_rows:].astype(jnp.float32) for piece in v.out_line)
    gains = gains.reshape(1, -1)[:, : gain_count * grid.count]
    v.gains = gains
    v.qkv_corners = plane_corners(grid, v.qkv_sides)
    v.gate_up_moved = {1: grid.shift(v.gate_up_low, "z", 1)}
    v.qkv_sides_swapped = swap_tree(grid, v.qkv_sides)
    v.drop("grad_feed", "out_line")
    v.close()

    every = tuple(range(size["z"]))
    middle_plane = size["z"] // 2
    gains = small_sum(grid, v.gains, "c")
    gain_one, gain_two = gains[:, :D], gains[:, D : 2 * D]
    gain_query = gains[:, 2 * D : 2 * D + HEAD_WIDTH]
    gain_key = gains[:, 2 * D + HEAD_WIDTH :]
    normed_one = (activations * scale_one * gain_one).astype(jnp.bfloat16)
    qkv_column_swapped, qkv_corners_swapped = swap_tree(grid, (v.qkv_column, v.qkv_corners))
    v.out_sides = plane_sides(grid, v.out_column)
    v.near_column = jnp.stack([v.gate_up_low, v.gate_up_moved[1]])
    v.near_sides = plane_sides(grid, v.near_column)
    v.gate_up_moved[2] = grid.shift(v.gate_up_low, "z", 2)
    kept, context, qkv_full = first_attention(
        grid,
        normed_one,
        plane_pieces(every, v.qkv_column, v.qkv_sides, v.qkv_corners),
        plane_pieces(every, qkv_column_swapped, v.qkv_sides_swapped, qkv_corners_swapped),
        tables,
        gain_query,
        gain_key,
        heads_of,
    )
    v.drop("qkv_column", "qkv_sides", "qkv_corners", "gate_up_low", "gains")
    v.drop("qkv_sides_swapped")
    parts = [kept]

    def attention_part(part, context):
        *kept, context = attention(
            after(normed_one, *flat(context)),
            qkv_full,
            tables,
            gain_query,
            gain_key,
            context,
            part * heads_of,
            heads_of,
        )
        parts.append(kept)
        return context

    v.gate_up_moved[3] = grid.shift(
        after(gate_up_low, context, v.gate_up_moved[2]), "z", 3
    )
    v.context = attention_part(1, context)
    v.close()

    v.far_column = jnp.stack([v.gate_up_moved[2], v.gate_up_moved[3]])
    v.out_corners = plane_corners(grid, v.out_sides)
    v.far_sides = plane_sides(grid, v.far_column)
    v.down_moved = {1: grid.shift(v.down_chip, "z", 1)}
    v.context = attention_part(3, attention_part(2, v.context))
    v.drop("gate_up_moved")
    v.close()

    v.gate_up_corners = plane_corners(grid, (v.near_sides[0], v.far_sides[1]), halved=False)
    v.down_moved[3] = grid.shift(v.down_chip, "z", 3)
    out_swapped = swap_together(grid, (v.out_column, v.out_sides, v.out_corners))
    v.near_sides_swapped = swap_tree(grid, after_tree(v.near_sides, out_swapped))
    out_full = assemble(
        grid,
        plane_pieces(every, v.out_column, v.out_sides, v.out_corners),
        plane_pieces(every, *out_swapped),
    )
    v.far_sides_swapped = swap_tree(
        grid, after_tree(v.far_sides, out_full, v.near_sides_swapped)
    )
    middle, v.normed_two = project(v.context, out_full, activations, gain_two)
    context = v.context
    v.drop("out_column", "out_sides", "out_corners", "context")
    v.close()

    normed_two = v.normed_two
    corners_swapped = swap_tree(grid, v.gate_up_corners)
    columns_swapped = swap_tree(grid, (v.near_column, v.far_column))
    v.down_moved[2] = grid.shift(v.down_chip, "z", 2)
    near, far = every[:middle_plane], every[middle_plane:]
    v.hidden, v.slope, v.lift, gate_up_full = feed(
        grid,
        normed_two,
        plane_pieces(near, v.near_column, v.near_sides, {})
        + plane_pieces(far, v.far_column, v.far_sides, {})
        + corner_pieces(every, v.gate_up_corners),
        plane_pieces(near, columns_swapped[0], v.near_sides_swapped, {})
        + plane_pieces(far, columns_swapped[1], v.far_sides_swapped, {})
        + corner_pieces(every, corners_swapped),
    )
    early = after_tree(
        [v.down_chip, v.down_moved[1], v.down_moved[3]], corners_swapped, columns_swapped
    )
    v.down_swapped = swap_tree(grid, early)
    v.down_parts = outer(grad_feed, v.hidden, down_rows)
    v.drop("near_column", "far_column", "near_sides", "far_sides", "gate_up_corners", "normed_two")
    v.drop("near_sides_swapped", "far_sides_swapped")
    v.close()

    hidden, slope, lift = v.hidden, v.slope, v.lift
    down_line = [v.down_chip, *[v.down_moved[hops] for hops in grid.hops("z")]]
    own_swapped, one_swapped, three_swapped = v.down_swapped
    two_swapped = grid.shift(v.down_moved[2], "c", 1)
    down_line_swapped = [own_swapped, one_swapped, two_swapped, three_swapped]
    slots = [(axis, hops) for axis in "zyx" for hops in range(size[axis])]
    numbers = jnp.stack([grid.ahead(axis, hops) for axis, hops in slots]).astype(jnp.int32)

    def here(axis, hops):
        return Place(slots.index((axis, hops)))

    def in_planes(pair):
        return [
            part.reshape(-1, size["y"], size["x"], *part.shape[-2:]) for part in pair
        ]

    down_full = assemble(
        grid, line_pieces(down_line, down_places), line_pieces(down_line_swapped, down_places)
    )

    v.down_terms = swapped(grid, in_planes(after_tree(v.down_parts, two_swapped)))

    def feed_part(half, total):
        *pair, total = feed_backward(
            grad_feed, down_full, slope, lift, normed_two, gate_up_full, total, half, gate_rows
        )
        return pair, total

    v.even_parts, v.total = feed_part(0, None)
    v.drop("down_chip", "down_moved", "down_swapped", "down_parts", "hidden", "slope", "lift")
    v.close()

    merge = Merge(grid, numbers)
    down_one = line(merge, here, [(v.down_terms, every)], 1, lead=2)
    made = merge.run()
    v.down_moved = [Source(down_one(made))]
    v.even = swapped(grid, in_planes(v.even_parts))
    v.odd_parts, v.total = feed_part(1, v.total)
    v.drop("even_parts")
    v.close()

    merge = Merge(grid, numbers)
    even_corners = corners(merge, here, v.even)
    down_three = line(merge, here, [(v.down_terms, every)], 3, lead=2)
    made = merge.run()
    v.even_corners = even_corners(made)
    v.down_moved.append(Source(down_three(made)))
    v.odd = swapped(grid, in_planes(v.odd_parts))
    *v.out_parts, v.grad_context, v.grad_middle, v.gain_two_part = project_backward(
        v.total, middle, out_grad, gain_two, context, out_full, out_rows
    )
    v.drop("odd_parts", "total")
    v.close()

    low, high = halves_of(v.down_terms)
    grad_context, grad_middle, gain_two_part = v.grad_context, v.grad_middle, v.gain_two_part
    v.drop("grad_context", "grad_middle", "gain_two_part")
    merge = Merge(grid, numbers)
    even_sides = sides(merge, here, v.even, v.even_corners)
    down_two = line(merge, here, [(v.down_terms, every)], 2, rows=low, lead=2)
    made = merge.run()
    v.even = even_sides(made)
    v.down_moved.append(Source(down_two(made)))
    v.out_terms = swapped(grid, in_planes(v.out_parts))
    v.gain_terms = []

    def backward_part(part, rows, total):
        *v.rows, v.total, terms_q, terms_k = attention_backward(
            *parts[part],
            grad_context,
            tables,
            gain_query,
            gain_key,
            normed_one,
            qkv_full,
            total,
            rows,
            part * heads_of,
            qkv_rows,
        )
        v.gain_terms = v.gain_terms + [(terms_q, terms_k)]

    backward_part(0, [], None)
    v.drop("out_parts", "even_corners")
    v.close()

    merge = Merge(grid, numbers)
    odd_corners = corners(merge, here, v.odd)
    out_corners = corners(merge, here, v.out_terms)
    down_two = line(merge, here, [(v.down_terms, every)], 2, rows=high, lead=2)
    down_own = line(merge, here, [(v.down_terms, every)], 0, lead=2)
    made = merge.run()
    v.odd_corners = odd_corners(made)
    v.out_corners = out_corners(made)
    v.down_moved += [Source(down_two(made), high[0]), Source(down_own(made))]
    backward_part(1, v.rows, v.total)
    v.drop("down_terms")
    v.close()

    merge = Merge(grid, numbers)
    odd_sides = sides(merge, here, v.odd, v.odd_corners)
    down_corners = corners(merge, here, v.down_moved, lead=0)
    made = merge.run()
    v.odd = odd_sides(made)
    v.down_corners = down_corners(made)
    v.first = swapped(grid, in_planes(v.rows[:2]))
    backward_part(2, v.rows[2:], v.total)
    v.drop("odd_corners")
    v.close()

    gate_up_groups = [(v.even, (0, 2)), (v.odd, (1, 3))]
    merge = Merge(grid, numbers)
    out_sides = sides(merge, here, v.out_terms, v.out_corners)
    gate_up_lines = [line(merge, here, gate_up_groups, hops) for hops in (1, 3, 0)]
    made = merge.run()
    v.out_terms = out_sides(made)
    v.gate_up_moved = [go(made) for go in gate_up_lines]
    backward_part(3, v.rows, v.total)
    v.drop("out_corners")
    v.close()

    v.last = swapped(grid, in_planes(v.rows))
    merge = Merge(grid, numbers)
    first_corners = corners(merge, here, v.first)
    down_sides = sides(merge, here, v.down_moved, v.down_corners, lead=0)
    made = merge.run()
    v.first_corners = first_corners(made)
    v.down_terms = down_sides(made)
    total, gain_terms = v.total, v.gain_terms
    grad_block, gain_one_terms = norm_backward(activations, scale_one, gain_one, after(total, made))
    v.gains_part = jnp.concatenate(
        [
            jnp.sum(gain_one_terms, axis=0, keepdims=True),
            gain_two_part,
            sum(terms for terms, _ in gain_terms),
            sum(terms for _, terms in gain_terms),
        ],
        axis=1,
    )
    v.drop("rows", "total", "gain_terms", "down_moved", "down_corners")
    v.close()

    gate_up_groups = [(v.even, (0, 2)), (v.odd, (1, 3))]
    merge = Merge(grid, numbers)
    last_corners = corners(merge, here, v.last)
    first_sides = sides(merge, here, v.first, v.first_corners)
    gate_up_two = line(merge, here, gate_up_groups, 2)
    made = merge.run()
    v.last_corners = last_corners(made)
    v.first = first_sides(made)
    v.gate_up_moved.append(gate_up_two(made))
    v.layer_output = finish(after(hidden, made), down_full, middle)
    v.gains_part = small_sum(grid, v.gains_part, "c")
    v.total = total
    v.drop("even", "odd", "first_corners")
    v.close()

    merge = Merge(grid, numbers)
    last_sides = sides(merge, here, v.last, v.last_corners)
    out_lines = [line(merge, here, [(v.out_terms, every)], hops) for hops in range(size["z"])]
    made = merge.run()
    v.last = last_sides(made)
    v.out_moved = [go(made) for go in out_lines]
    v.gains_part = small_sum(grid, after(v.gains_part, v.out_moved), "z")
    v.gate_up_new = adamw(
        gate_up_weight, gate_up_first, gate_up_second, total_of(*v.gate_up_moved), 0.06, 0.1
    )
    down_total = total_of(*[term.array for term in v.down_terms])
    v.down_new = adamw(down_weight, down_first, down_second, down_total, 0.04, 0.1)
    grad_block, _ = norm_backward(activations, scale_one, gain_one, after(v.total, made))
    v.input_grad = grad_middle + grad_block
    v.drop("last_corners", "gate_up_moved", "down_terms", "out_terms", "total")
    v.close()

    qkv_groups = [(v.first, (0,)), (v.last, (1, 2, 3))]
    merge = Merge(grid, numbers)
    qkv_lines = [line(merge, here, qkv_groups, hops) for hops in range(size["z"])]
    made = merge.run()
    qkv_total = total_of(*[go(made) for go in qkv_lines])
    out_new = adamw(out_weight, out_first, out_second, total_of(*v.out_moved), 0.25, 0.1)
    gains_total = small_sum(grid, v.gains_part, "xy")
    gains_total = lax.dynamic_slice(gains_total, (0, gain_start), (1, gain_count))[0]

    return (
        v.layer_output,
        v.input_grad,
        *adamw(qkv_weight, qkv_first, qkv_second, qkv_total, 0.06, 0.1),
        *out_new,
        *v.gate_up_new,
        *v.down_new,
        *adamw(norm_gains, gains_first, gains_second, gains_total, 0.3, 0.0),
    )


def solution(mesh):
    return jax.shard_map(
        functools.partial(per_device, Grid(mesh.shape["dp"])),
        mesh=mesh,
        in_specs=(
            P("dp", None),
            P("dp", None),
            P("dp", None),
            P("dp", None),
            P("dp", None),
            P("dp", None),
            P("dp", None),
            P("dp", None),
            P("dp", None),
            P("dp", None),
            P("dp", None),
            P("dp", None),
            P("dp", None),
            P("dp", None),
            P("dp", None),
            P("dp"),
            P("dp"),
            P("dp"),
        ),
        out_specs=(
            P("dp", None),
            P("dp", None),
            P("dp", None),
            P("dp", None),
            P("dp", None),
            P("dp", None),
            P("dp", None),
            P("dp", None),
            P("dp", None),
            P("dp", None),
            P("dp", None),
            P("dp", None),
            P("dp", None),
            P("dp", None),
            P("dp"),
            P("dp"),
            P("dp"),
        ),
        check_vma=False,
    )
```

```python
import functools
import itertools
import math

import jax
import jax.numpy as jnp
from jax import lax
from jax.experimental import pallas as pl
from jax.experimental.pallas import tpu as pltpu
from jax.sharding import PartitionSpec as P

D = 1024
QUERY_HEADS = 16
KEY_VALUE_HEADS = 8
HEAD_WIDTH = 128
FF = 3072
STEP = 10


NORM_EPS = 1e-06
ROPE_BASE = 1000000.0
BETA_ONE = 0.9
BETA_TWO = 0.95
ADAM_EPS = 1e-08


def contract_last(left_side, right_side):
    return lax.dot_general(
        left_side, right_side, (((1,), (1,)), ((), ())), preferred_element_type=jnp.float32
    )


def contract_first(left_side, right_side):
    return lax.dot_general(
        left_side, right_side, (((0,), (0,)), ((), ())), preferred_element_type=jnp.float32
    )


def plain_product(left_side, right_side):
    return jnp.dot(left_side, right_side, preferred_element_type=jnp.float32)


def rms_scale(values):
    return lax.rsqrt(jnp.mean(values * values, axis=-1, keepdims=True) + NORM_EPS)


class Grid:
    def __init__(self, count):
        chips = count // 2
        flat = 2 if chips <= 16 else 4
        self.size = {"z": chips // (flat * flat), "y": flat, "x": flat, "c": 2}
        self.step = {"z": 2 * flat * flat, "y": 2 * flat, "x": 2, "c": 1}
        self.count = count

    def at(self, axis):
        return (lax.axis_index("dp") // self.step[axis]) % self.size[axis]

    def ahead(self, axis, hops):
        return (self.at(axis) + hops) % self.size[axis]

    def hops(self, axis):
        return range(1, self.size[axis])

    def shift(self, value, axis, hops):
        size, step = self.size[axis], self.step[axis]
        pairs = []
        for device in range(self.count):
            here = (device // step) % size
            pairs.append((device, device + ((here + hops) % size - here) * step))
        return lax.ppermute(value, "dp", pairs)


def after(value, *others):
    return lax.optimization_barrier((value, *jax.tree.leaves(others)))[0]


GROUP = QUERY_HEADS // KEY_VALUE_HEADS
SCORE_SCALE = HEAD_WIDTH ** (-0.5)
EXP2_SCALE = SCORE_SCALE * math.log2(math.e)
VMEM_BYTES = 60 * 1024 * 1024
VMEM_LESS = 50 * 1024 * 1024
VMEM_OF = {name: 46 * 1024 * 1024 for name in ("finish", "outer", "project")}


def norm_backward(values, scale_rows, gain, grad_out):
    scaled = gain * grad_out
    grad_in = scale_rows * scaled - values * scale_rows**3 * jnp.mean(
        scaled * values, axis=-1, keepdims=True
    )
    return (grad_in, grad_out * values * scale_rows)


def z_pieces(grid, shard, chained, *dependencies):
    moved = [shard]
    for hops in grid.hops("z"):
        moved.append(grid.shift(after(shard, *dependencies) if dependencies else shard, "z", hops))
        if chained:
            dependencies = (moved[-1],)
    return moved


def swap_tree(grid, buffers):
    return jax.tree.map(lambda buffer: grid.shift(buffer, "c", 1), buffers)


def swap_together(grid, buffers):
    leaves, shape = jax.tree.flatten(buffers)
    moved = grid.shift(jnp.concatenate(leaves, axis=0), "c", 1)
    starts = itertools.accumulate([0] + [leaf.shape[0] for leaf in leaves])
    return jax.tree.unflatten(
        shape, [Part(moved, start, leaf.shape[0]) for start, leaf in zip(starts, leaves)]
    )


@jax.tree_util.register_pytree_node_class
class Part:
    def __init__(self, array, start, count):
        self.array, self.start, self.count = array, start, count

    def tree_flatten(self):
        return (self.array,), (self.start, self.count)

    @classmethod
    def tree_unflatten(cls, held, leaves):
        return cls(*leaves, *held)


def plane_sides(grid, column, *dependencies):
    sent = after(column, *dependencies) if dependencies else column
    from_x = {hops: grid.shift(sent, "x", hops) for hops in grid.hops("x")}
    from_y = {hops: grid.shift(sent, "y", hops) for hops in grid.hops("y")}
    return from_x, from_y


def plane_corners(grid, sides, *dependencies, halved=True, cut_at=None):
    from_x, from_y = sides
    half = from_x[1].shape[0] // 2 if cut_at is None else cut_at
    corners = {}
    for j in from_x:
        for l in from_y:
            first, second = from_x[j], from_y[l]
            if halved:
                first, second = first[:half], second[half:]
            if dependencies:
                first, second = after(first, *dependencies), after(second, *dependencies)
            corners[j, l] = (grid.shift(first, "y", l), grid.shift(second, "x", j))
    return corners


def corner_pieces(planes, corners):
    half = len(planes) // 2
    pieces = []
    for (j, l), (first, second) in corners.items():
        pieces.append((first, [{"z": hops, "x": j, "y": l} for hops in planes[:half]]))
        pieces.append((second, [{"z": hops, "x": j, "y": l} for hops in planes[half:]]))
    return pieces


def plane_pieces(planes, column, sides, corners):
    from_x, from_y = sides
    pieces = [(column, [{"z": hops} for hops in planes])]
    pieces += [(from_x[j], [{"z": hops, "x": j} for hops in planes]) for j in from_x]
    pieces += [(from_y[l], [{"z": hops, "y": l} for hops in planes]) for l in from_y]
    return pieces + corner_pieces(planes, corners)


def after_tree(tree, *dependencies):
    leaves, shape = jax.tree.flatten(tree)
    tied = lax.optimization_barrier((*leaves, *flat(dependencies)))
    return jax.tree.unflatten(shape, tied[: len(leaves)])


def flat(*groups):
    return [leaf for leaf in jax.tree.leaves(groups)]


def rows_of_gains(gains, width):
    rows = -(-gains.shape[1] // width)
    block = jnp.pad(gains, ((0, 0), (0, rows * width - gains.shape[1]))).reshape(rows, width)
    return jnp.pad(block, ((0, 16 - rows), (0, 0)))


def chip_plane(block, sides_received, corners_received, rows):
    from_x, from_y = sides_received
    blocks = [block, *from_x.values(), *from_y.values()]
    shards = [part[:rows] for part in blocks]
    below = [part[rows:] for part in blocks]
    places = [{}] + [{"x": j} for j in from_x] + [{"y": l} for l in from_y]
    for (j, l), (shard, rest) in corners_received.items():
        shards.append(shard)
        below.append(rest)
        places.append({"x": j, "y": l})
    return jnp.stack(shards), sum(below), places


def arrivals(grid, places_of, pieces, held, came):
    copies = []
    for which, first, places in places_of:
        for slot, place in enumerate(places, first):
            index = 0
            for axis in ("z", "y", "x", "c"):
                size = grid.size[axis]
                index = index + (grid.at(axis) + size - place.get(axis, 0)) % size * grid.step[axis]
            copies.append(
                pltpu.make_async_copy(pieces[which].at[slot], held.at[index], came.at[index])
            )
    return copies


def arrived(held, device, came):
    return pltpu.make_async_copy(held.at[device], held.at[device], came.at[device])


def leaving(held, device, out, went):
    return pltpu.make_async_copy(held.at[device], out.at[device], went.at[device])


def assemble_kernel(grid, places_of, *refs):
    pieces, (out, held, came, went) = refs[:-4], refs[-4:]
    for copy in arrivals(grid, places_of, pieces, held, came):
        copy.start()
    for device in range(grid.count):
        arrived(held, device, came).wait()
        leaving(held, device, out, went).start()
    for device in range(grid.count):
        leaving(held, device, out, went).wait()


def line_pieces(line, places):
    return [
        (buffer, [dict(place, z=hops) for place in places]) for hops, buffer in enumerate(line)
    ]


def gather_plan(own_pieces, swapped_pieces):
    pieces = own_pieces + [
        (buffer, [dict(place, c=1) for place in places]) for buffer, places in swapped_pieces
    ]
    arrays, places_of = [], []
    for buffer, places in pieces:
        array, first = (buffer.array, buffer.start) if isinstance(buffer, Part) else (buffer, 0)
        which = next((at for at, known in enumerate(arrays) if known is array), len(arrays))
        if which == len(arrays):
            arrays.append(array)
        places_of.append((which, first, places))
    return arrays, places_of


def assemble(grid, own_pieces, swapped_pieces):
    arrays, places_of = gather_plan(own_pieces, swapped_pieces)
    rows, width = arrays[0].shape[1:]
    dims = (grid.count, rows, width)
    gathered = pl.pallas_call(
        functools.partial(assemble_kernel, grid, places_of),
        out_shape=jax.ShapeDtypeStruct(dims, jnp.bfloat16),
        in_specs=[pl.BlockSpec(memory_space=pl.ANY)] * len(arrays),
        out_specs=pl.BlockSpec(memory_space=pl.ANY),
        scratch_shapes=[
            pltpu.VMEM(dims, jnp.bfloat16),
            pltpu.SemaphoreType.DMA((grid.count,)),
            pltpu.SemaphoreType.DMA((grid.count,)),
        ],
        compiler_params=pltpu.CompilerParams(vmem_limit_bytes=VMEM_BYTES),
        cost_estimate=LITTLE,
        name="assemble",
    )(*arrays)
    return gathered.reshape(grid.count * rows, width)


@jax.tree_util.register_pytree_node_class
class Source:
    def __init__(self, array, first=0):
        self.array, self.first = array, first

    def tree_flatten(self):
        return (self.array,), self.first

    @classmethod
    def tree_unflatten(cls, first, leaves):
        return cls(*leaves, first)


class Place:
    def __init__(self, slot, table=None):
        self.slot, self.table = slot, table

    def of(self, numbers):
        here = numbers[self.slot]
        if self.table is None:
            return here
        return sum(jnp.where(here == at, entry, 0) for at, entry in enumerate(self.table))

    def __eq__(self, other):
        return isinstance(other, Place) and (self.slot, self.table) == (other.slot, other.table)

    def __hash__(self):
        return hash((self.slot, self.table))


class Merge:
    STRIP = 16
    STEPS = 2

    def __init__(self, grid, numbers):
        self.grid, self.numbers = grid, numbers
        self.inputs, self.outputs, self.keys = [], [], {}

    def cut(self, array, places):
        key = (id(array), places)
        if key not in self.keys:
            self.keys[key] = len(self.inputs)
            self.inputs.append((array, places))
        return self.keys[key]

    def terms(self, sources, places, low, high):
        found = []
        for source in sources:
            first = source.first
            if first <= low and high <= first + source.array.shape[-2]:
                found.append((self.cut(source.array, places), low - first, high - first))
        return found

    def add(self, *options, chosen=None):
        self.outputs.append((options, chosen))
        return len(self.outputs) - 1

    def shape(self, options):
        array, places = self.inputs[options[0][0][0][0]]
        lead = [size for size, place in zip(array.shape, places) if place is None]
        rows = sum(segment[0][2] - segment[0][1] for segment in options[0])
        return (*lead, rows, array.shape[-1])

    def run(self):
        edges = [
            edge
            for options, _ in self.outputs
            for segments in options
            for segment in segments
            for term in segment
            for edge in term[1:]
        ]
        if any(edge % self.STRIP for edge in edges):
            return self.run_plain()
        shapes = [self.shape(options) for options, _ in self.outputs]
        def spec(array, places):
            block = [
                None if place is not None else size for size, place in zip(array.shape, places)
            ]
            return pl.BlockSpec(
                (*block, array.shape[-2], array.shape[-1] // self.STEPS),
                lambda step, held: (
                    *[0 if place is None else place.of(held) for place in places], 0, step
                ),
            )

        return pl.pallas_call(
            self.kernel,
            grid_spec=pltpu.PrefetchScalarGridSpec(
                num_scalar_prefetch=1,
                grid=(self.STEPS,),
                in_specs=[spec(*pair) for pair in self.inputs],
                out_specs=[
                    pl.BlockSpec(
                        (*dims[:-1], dims[-1] // self.STEPS),
                        lambda step, held, axes=len(dims): (0,) * (axes - 1) + (step,),
                    )
                    for dims in shapes
                ],
            ),
            out_shape=[jax.ShapeDtypeStruct(dims, jnp.bfloat16) for dims in shapes],
            compiler_params=pltpu.CompilerParams(vmem_limit_bytes=VMEM_LESS),
            cost_estimate=LITTLE,
            name="merge",
        )(self.numbers, *[array for array, _ in self.inputs])

    def kernel(self, held, *refs):
        inputs, outputs = refs[: len(self.inputs)], refs[len(self.inputs) :]
        for out, (options, chosen) in zip(outputs, self.outputs):
            for number, segments in enumerate(options):
                write = functools.partial(self.write, out, segments, inputs)
                if chosen is None:
                    write()
                else:
                    pl.when(chosen.of(held) == number)(write)

    def write(self, out, segments, inputs):
        start = 0
        for segment in segments:
            count = segment[0][2] - segment[0][1]
            strips = count // self.STRIP
            unroll = max(part for part in range(1, 9) if strips % part == 0)
            for lead in itertools.product(*[range(size) for size in out.shape[:-2]]):

                @pl.loop(0, strips, unroll=unroll)
                def _(strip, start=start, lead=lead, segment=segment):
                    def rows(first):
                        at = pl.multiple_of(first + strip * self.STRIP, self.STRIP)
                        return (*lead, pl.ds(at, self.STRIP), slice(None))

                    added = sum(inputs[k][rows(low)].astype(jnp.float32) for k, low, _ in segment)
                    out[rows(start)] = added.astype(jnp.bfloat16)

            start += count

    def run_plain(self):
        def part(term):
            array, places = self.inputs[term[0]]
            axis = 0
            for place in places:
                if place is None:
                    axis += 1
                else:
                    array = lax.dynamic_index_in_dim(
                        array, place.of(self.numbers), axis, keepdims=False
                    )
            return lax.slice_in_dim(array, term[1], term[2], axis=-2 + array.ndim)

        results = []
        for options, chosen in self.outputs:
            made = []
            for segments in options:
                sums = [
                    sum(part(term).astype(jnp.float32) for term in segment).astype(jnp.bfloat16)
                    for segment in segments
                ]
                made.append(jnp.concatenate(sums, axis=-2) if len(sums) > 1 else sums[0])
            results.append(made[0])
            for number in range(1, len(made)):
                results[-1] = jnp.where(chosen.of(self.numbers) == number, made[number], results[-1])
        return results


def swapped(grid, kept_and_sent):
    kept, sent = kept_and_sent
    return [Source(kept), Source(grid.shift(sent, "c", 1))]


def halves_of(sources):
    rows = sources[0].array.shape[-2]
    return (0, rows // 2), (rows // 2, rows)


def corners(merge, here, sources, lead=1):
    low, high = halves_of(sources)
    grid, whole_axes = merge.grid, (None,) * lead
    slots = {}
    for j in grid.hops("x"):
        for l in grid.hops("y"):
            place = (*whole_axes, here("y", l), here("x", j))
            slots[j, l] = (
                merge.add([merge.terms(sources, place, *low)]),
                merge.add([merge.terms(sources, place, *high)]),
            )

    def go(made):
        return {
            (j, l): (grid.shift(made[first], "x", j), grid.shift(made[second], "y", l))
            for (j, l), (first, second) in slots.items()
        }

    return go


def sides(merge, here, sources, crossed, lead=1):
    low, high = halves_of(sources)
    grid, whole_axes = merge.grid, (None,) * lead
    own_place = (*whole_axes, here("y", 0), here("x", 0))
    bare = (None,) * lead
    own = merge.add([merge.terms(sources, own_place, *half) for half in (low, high)])
    to_x, to_y = {}, {}
    for j in grid.hops("x"):
        place = (*whole_axes, here("y", 0), here("x", j))
        received = [Source(crossed[j, l][1], high[0]) for l in grid.hops("y")]
        to_x[j] = merge.add(
            [
                merge.terms(sources, place, *low),
                merge.terms(sources, place, *high) + merge.terms(received, bare, *high),
            ]
        )
    for l in grid.hops("y"):
        place = (*whole_axes, here("y", l), here("x", 0))
        received = [Source(crossed[j, l][0]) for j in grid.hops("x")]
        to_y[l] = merge.add(
            [
                merge.terms(sources, place, *low) + merge.terms(received, bare, *low),
                merge.terms(sources, place, *high),
            ]
        )

    def go(made):
        terms = [made[own]]
        terms += [grid.shift(made[to_x[j]], "x", j) for j in to_x]
        terms += [grid.shift(made[to_y[l]], "y", l) for l in to_y]
        return [Source(term) for term in terms]

    return go


def line(merge, here, groups, hops, rows=None, lead=0):
    grid = merge.grid
    plane = here("z", hops)
    owner = {
        number: (group, at)
        for group, (_, planes) in enumerate(groups)
        for at, number in enumerate(planes)
    }
    numbers = range(grid.size["z"])
    options = []
    for group, (sources, _) in enumerate(groups):
        index = Place(
            plane.slot, tuple(owner[n][1] if owner[n][0] == group else 0 for n in numbers)
        )
        place = (index, *(None,) * lead)
        parts = halves_of(sources) if rows is None else (rows,)
        options.append([merge.terms(sources, place, *part) for part in parts])
    chosen = Place(plane.slot, tuple(owner[n][0] for n in numbers)) if len(groups) > 1 else None
    slot = merge.add(*options, chosen=chosen)
    return lambda made: grid.shift(made[slot], "z", hops) if hops else made[slot]


def total_of(*terms):
    return sum(term.astype(jnp.float32) for term in terms)


class Steps:
    def __init__(self, **live):
        self.__dict__.update(live)

    def close(self):
        self.__dict__.update(after_tree(dict(self.__dict__)))

    def drop(self, *names):
        for name in names:
            del self.__dict__[name]


def small_sum(grid, value, axes):
    for axis in axes:
        value = value + sum(grid.shift(value, axis, hops) for hops in grid.hops(axis))
    return value


LITTLE = pl.CostEstimate(flops=1, bytes_accessed=1, transcendentals=0)


def whole(array):
    return pl.BlockSpec(array.shape, lambda *k: (0,) * array.ndim)


def in_vmem(array):
    return pl.BlockSpec(memory_space=pltpu.VMEM)


def kernel_call(
    body, name, grid, in_specs, out_shape, out_specs, scratch=(), aliases=None, vmem=VMEM_BYTES
):
    return pl.pallas_call(
        body,
        grid=grid,
        in_specs=in_specs,
        out_shape=out_shape,
        out_specs=out_specs,
        scratch_shapes=scratch,
        input_output_aliases=aliases or {},
        compiler_params=pltpu.CompilerParams(vmem_limit_bytes=VMEM_OF.get(name, vmem)),
        cost_estimate=LITTLE,
        name=name,
    )


def shape_of(dims, dtype):
    return jax.ShapeDtypeStruct(dims, dtype)


TRIO = (GROUP + 1) * HEAD_WIDTH


def lanes_of(head):
    return slice(head * HEAD_WIDTH, (head + 1) * HEAD_WIDTH)


def turned(values):
    return pltpu.roll(values, HEAD_WIDTH // 2, 1)


def stacked(values, rows, heads=GROUP):
    return jnp.concatenate([values[rows, lanes_of(g)] for g in range(heads)], axis=0)


def query_blocks(micro_rows):
    half = micro_rows // 2
    return [(0, half), (half, micro_rows)]


def powers_of(queries, keys, bias):
    return jnp.exp2(contract_last(queries, keys) * EXP2_SCALE + bias)


def group_bias(bias, micro, begin, end):
    return jnp.concatenate([bias[micro, begin:end, :end]] * GROUP, axis=0)


def attention_kernel(normed, wq, wk, wv, cosine, sine, bias, gain_q, gain_k, *outputs):
    keys_values = jnp.concatenate([wk[...], wv[...]], axis=0)
    attend(normed, wq[...], keys_values, cosine, sine, bias, gain_q, gain_k, *outputs[-6:])


def first_attention_kernel(grid, places_of, pieces_count, head_count, *refs):
    pieces, (normed, *tables) = refs[:pieces_count], refs[pieces_count : pieces_count + 6]
    *outputs, out, raw, held, came, went = refs[pieces_count + 6 :]
    step = pl.program_id(0)
    rows = held.shape[1]
    stretches = [
        (0, GROUP * HEAD_WIDTH),
        (QUERY_HEADS * HEAD_WIDTH, HEAD_WIDTH),
        ((QUERY_HEADS + KEY_VALUE_HEADS) * HEAD_WIDTH, HEAD_WIDTH),
    ]

    @pl.when(step == 0)
    def _():
        for copy in arrivals(grid, places_of, pieces, held, came):
            copy.start()

    def pass_on(device):
        arrived(held, device, came).wait()
        leaving(held, device, out, went).start()

    weights, early = [], set()
    for first, count in stretches:
        each = count // rows
        device = first // rows + step * each
        for number in range(each):
            pass_on(device + number)
        weights.append(held[pl.ds(device, each)].reshape(count, held.shape[2]))
        early |= set(range(first // rows, first // rows + head_count * each))
    keys_values = jnp.concatenate(weights[1:], axis=0)
    attend(normed, weights[0], keys_values, *tables, *outputs, raw)

    @pl.when(step == head_count - 1)
    def _():
        for device in range(grid.count):
            if device not in early:
                pass_on(device)
        for device in range(grid.count):
            leaving(held, device, out, went).wait()


def attend(
    normed, wq, keys_values, cosine, sine, bias, gain_q, gain_k,
    norms, scales, turns, value, context, held,
):
    held[:, : GROUP * HEAD_WIDTH] = contract_last(normed[...], wq)
    both = contract_last(normed[...], keys_values)
    held[:, GROUP * HEAD_WIDTH :] = both[:, :HEAD_WIDTH]
    value[...] = both[:, HEAD_WIDTH:].astype(jnp.bfloat16)
    micro_count, micro_rows, _ = bias.shape
    for micro in range(micro_count):
        start = micro * micro_rows
        rows = slice(start, start + micro_rows)
        for head in range(GROUP + 1):
            raw = held[rows, lanes_of(head)]
            scale = lax.rsqrt(jnp.mean(raw * raw, axis=-1, keepdims=True) + NORM_EPS)
            scale = jnp.broadcast_to(scale, raw.shape)
            normal = raw * scale
            gained = normal * (gain_q[...] if head < GROUP else gain_k[...])
            norms[rows, lanes_of(head)] = normal.astype(jnp.bfloat16)
            scales[rows, lanes_of(head)] = scale.astype(jnp.bfloat16)
            turns[rows, lanes_of(head)] = (
                gained * cosine[rows, :] + turned(gained) * sine[rows, :]
            ).astype(jnp.bfloat16)
        keys = turns[rows, lanes_of(GROUP)]
        for begin, end in query_blocks(micro_rows):
            block = slice(start + begin, start + end)
            count = end - begin
            powers = powers_of(
                stacked(turns, block), keys[:end], group_bias(bias, micro, begin, end)
            )
            inverse = 1.0 / jnp.sum(powers, axis=-1, keepdims=True)
            probs = (powers * inverse).astype(jnp.bfloat16)
            mixed = plain_product(probs, value[start : start + end, :]).astype(jnp.bfloat16)
            for g in range(GROUP):
                context[block, lanes_of(g)] = mixed[g * count : (g + 1) * count, :]


def with_turn(values):
    return jnp.concatenate([values, turned(values)], axis=1)


def head_backward(normal, scale, gain, grad, cos, sin):
    normal, scale = normal.astype(jnp.float32), scale.astype(jnp.float32)
    grad_normed = (grad[:, :HEAD_WIDTH] * cos - grad[:, HEAD_WIDTH:] * sin) * SCORE_SCALE
    scaled = gain * grad_normed
    terms = grad_normed * normal
    mean = jnp.mean(scaled * normal, axis=-1, keepdims=True)
    grad_raw = scale * (scaled - normal * mean)
    return grad_raw.astype(jnp.bfloat16), jnp.sum(terms, axis=0, keepdims=True)


def put_by_core(rows_per_device, result, part, at, plane, kept, sent, sems, sem):
    rows = result.shape[0]
    if rows >= 2 * rows_per_device:
        chips = rows // (2 * rows_per_device)
        part[0], part[1] = by_core(rows_per_device, result)
        stretch = pl.ds(at * chips, chips)
        return [
            pltpu.make_async_copy(part.at[0], kept.at[plane, stretch], sems.at[sem]),
            pltpu.make_async_copy(part.at[1], sent.at[plane, stretch], sems.at[sem + 1]),
        ]
    part[0, 0] = result
    mine = (at + lax.axis_index("dp")) % 2 == 0
    return [
        Either(
            mine,
            pltpu.make_async_copy(part.at[0, 0], kept.at[plane, at // 2], sems.at[sem]),
            pltpu.make_async_copy(part.at[0, 0], sent.at[plane, at // 2], sems.at[sem + 1]),
        )
    ]


class Either:
    def __init__(self, first_one, first, second):
        self.first_one, self.first, self.second = first_one, first, second

    def start(self):
        pl.when(self.first_one)(self.first.start)
        pl.when(jnp.logical_not(self.first_one))(self.second.start)

    def wait(self):
        pl.when(self.first_one)(self.first.wait)
        pl.when(jnp.logical_not(self.first_one))(self.second.wait)


def attention_backward_kernel(
    first, rows_per_device, held, norms, scales, turns, value, grad_context, cosine, sine, bias,
    gain_q, gain_k, normed, wq, wk, wv, *others,
):
    grad_raw_all, part_q, part_k, part_v, sems = others[-5:]
    kv_kept, kv_sent, total, terms_q, terms_k = others[-10:-5]

    @pl.when(pl.program_id(0) == 0)
    def _():
        terms_q[...] = jnp.zeros_like(terms_q)
        terms_k[...] = jnp.zeros_like(terms_k)
        if held:
            total[...] = others[0][...]
        else:
            total[...] = jnp.zeros_like(total)

    micro_count, micro_rows, _ = bias.shape
    for micro in range(micro_count):
        start = micro * micro_rows
        rows = slice(start, start + micro_rows)
        keys = turns[rows, lanes_of(GROUP)]
        both_keys = with_turn(keys)
        grad_values, grad_keys = 0.0, 0.0
        for begin, end in query_blocks(micro_rows):
            block = slice(start + begin, start + end)
            count = end - begin
            cos, sin = cosine[block, :], sine[block, :]
            queries = stacked(turns, block)
            powers = powers_of(queries, keys[:end], group_bias(bias, micro, begin, end))
            probs = powers * (1.0 / jnp.sum(powers, axis=-1, keepdims=True))
            grads = stacked(grad_context, block)
            grad_probs = contract_last(grads, value[start : start + end, :])
            weighted = probs * grad_probs
            centre = jnp.sum(weighted, axis=-1, keepdims=True)
            grad_scores = (weighted - probs * centre).astype(jnp.bfloat16)
            pad = ((0, micro_rows - end), (0, 0))
            grad_values += jnp.pad(contract_first(probs.astype(jnp.bfloat16), grads), pad)
            grad_keys += jnp.pad(contract_first(grad_scores, with_turn(queries)), pad)
            grad_queries = plain_product(grad_scores, both_keys[:end])
            for g in range(GROUP):
                grad_raw, terms = head_backward(
                    norms[block, lanes_of(g)],
                    scales[block, lanes_of(g)],
                    gain_q[...],
                    grad_queries[g * count : (g + 1) * count, :],
                    cos,
                    sin,
                )
                grad_raw_all[block, lanes_of(g)] = grad_raw
                terms_q[...] += terms
        grad_raw_all[rows, lanes_of(GROUP + 1)] = grad_values.astype(jnp.bfloat16)
        grad_raw, terms = head_backward(
            norms[rows, lanes_of(GROUP)],
            scales[rows, lanes_of(GROUP)],
            gain_k[...],
            grad_keys,
            cosine[rows, :],
            sine[rows, :],
        )
        grad_raw_all[rows, lanes_of(GROUP)] = grad_raw
        terms_k[...] += terms
    head = first + pl.program_id(0)
    half = KEY_VALUE_HEADS // 2
    queries_kept, queries_sent = (kv_kept, kv_sent) if first >= half else others[-12:-10]
    wide = GROUP * HEAD_WIDTH
    result = contract_first(grad_raw_all[...], normed[...]).astype(jnp.bfloat16)
    result_q, result_k, result_v = (
        result[:wide, :],
        result[wide : wide + HEAD_WIDTH, :],
        result[wide + HEAD_WIDTH :, :],
    )
    copies = [
        *put_by_core(
            rows_per_device, result_q, part_q, head % half, 0, queries_kept, queries_sent, sems, 0
        ),
        *put_by_core(rows_per_device, result_k, part_k, head, 1, kv_kept, kv_sent, sems, 2),
        *put_by_core(rows_per_device, result_v, part_v, head, 2, kv_kept, kv_sent, sems, 4),
    ]
    for copy in copies:
        copy.start()
    weights = jnp.concatenate([wq[...], wk[...], wv[...]], axis=0)
    total[...] += plain_product(grad_raw_all[...], weights)
    for copy in copies:
        copy.wait()


def by_core(rows_per_device, part):
    pairs = part.reshape(-1, 2, rows_per_device, part.shape[-1])
    here = lax.axis_index("dp") % 2 == 0
    first, second = pairs[:, 0], pairs[:, 1]
    return jnp.where(here, first, second), jnp.where(here, second, first)


def heads(rows, width, first=0):
    return pl.BlockSpec((rows, width), lambda k: (0, first + k))


def head_rows(heads_in, depth, first):
    return pl.BlockSpec((heads_in * HEAD_WIDTH, depth), lambda k: (first + k, 0))


def qkv_rows_of(depth, first):
    return [
        head_rows(GROUP, depth, first),
        head_rows(1, depth, QUERY_HEADS + first),
        head_rows(1, depth, QUERY_HEADS + KEY_VALUE_HEADS + first),
    ]


def attention(normed, qkv_full, tables, gain_q, gain_k, context, first, count):
    tokens, depth = normed.shape
    wide = GROUP * HEAD_WIDTH
    whole_context = shape_of((tokens, QUERY_HEADS * HEAD_WIDTH), jnp.bfloat16)
    held = [] if context is None else [context]
    return kernel_call(
        attention_kernel,
        "attention",
        (count,),
        [
            in_vmem(normed),
            *qkv_rows_of(depth, first),
            *[in_vmem(table) for table in tables],
            in_vmem(gain_q),
            in_vmem(gain_k),
            *[pl.BlockSpec(memory_space=pl.ANY)] * len(held),
        ],
        (
            shape_of((tokens, count * TRIO), jnp.bfloat16),
            shape_of((tokens, count * TRIO), jnp.bfloat16),
            shape_of((tokens, count * TRIO), jnp.bfloat16),
            shape_of((tokens, count * HEAD_WIDTH), jnp.bfloat16),
            whole_context,
        ),
        (
            heads(tokens, TRIO),
            heads(tokens, TRIO),
            heads(tokens, TRIO),
            heads(tokens, HEAD_WIDTH),
            heads(tokens, wide, first),
        ),
        scratch=[pltpu.VMEM((tokens, TRIO), jnp.float32)],
        aliases={9: 4} if held else None,
        vmem=VMEM_LESS,
    )(normed, qkv_full, qkv_full, qkv_full, *tables, gain_q, gain_k, *held)


def first_attention(grid, normed, own_pieces, swapped_pieces, tables, gain_q, gain_k, count):
    arrays, places_of = gather_plan(own_pieces, swapped_pieces)
    tokens, depth = normed.shape
    rows = arrays[0].shape[1]
    dims = (grid.count, rows, depth)
    anywhere = pl.BlockSpec(memory_space=pl.ANY)
    trio = shape_of((tokens, count * TRIO), jnp.bfloat16)
    *kept, context, weight = kernel_call(
        functools.partial(first_attention_kernel, grid, places_of, len(arrays), count),
        "attention",
        (count,),
        [
            *[anywhere] * len(arrays),
            in_vmem(normed),
            *[in_vmem(table) for table in tables],
            in_vmem(gain_q),
            in_vmem(gain_k),
        ],
        (
            trio,
            trio,
            trio,
            shape_of((tokens, count * HEAD_WIDTH), jnp.bfloat16),
            shape_of((tokens, QUERY_HEADS * HEAD_WIDTH), jnp.bfloat16),
            shape_of(dims, jnp.bfloat16),
        ),
        (
            heads(tokens, TRIO),
            heads(tokens, TRIO),
            heads(tokens, TRIO),
            heads(tokens, HEAD_WIDTH),
            heads(tokens, GROUP * HEAD_WIDTH),
            anywhere,
        ),
        scratch=[
            pltpu.VMEM((tokens, TRIO), jnp.float32),
            pltpu.VMEM(dims, jnp.bfloat16),
            pltpu.SemaphoreType.DMA((grid.count,)),
            pltpu.SemaphoreType.DMA((grid.count,)),
        ],
        vmem=VMEM_LESS,
    )(*arrays, normed, *tables, gain_q, gain_k)
    return kept, context, weight.reshape(grid.count * rows, depth)


def attention_backward(
    norms, scales, turns, value, grad_context, tables, gain_q, gain_k,
    normed, qkv_full, total, parts, first, rows_per_device,
):
    tokens, depth = normed.shape
    wide = GROUP * HEAD_WIDTH
    count = value.shape[1] // HEAD_WIDTH
    half = KEY_VALUE_HEADS // 2
    stretch = half * wide // (2 * rows_per_device)
    early = shape_of((1, stretch, rows_per_device, depth), jnp.bfloat16)
    late = shape_of((3, stretch, rows_per_device, depth), jnp.bfloat16)
    shapes = [late, late] if first >= half else [early, early, late, late]
    held = [] if total is None else [total, *parts]

    def part_scratch(rows):
        chips = max(rows // (2 * rows_per_device), 1)
        height = min(rows, rows_per_device)
        return pltpu.VMEM((2, chips, height, depth), jnp.bfloat16)

    anywhere = pl.BlockSpec(memory_space=pl.ANY)
    return kernel_call(
        functools.partial(attention_backward_kernel, first, rows_per_device, len(held)),
        "attention_backward",
        (count,),
        [
            heads(tokens, TRIO),
            heads(tokens, TRIO),
            heads(tokens, TRIO),
            heads(tokens, HEAD_WIDTH),
            heads(tokens, wide, first),
            *[in_vmem(table) for table in tables],
            in_vmem(gain_q),
            in_vmem(gain_k),
            in_vmem(normed),
            *qkv_rows_of(depth, first),
            *[in_vmem(total)] * min(len(held), 1),
            *[anywhere] * max(len(held) - 1, 0),
        ],
        (
            *shapes,
            shape_of((tokens, depth), jnp.float32),
            shape_of(gain_q.shape, jnp.float32),
            shape_of(gain_k.shape, jnp.float32),
        ),
        (*[anywhere] * len(shapes), in_vmem(normed), in_vmem(gain_q), in_vmem(gain_k)),
        scratch=[
            pltpu.VMEM((tokens, TRIO + HEAD_WIDTH), jnp.bfloat16),
            part_scratch(wide),
            part_scratch(HEAD_WIDTH),
            part_scratch(HEAD_WIDTH),
            pltpu.SemaphoreType.DMA((6,)),
        ],
        aliases={15 + slot: slot for slot in range(len(shapes))} if held else None,
        vmem=VMEM_LESS,
    )(
        norms, scales, turns, value, grad_context, *tables, gain_q, gain_k,
        normed, qkv_full, qkv_full, qkv_full, *held,
    )


ROW_TILE = 256
FF_TILE = 512
BACK_TILE = 384
STRIP = 64


def project_kernel(context, weight, residual, gain, middle, normed):
    middle[...] = residual[...] + contract_last(context[...], weight[...])

    @pl.loop(0, middle.shape[0] // STRIP)
    def _(strip):
        rows = pl.ds(pl.multiple_of(strip * STRIP, STRIP), STRIP)
        values = middle[rows, :]
        normed[rows, :] = (values * rms_scale(values) * gain[...]).astype(jnp.bfloat16)


def rows_of(array, tile):
    return pl.BlockSpec((tile, array.shape[1]), lambda k: (k, 0))


def project(context, weight, residual, gain):
    return kernel_call(
        project_kernel,
        "project",
        (residual.shape[0] // ROW_TILE,),
        [rows_of(context, ROW_TILE), whole(weight), rows_of(residual, ROW_TILE), whole(gain)],
        (shape_of(residual.shape, jnp.float32), shape_of(residual.shape, jnp.bfloat16)),
        (rows_of(residual, ROW_TILE), rows_of(residual, ROW_TILE)),
    )(context, weight, residual, gain)


def feed_kernel(grid, places_of, pieces_count, *refs):
    pieces, normed = refs[:pieces_count], refs[pieces_count]
    hidden, slope, lift, out, held, came, went = refs[pieces_count + 1 :]
    step = pl.program_id(0)
    rows = held.shape[1]
    tile = hidden.shape[1]
    each = tile // rows
    half = grid.count // 2

    @pl.when(step == 0)
    def _():
        for copy in arrivals(grid, places_of, pieces, held, came):
            copy.start()

    for number in range(each):
        for first in (0, half):
            device = first + step * each + number
            arrived(held, device, came).wait()
            leaving(held, device, out, went).start()
    weights = jnp.concatenate(
        [held[pl.ds(first + step * each, each)].reshape(tile, -1) for first in (0, half)], axis=0
    )
    both = contract_last(normed[...], weights)
    gate, upward = both[:, :tile], both[:, tile:]
    sigma = jax.nn.sigmoid(gate)
    lifted = gate * sigma
    lift[...] = lifted.astype(jnp.bfloat16)
    slope[...] = (upward * sigma * (1.0 + gate * (1.0 - sigma))).astype(jnp.bfloat16)
    hidden[...] = (lifted * upward).astype(jnp.bfloat16)

    @pl.when(step == pl.num_programs(0) - 1)
    def _():
        for device in range(grid.count):
            leaving(held, device, out, went).wait()


def columns_of(rows, tile, first=0):
    return pl.BlockSpec((rows, tile), lambda k: (0, first + k))


def gate_and_up(tile, depth, first=0):
    return pl.BlockSpec((2, tile, depth), lambda k: (0, first + k, 0))


def feed(grid, normed, own_pieces, swapped_pieces):
    arrays, places_of = gather_plan(own_pieces, swapped_pieces)
    tokens, depth = normed.shape
    rows = arrays[0].shape[1]
    columns = columns_of(tokens, BACK_TILE)
    anywhere = pl.BlockSpec(memory_space=pl.ANY)
    dims = (grid.count, rows, depth)
    hidden, slope, lift, weight = kernel_call(
        functools.partial(feed_kernel, grid, places_of, len(arrays)),
        "feed",
        (FF // BACK_TILE,),
        [*[anywhere] * len(arrays), whole(normed)],
        (
            shape_of((tokens, FF), jnp.bfloat16),
            shape_of((tokens, FF), jnp.bfloat16),
            shape_of((tokens, FF), jnp.bfloat16),
            shape_of(dims, jnp.bfloat16),
        ),
        (columns, columns, columns, anywhere),
        scratch=[
            pltpu.VMEM(dims, jnp.bfloat16),
            pltpu.SemaphoreType.DMA((grid.count,)),
            pltpu.SemaphoreType.DMA((grid.count,)),
        ],
    )(*arrays, normed)
    return hidden, slope, lift, weight.reshape(grid.count * rows, depth)


def finish_kernel(hidden, weight, residual, output):
    output[...] = residual[...] + contract_last(hidden[...], weight[...])


def finish(hidden, weight, residual):
    return kernel_call(
        finish_kernel,
        "finish",
        (residual.shape[0] // ROW_TILE,),
        [rows_of(hidden, ROW_TILE), whole(weight), rows_of(residual, ROW_TILE)],
        shape_of(residual.shape, jnp.float32),
        rows_of(residual, ROW_TILE),
    )(hidden, weight, residual)


def outer_kernel(rows_per_device, left, right, kept, sent, turned_left):
    @pl.when(pl.program_id(0) == 0)
    def _():
        turned_left[...] = left[...].T

    part = plain_product(turned_left[...], right[...]).astype(jnp.bfloat16)
    kept[...], sent[...] = by_core(rows_per_device, part)


def chip_columns(chips, rows, width):
    return pl.BlockSpec((chips, rows, width), lambda k: (0, 0, k))


def outer(left, right, rows_per_device):
    chips = left.shape[1] // (2 * rows_per_device)
    shape = shape_of((chips, rows_per_device, right.shape[1]), jnp.bfloat16)
    block = chip_columns(chips, rows_per_device, FF_TILE)
    return kernel_call(
        functools.partial(outer_kernel, rows_per_device),
        "outer",
        (right.shape[1] // FF_TILE,),
        [whole(left), columns_of(right.shape[0], FF_TILE)],
        (shape, shape),
        (block, block),
        scratch=[pltpu.VMEM((left.shape[1], left.shape[0]), jnp.bfloat16)],
    )(left, right)


def first_feed_backward_kernel(grid, places_of, pieces_count, rows_per_device, *refs):
    pieces, (grad_feed, *inputs) = refs[:pieces_count], refs[pieces_count : pieces_count + 5]
    *outputs, out, held, came, went = refs[pieces_count + 5 :]
    step = pl.program_id(0)

    @pl.when(step == 0)
    def _():
        for copy in arrivals(grid, places_of, pieces, held, came):
            copy.start()
        for device in range(grid.count):
            arrived(held, device, came).wait()
            leaving(held, device, out, went).start()

    columns = pl.ds(pl.multiple_of(step * BACK_TILE, BACK_TILE), BACK_TILE)
    down = held[:, :, columns].reshape(-1, BACK_TILE)
    feed_backward_kernel(rows_per_device, grad_feed, down, *inputs, *outputs)

    @pl.when(step == pl.num_programs(0) - 1)
    def _():
        for device in range(grid.count):
            leaving(held, device, out, went).wait()


def first_feed_backward(
    grid, grad_feed, own_pieces, swapped_pieces, slope, lift, normed, weight, rows_per_device
):
    arrays, places_of = gather_plan(own_pieces, swapped_pieces)
    tokens, depth = normed.shape
    count = FF // BACK_TILE // 2
    chips = BACK_TILE // (2 * rows_per_device)
    shape = shape_of((2, count * chips, rows_per_device, depth), jnp.bfloat16)
    block = pl.BlockSpec((2, chips, rows_per_device, depth), lambda k: (0, k, 0, 0))
    anywhere = pl.BlockSpec(memory_space=pl.ANY)
    rows = arrays[0].shape[1]
    dims = (grid.count, rows, FF)
    *results, down = kernel_call(
        functools.partial(
            first_feed_backward_kernel, grid, places_of, len(arrays), rows_per_device
        ),
        "feed_backward",
        (count,),
        [
            *[anywhere] * len(arrays),
            whole(grad_feed),
            columns_of(tokens, BACK_TILE),
            columns_of(tokens, BACK_TILE),
            whole(normed),
            gate_and_up(BACK_TILE, depth),
        ],
        (shape, shape, shape_of((tokens, depth), jnp.float32), shape_of(dims, jnp.bfloat16)),
        (block, block, pl.BlockSpec((tokens, depth), lambda k: (0, 0)), anywhere),
        scratch=[
            pltpu.VMEM(dims, jnp.bfloat16),
            pltpu.SemaphoreType.DMA((grid.count,)),
            pltpu.SemaphoreType.DMA((grid.count,)),
        ],
    )(*arrays, grad_feed, slope, lift, normed, weight.reshape(2, FF, depth))
    return results, down.reshape(grid.count * rows, FF)


def feed_backward_kernel(
    rows_per_device, grad_feed, down, slope, lift, normed, weights, *others
):
    kept, sent, total = others[-3:]

    @pl.when(pl.program_id(0) == 0)
    def _():
        total[...] = others[0][...] if len(others) > 3 else jnp.zeros_like(total)

    grad_hidden = plain_product(grad_feed[...], down[...])
    grads = jnp.concatenate(
        [
            (grad_hidden * slope[...].astype(jnp.float32)).astype(jnp.bfloat16),
            (grad_hidden * lift[...].astype(jnp.float32)).astype(jnp.bfloat16),
        ],
        axis=1,
    )
    tile = grad_hidden.shape[1]
    part = contract_first(grads, normed[...]).astype(jnp.bfloat16)
    for plane in range(2):
        kept[plane], sent[plane] = by_core(
            rows_per_device, part[plane * tile : (plane + 1) * tile, :]
        )
    total[...] += plain_product(grads, weights[...].reshape(2 * tile, -1))


def feed_backward(grad_feed, down, slope, lift, normed, weight, total, half, rows_per_device):
    tokens, depth = normed.shape
    tiles = FF // BACK_TILE
    count = tiles // 2
    first = half * count
    held = [] if total is None else [total]
    chips = BACK_TILE // (2 * rows_per_device)
    shape = shape_of((2, count * chips, rows_per_device, depth), jnp.bfloat16)
    block = pl.BlockSpec((2, chips, rows_per_device, depth), lambda k: (0, k, 0, 0))
    return kernel_call(
        functools.partial(feed_backward_kernel, rows_per_device),
        "feed_backward",
        (count,),
        [
            whole(grad_feed),
            columns_of(depth, BACK_TILE, first),
            columns_of(tokens, BACK_TILE, first),
            columns_of(tokens, BACK_TILE, first),
            whole(normed),
            gate_and_up(BACK_TILE, depth, first),
            *[whole(total) for total in held],
        ],
        (shape, shape, shape_of((tokens, depth), jnp.float32)),
        (block, block, pl.BlockSpec((tokens, depth), lambda k: (0, 0))),
    )(grad_feed, down, slope, lift, normed, weight.reshape(2, FF, depth), *held)


def project_backward_kernel(
    rows_per_device, grad_normed, middle, out_grad, gain, context, weight,
    kept, sent, grad_context, grad_middle, gain_terms, branch, turned_branch,
):
    step = pl.program_id(0)
    row_steps = branch.shape[0] // ROW_TILE

    @pl.when(step == 0)
    def _():
        gain_terms[...] = jnp.zeros_like(gain_terms)

    @pl.when(step < row_steps)
    def _():
        start = pl.multiple_of(step * ROW_TILE, ROW_TILE)

        @pl.loop(0, ROW_TILE // STRIP)
        def _(strip):
            rows = pl.ds(pl.multiple_of(strip * STRIP, STRIP), STRIP)
            values = middle[rows, :]
            grad, terms = norm_backward(values, rms_scale(values), gain[...], grad_normed[rows, :])
            grad = out_grad[rows, :] + grad
            grad_middle[rows, :] = grad
            branch[pl.ds(pl.multiple_of(start + strip * STRIP, STRIP), STRIP), :] = grad.astype(
                jnp.bfloat16
            )
            gain_terms[...] += jnp.sum(terms, axis=0, keepdims=True)

    @pl.when(step == row_steps)
    def _():
        turned_branch[...] = branch[...].T

    @pl.when(step >= row_steps)
    def _():
        part = plain_product(turned_branch[...], context[...]).astype(jnp.bfloat16)
        kept[...], sent[...] = by_core(rows_per_device, part)
        grad_context[...] = plain_product(branch[...], weight[...]).astype(jnp.bfloat16)


def project_backward(grad_normed, middle, out_grad, gain, context, weight, rows_per_device):
    tokens, depth = middle.shape
    width = context.shape[1]
    chips = depth // (2 * rows_per_device)
    shape = shape_of((chips, rows_per_device, width), jnp.bfloat16)
    row_steps = tokens // ROW_TILE

    def column(k):
        return jnp.maximum(k - row_steps, 0)

    def row_block(k):
        return (jnp.minimum(k, row_steps - 1), 0)

    rows = pl.BlockSpec((ROW_TILE, depth), row_block)
    block = pl.BlockSpec((chips, rows_per_device, FF_TILE), lambda k: (0, 0, column(k)))

    def columns(count):
        return pl.BlockSpec((count, FF_TILE), lambda k: (0, column(k)))

    return kernel_call(
        functools.partial(project_backward_kernel, rows_per_device),
        "project_backward",
        (row_steps + width // FF_TILE,),
        [rows, rows, rows, whole(gain), columns(tokens), columns(depth)],
        (
            shape,
            shape,
            shape_of((tokens, width), jnp.bfloat16),
            shape_of((tokens, depth), jnp.float32),
            shape_of(gain.shape, jnp.float32),
        ),
        (block, block, columns(tokens), rows, whole(gain)),
        scratch=[
            pltpu.VMEM((tokens, depth), jnp.bfloat16),
            pltpu.VMEM((depth, tokens), jnp.bfloat16),
        ],
    )(grad_normed, middle, out_grad, gain, context, weight)


def position_tables(segment_ids):
    _, micro_rows = segment_ids.shape
    order = jnp.arange(micro_rows, dtype=jnp.int32)
    same = segment_ids[:, :, None] == segment_ids[:, None, :]
    earlier = order[None, :] < order[:, None]
    positions = jnp.sum(jnp.where(same & earlier[None], 1, 0), axis=2).astype(jnp.int32)
    half_size = HEAD_WIDTH // 2
    frequency = ROPE_BASE ** (-(jnp.arange(half_size, dtype=jnp.float32) * (2.0 / HEAD_WIDTH)))
    angles = positions.reshape(-1, 1).astype(jnp.float32) * frequency[None, :]
    cosine, sine = jnp.cos(angles), jnp.sin(angles)
    allowed = same & (earlier | (order[None, :] == order[:, None]))[None]
    return (
        jnp.concatenate([cosine, cosine], axis=-1),
        jnp.concatenate([-sine, sine], axis=-1),
        jnp.where(allowed, 0.0, -1e30).astype(jnp.float32),
    )


def adamw(weight, first, second, grad, rate, decay):
    first_new = BETA_ONE * first + (1.0 - BETA_ONE) * grad
    second_new = BETA_TWO * second + (1.0 - BETA_TWO) * grad * grad
    corrected = (
        first_new
        / (1.0 - BETA_ONE**STEP)
        / (jnp.sqrt(second_new / (1.0 - BETA_TWO**STEP)) + ADAM_EPS)
    )
    return (weight - rate * (corrected + decay * weight), first_new, second_new)


def per_device(
    grid,
    activations,
    segment_ids,
    out_grad,
    qkv_weight,
    qkv_first,
    qkv_second,
    out_weight,
    out_first,
    out_second,
    gate_up_weight,
    gate_up_first,
    gate_up_second,
    down_weight,
    down_first,
    down_second,
    norm_gains,
    gains_first,
    gains_second,
):
    qkv_low = qkv_weight.astype(jnp.bfloat16)
    out_low = out_weight.astype(jnp.bfloat16)
    gate_up_low = gate_up_weight.astype(jnp.bfloat16)
    down_low = down_weight.astype(jnp.bfloat16)

    gain_count = norm_gains.shape[0]
    gain_start = lax.axis_index("dp") * gain_count
    all_gains = jnp.zeros((1, gain_count * grid.count), jnp.bfloat16)
    all_gains = lax.dynamic_update_slice(
        all_gains, norm_gains.astype(jnp.bfloat16)[None], (0, gain_start)
    )
    size = grid.size
    heads_of = KEY_VALUE_HEADS // 4
    out_rows, gate_rows = out_low.shape[0], gate_up_low.shape[0]
    qkv_rows, down_rows = qkv_low.shape[0], down_low.shape[0]

    tables = position_tables(segment_ids)
    scale_one = rms_scale(activations)
    v = Steps(out_low=out_low, gate_up_low=gate_up_low)
    v.qkv_line = z_pieces(grid, qkv_low, False)
    down_block = jnp.concatenate([down_low, rows_of_gains(all_gains, down_low.shape[1])], axis=0)
    down_sides = plane_sides(grid, down_block)
    down_corners = plane_corners(grid, down_sides, cut_at=down_rows)
    v.down_chip, v.gains, down_places = chip_plane(down_block, down_sides, down_corners, down_rows)
    v.close()

    v.qkv_column = jnp.stack(v.qkv_line)
    v.qkv_sides = plane_sides(grid, v.qkv_column)
    all_gains = v.gains.reshape(1, -1)[:, : gain_count * grid.count]
    out_block = jnp.concatenate([v.out_low, rows_of_gains(all_gains, out_low.shape[1])], axis=0)
    v.out_line = z_pieces(grid, out_block, False)
    v.grad_feed = out_grad.astype(jnp.bfloat16)
    v.drop("qkv_line", "out_low", "gains")
    v.close()

    grad_feed = v.grad_feed
    v.out_column = jnp.stack([piece[:out_rows] for piece in v.out_line])
    gains = sum(piece[out_rows:].astype(jnp.float32) for piece in v.out_line)
    gains = gains.reshape(1, -1)[:, : gain_count * grid.count]
    v.gains = gains
    v.qkv_corners = plane_corners(grid, v.qkv_sides)
    v.gate_up_moved = {1: grid.shift(v.gate_up_low, "z", 1)}
    v.qkv_sides_swapped = swap_tree(grid, v.qkv_sides)
    v.drop("grad_feed", "out_line")
    v.close()

    every = tuple(range(size["z"]))
    middle_plane = size["z"] // 2
    gains = small_sum(grid, v.gains, "c")
    gain_one, gain_two = gains[:, :D], gains[:, D : 2 * D]
    gain_query = gains[:, 2 * D : 2 * D + HEAD_WIDTH]
    gain_key = gains[:, 2 * D + HEAD_WIDTH :]
    normed_one = (activations * scale_one * gain_one).astype(jnp.bfloat16)
    qkv_column_swapped, qkv_corners_swapped = swap_tree(grid, (v.qkv_column, v.qkv_corners))
    v.out_sides = plane_sides(grid, v.out_column)
    v.near_column = jnp.stack([v.gate_up_low, v.gate_up_moved[1]])
    v.near_sides = plane_sides(grid, v.near_column)
    v.gate_up_moved[2] = grid.shift(v.gate_up_low, "z", 2)
    kept, context, qkv_full = first_attention(
        grid,
        normed_one,
        plane_pieces(every, v.qkv_column, v.qkv_sides, v.qkv_corners),
        plane_pieces(every, qkv_column_swapped, v.qkv_sides_swapped, qkv_corners_swapped),
        tables,
        gain_query,
        gain_key,
        heads_of,
    )
    v.drop("qkv_column", "qkv_sides", "qkv_corners", "gate_up_low", "gains")
    v.drop("qkv_sides_swapped")
    parts = [kept]

    def attention_part(part, context):
        *kept, context = attention(
            after(normed_one, *flat(context)),
            qkv_full,
            tables,
            gain_query,
            gain_key,
            context,
            part * heads_of,
            heads_of,
        )
        parts.append(kept)
        return context

    v.gate_up_moved[3] = grid.shift(
        after(gate_up_low, context, v.gate_up_moved[2]), "z", 3
    )
    v.context = attention_part(1, context)
    v.close()

    v.far_column = jnp.stack([v.gate_up_moved[2], v.gate_up_moved[3]])
    v.out_corners = plane_corners(grid, v.out_sides)
    v.far_sides = plane_sides(grid, v.far_column)
    v.down_moved = {1: grid.shift(v.down_chip, "z", 1)}
    v.context = attention_part(3, attention_part(2, v.context))
    v.drop("gate_up_moved")
    v.close()

    v.gate_up_corners = plane_corners(grid, (v.near_sides[0], v.far_sides[1]), halved=False)
    v.down_moved[3] = grid.shift(v.down_chip, "z", 3)
    out_swapped = swap_together(grid, (v.out_column, v.out_sides, v.out_corners))
    v.near_sides_swapped = swap_tree(grid, after_tree(v.near_sides, out_swapped))
    out_full = assemble(
        grid,
        plane_pieces(every, v.out_column, v.out_sides, v.out_corners),
        plane_pieces(every, *out_swapped),
    )
    v.far_sides_swapped = swap_tree(
        grid, after_tree(v.far_sides, out_full, v.near_sides_swapped)
    )
    middle, v.normed_two = project(v.context, out_full, activations, gain_two)
    context = v.context
    v.drop("out_column", "out_sides", "out_corners", "context")
    v.close()

    normed_two = v.normed_two
    corners_swapped = swap_tree(grid, v.gate_up_corners)
    columns_swapped = swap_tree(grid, (v.near_column, v.far_column))
    v.down_moved[2] = grid.shift(v.down_chip, "z", 2)
    near, far = every[:middle_plane], every[middle_plane:]
    v.hidden, v.slope, v.lift, gate_up_full = feed(
        grid,
        normed_two,
        plane_pieces(near, v.near_column, v.near_sides, {})
        + plane_pieces(far, v.far_column, v.far_sides, {})
        + corner_pieces(every, v.gate_up_corners),
        plane_pieces(near, columns_swapped[0], v.near_sides_swapped, {})
        + plane_pieces(far, columns_swapped[1], v.far_sides_swapped, {})
        + corner_pieces(every, corners_swapped),
    )
    early = after_tree(
        [v.down_chip, v.down_moved[1], v.down_moved[3]], corners_swapped, columns_swapped
    )
    v.down_swapped = swap_tree(grid, early)
    v.down_parts = outer(grad_feed, v.hidden, down_rows)
    v.drop("near_column", "far_column", "near_sides", "far_sides", "gate_up_corners", "normed_two")
    v.drop("near_sides_swapped", "far_sides_swapped")
    v.close()

    hidden, slope, lift = v.hidden, v.slope, v.lift
    down_line = [v.down_chip, *[v.down_moved[hops] for hops in grid.hops("z")]]
    own_swapped, one_swapped, three_swapped = v.down_swapped
    two_swapped = grid.shift(v.down_moved[2], "c", 1)
    down_line_swapped = [own_swapped, one_swapped, two_swapped, three_swapped]
    slots = [(axis, hops) for axis in "zyx" for hops in range(size[axis])]
    numbers = jnp.stack([grid.ahead(axis, hops) for axis, hops in slots]).astype(jnp.int32)

    def here(axis, hops):
        return Place(slots.index((axis, hops)))

    def in_planes(pair):
        return [
            part.reshape(-1, size["y"], size["x"], *part.shape[-2:]) for part in pair
        ]

    v.down_terms = swapped(grid, in_planes(after_tree(v.down_parts, two_swapped)))

    def feed_part(half, total):
        *pair, total = feed_backward(
            grad_feed, down_full, slope, lift, normed_two, gate_up_full, total, half, gate_rows
        )
        return pair, total

    (*v.even_parts, v.total), down_full = first_feed_backward(
        grid,
        grad_feed,
        line_pieces(down_line, down_places),
        line_pieces(down_line_swapped, down_places),
        slope,
        lift,
        normed_two,
        gate_up_full,
        gate_rows,
    )
    v.drop("down_chip", "down_moved", "down_swapped", "down_parts", "hidden", "slope", "lift")
    v.close()

    merge = Merge(grid, numbers)
    down_one = line(merge, here, [(v.down_terms, every)], 1, lead=2)
    made = merge.run()
    v.down_moved = [Source(down_one(made))]
    v.even = swapped(grid, in_planes(v.even_parts))
    v.odd_parts, v.total = feed_part(1, v.total)
    v.drop("even_parts")
    v.close()

    merge = Merge(grid, numbers)
    even_corners = corners(merge, here, v.even)
    down_three = line(merge, here, [(v.down_terms, every)], 3, lead=2)
    made = merge.run()
    v.even_corners = even_corners(made)
    v.down_moved.append(Source(down_three(made)))
    v.odd = swapped(grid, in_planes(v.odd_parts))
    *v.out_parts, v.grad_context, v.grad_middle, v.gain_two_part = project_backward(
        v.total, middle, out_grad, gain_two, context, out_full, out_rows
    )
    v.drop("odd_parts", "total")
    v.close()

    low, high = halves_of(v.down_terms)
    grad_context, grad_middle, gain_two_part = v.grad_context, v.grad_middle, v.gain_two_part
    v.drop("grad_context", "grad_middle", "gain_two_part")
    merge = Merge(grid, numbers)
    even_sides = sides(merge, here, v.even, v.even_corners)
    down_two = line(merge, here, [(v.down_terms, every)], 2, rows=low, lead=2)
    made = merge.run()
    v.even = even_sides(made)
    v.down_moved.append(Source(down_two(made)))
    v.out_terms = swapped(grid, in_planes(v.out_parts))
    v.gain_terms = []

    def backward_part(part, rows, total):
        *v.rows, v.total, terms_q, terms_k = attention_backward(
            *parts[part],
            grad_context,
            tables,
            gain_query,
            gain_key,
            normed_one,
            qkv_full,
            total,
            rows,
            part * heads_of,
            qkv_rows,
        )
        v.gain_terms = v.gain_terms + [(terms_q, terms_k)]

    backward_part(0, [], None)
    v.drop("out_parts", "even_corners")
    v.close()

    merge = Merge(grid, numbers)
    odd_corners = corners(merge, here, v.odd)
    out_corners = corners(merge, here, v.out_terms)
    down_two = line(merge, here, [(v.down_terms, every)], 2, rows=high, lead=2)
    down_own = line(merge, here, [(v.down_terms, every)], 0, lead=2)
    made = merge.run()
    v.odd_corners = odd_corners(made)
    v.out_corners = out_corners(made)
    v.down_moved += [Source(down_two(made), high[0]), Source(down_own(made))]
    backward_part(1, v.rows, v.total)
    v.drop("down_terms")
    v.close()

    merge = Merge(grid, numbers)
    odd_sides = sides(merge, here, v.odd, v.odd_corners)
    down_corners = corners(merge, here, v.down_moved, lead=0)
    made = merge.run()
    v.odd = odd_sides(made)
    v.down_corners = down_corners(made)
    v.first = swapped(grid, in_planes(v.rows[:2]))
    backward_part(2, v.rows[2:], v.total)
    v.drop("odd_corners")
    v.close()

    gate_up_groups = [(v.even, (0, 2)), (v.odd, (1, 3))]
    merge = Merge(grid, numbers)
    out_sides = sides(merge, here, v.out_terms, v.out_corners)
    gate_up_lines = [line(merge, here, gate_up_groups, hops) for hops in (1, 3, 0)]
    made = merge.run()
    v.out_terms = out_sides(made)
    v.gate_up_moved = [go(made) for go in gate_up_lines]
    backward_part(3, v.rows, v.total)
    v.drop("out_corners")
    v.close()

    v.last = swapped(grid, in_planes(v.rows))
    merge = Merge(grid, numbers)
    first_corners = corners(merge, here, v.first)
    down_sides = sides(merge, here, v.down_moved, v.down_corners, lead=0)
    made = merge.run()
    v.first_corners = first_corners(made)
    v.down_terms = down_sides(made)
    total, gain_terms = v.total, v.gain_terms
    grad_block, gain_one_terms = norm_backward(activations, scale_one, gain_one, after(total, made))
    v.gains_part = jnp.concatenate(
        [
            jnp.sum(gain_one_terms, axis=0, keepdims=True),
            gain_two_part,
            sum(terms for terms, _ in gain_terms),
            sum(terms for _, terms in gain_terms),
        ],
        axis=1,
    )
    v.drop("rows", "total", "gain_terms", "down_moved", "down_corners")
    v.close()

    gate_up_groups = [(v.even, (0, 2)), (v.odd, (1, 3))]
    merge = Merge(grid, numbers)
    last_corners = corners(merge, here, v.last)
    first_sides = sides(merge, here, v.first, v.first_corners)
    gate_up_two = line(merge, here, gate_up_groups, 2)
    made = merge.run()
    v.last_corners = last_corners(made)
    v.first = first_sides(made)
    v.gate_up_moved.append(gate_up_two(made))
    v.layer_output = finish(after(hidden, made), down_full, middle)
    v.gains_part = small_sum(grid, v.gains_part, "c")
    v.total = total
    v.drop("even", "odd", "first_corners")
    v.close()

    merge = Merge(grid, numbers)
    last_sides = sides(merge, here, v.last, v.last_corners)
    out_lines = [line(merge, here, [(v.out_terms, every)], hops) for hops in range(size["z"])]
    made = merge.run()
    v.last = last_sides(made)
    v.out_moved = [go(made) for go in out_lines]
    v.gains_part = small_sum(grid, after(v.gains_part, v.out_moved), "z")
    v.gate_up_new = adamw(
        gate_up_weight, gate_up_first, gate_up_second, total_of(*v.gate_up_moved), 0.06, 0.1
    )
    down_total = total_of(*[term.array for term in v.down_terms])
    v.down_new = adamw(down_weight, down_first, down_second, down_total, 0.04, 0.1)
    grad_block, _ = norm_backward(activations, scale_one, gain_one, after(v.total, made))
    v.input_grad = grad_middle + grad_block
    v.drop("last_corners", "gate_up_moved", "down_terms", "out_terms", "total")
    v.close()

    qkv_groups = [(v.first, (0,)), (v.last, (1, 2, 3))]
    merge = Merge(grid, numbers)
    qkv_lines = [line(merge, here, qkv_groups, hops) for hops in range(size["z"])]
    made = merge.run()
    qkv_total = total_of(*[go(made) for go in qkv_lines])
    out_new = adamw(out_weight, out_first, out_second, total_of(*v.out_moved), 0.25, 0.1)
    gains_total = small_sum(grid, v.gains_part, "xy")
    gains_total = lax.dynamic_slice(gains_total, (0, gain_start), (1, gain_count))[0]

    return (
        v.layer_output,
        v.input_grad,
        *adamw(qkv_weight, qkv_first, qkv_second, qkv_total, 0.06, 0.1),
        *out_new,
        *v.gate_up_new,
        *v.down_new,
        *adamw(norm_gains, gains_first, gains_second, gains_total, 0.3, 0.0),
    )


def solution(mesh):
    return jax.shard_map(
        functools.partial(per_device, Grid(mesh.shape["dp"])),
        mesh=mesh,
        in_specs=(
            P("dp", None),
            P("dp", None),
            P("dp", None),
            P("dp", None),
            P("dp", None),
            P("dp", None),
            P("dp", None),
            P("dp", None),
            P("dp", None),
            P("dp", None),
            P("dp", None),
            P("dp", None),
            P("dp", None),
            P("dp", None),
            P("dp", None),
            P("dp"),
            P("dp"),
            P("dp"),
        ),
        out_specs=(
            P("dp", None),
            P("dp", None),
            P("dp", None),
            P("dp", None),
            P("dp", None),
            P("dp", None),
            P("dp", None),
            P("dp", None),
            P("dp", None),
            P("dp", None),
            P("dp", None),
            P("dp", None),
            P("dp", None),
            P("dp", None),
            P("dp"),
            P("dp"),
            P("dp"),
        ),
        check_vma=False,
    )
```
